32 devices in a mesh: blk: 16 (over z, y, x), row: 2 (over core).
Axes of the slice: x: 2, y: 2, z: 4, core: 2. Of those that a mesh axis runs over, the one named last changes fastest.
Arguments:
- diag_block: float32 [1024, 1024], P('row'), as said below
- panel_rows: float32 [2, 512, 1024], P('row', 'blk'), may hold values from -6 to 6
- row_ids: int32 [4], replicated, may hold values from 0 to 31, as said below
- col_ids: int32 [96], P('blk'), may hold values from -1 to 31, as said below
- block_rows: int32 [96, 8], P('blk'), may hold values from -1 to 31, as said below
- blocks: float32 [96, 8, 256, 256], P('blk', None, 'row'), may hold values from -6 to 6
Outputs:
- factor_rows: float32 [2, 512, 1024], P('row', 'blk')
- new_blocks: float32 [96, 8, 256, 256], P('blk', None, 'row')
The draws below stay inside these ranges and needn't reach their ends.
Inputs may be any that keep to these rules, and one draw needn't show every extreme that they name: `row_ids`: strictly increasing and distinct; the last is 31. `col_ids`: each of the 32 block columns stands in exactly one slot; an owner's slots s * 6 to s * 6 + 5 hold its columns first, then -1; owners hold 0 to 6 columns, one owner exactly 6. `block_rows`: for a live slot, entry 0 is its own column, live entries rise strictly and are followed only by -1; an empty slot holds -1 only. A column among row_ids stores the block rows of row_ids from itself on, up to 8 of them. `diag_block`: symmetric positive definite.
All inputs are finite; a program needn't handle non-finite values.
Results may differ from the reference program's by a relative error of at most 0.0003.
Values may be sent and summed in bfloat16 or wider, within the bound.
No kernel may reach another device: no remote copies, remote signals or barrier semaphores. Data moves between devices by JAX's collectives and lax.ppermute only.
A program may use at most 128 MiB of HBM per device.

```python
import math
import jax
import jax.numpy as jnp
from jax import lax

BLOCK_SIZE = 256
W = 512
MEAN = 2
CS = 6
STORED_BLOCKS = 8
PR = 4
NCOL = 32
SLOT_COUNT = 96
N_BLK = 16


def edge_weights(key, order):
    return jax.random.uniform(key, (order,), jnp.float32, 32.0, 96.0)


def shifted(values, offset, order):
    return jnp.concatenate([jnp.zeros((offset,), jnp.float32), values[:order - offset]])


def kernel_part(key, order):
    key_place, key_scale = jax.random.split(key, 2)
    places = jax.random.uniform(key_place, (order,), jnp.float32, 0.0, 1.0)
    scales = jnp.exp(jax.random.uniform(key_scale, (order,), jnp.float32, math.log(0.7), math.log(1.4)))
    reach = 20.0 / order
    apart = jnp.abs(places[:, None] - places[None, :])
    return 8.0 * scales[:, None] * scales[None, :] * jnp.exp(-apart / reach)


def draw_diag_block(key, part):
    key_horiz, key_vert, right_random_key, key_left, key_ridge = jax.random.split(key, 5)
    order = 2 * W
    span = W // 16
    index = jnp.arange(order)
    column = index % span
    horiz = edge_weights(key_horiz, order) * ((column < span - 1) & (index + 1 < order)).astype(jnp.float32)
    vert = edge_weights(key_vert, order) * (index + span < order).astype(jnp.float32)
    down_right = edge_weights(right_random_key, order) * ((column < span - 1) & (index + span + 1 < order)).astype(jnp.float32)
    down_left = edge_weights(key_left, order) * ((column > 0) & (index + span - 1 < order)).astype(jnp.float32)
    ridge = 64.0 * jnp.exp(jax.random.uniform(key_ridge, (order,), jnp.float32, math.log(0.02), math.log(0.2)))
    total = horiz + shifted(horiz, 1, order)
    total = total + vert + shifted(vert, span, order)
    total = total + down_right + shifted(down_right, span + 1, order)
    total = total + down_left + shifted(down_left, span - 1, order)
    diagonal = total + ridge
    dense_matrix = jnp.diag(diagonal)
    dense_matrix = dense_matrix - jnp.diag(horiz[:order - 1], 1) - jnp.diag(horiz[:order - 1], -1)
    dense_matrix = dense_matrix - jnp.diag(vert[:order - span], span) - jnp.diag(vert[:order - span], -span)
    dense_matrix = dense_matrix - jnp.diag(down_right[:order - span - 1], span + 1) - jnp.diag(down_right[:order - span - 1], -(span + 1))
    dense_matrix = dense_matrix - jnp.diag(down_left[:order - span + 1], span - 1) - jnp.diag(down_left[:order - span + 1], -(span - 1))
    dense_matrix = dense_matrix + kernel_part(jax.random.fold_in(key, 41), order)
    return dense_matrix


def pattern_rows(key):
    shuffled = jax.random.permutation(jax.random.fold_in(key, 11), NCOL - 1)
    leading = jnp.sort(shuffled[:PR - 1]).astype(jnp.int32)
    return jnp.concatenate([leading, jnp.full((1,), NCOL - 1, jnp.int32)]).astype(jnp.int32)


def owner_columns(key):
    shuffle = jax.random.permutation(jax.random.fold_in(key, 23), N_BLK)
    ranks = jnp.arange(N_BLK)
    by_rank = jnp.where(ranks == 0, 3 * MEAN, MEAN)
    by_rank = jnp.where((ranks == 1) | (ranks == 2) | (ranks == 4), 0, by_rank)
    by_rank = jnp.where(ranks == 3, 2 * MEAN, by_rank)
    counts = jnp.zeros((N_BLK,), jnp.int32).at[shuffle].set(by_rank.astype(jnp.int32))
    live = jnp.arange(CS)[None, :] < counts[:, None]
    flat_live = live.reshape(-1).astype(jnp.int32)
    rank_of = jnp.cumsum(flat_live) - 1
    column_order = jax.random.permutation(jax.random.fold_in(key, 29), NCOL)
    picked = column_order[jnp.clip(rank_of, 0, NCOL - 1)]
    return jnp.where(flat_live > 0, picked, -1).astype(jnp.int32)


def draw_row_ids(key, part):
    return pattern_rows(key)


def draw_col_ids(key, part):
    return owner_columns(key)


def draw_block_rows(key, part):
    columns = owner_columns(key)
    rows = pattern_rows(key)
    match_flags = rows[None, :] == columns[:, None]
    inside = jnp.any(match_flags, axis=1)
    position = jnp.sum(jnp.where(match_flags, jnp.arange(PR)[None, :], 0), axis=1)
    follow = position[:, None] + jnp.arange(STORED_BLOCKS)[None, :]
    set_rows = jnp.where(follow < PR, rows[jnp.clip(follow, 0, PR - 1)], -1)
    stride_steps = jax.random.randint(jax.random.fold_in(key, 31), (SLOT_COUNT, STORED_BLOCKS), 1, 4)
    stride_steps = jnp.where(jnp.arange(STORED_BLOCKS)[None, :] == 0, 0, stride_steps)
    offsets = jnp.cumsum(stride_steps, axis=1)
    loose_rows = columns[:, None] + offsets
    loose_rows = jnp.where(loose_rows < NCOL, loose_rows, -1)
    chosen = jnp.where(inside[:, None], set_rows, loose_rows)
    return jnp.where(columns[:, None] >= 0, chosen, -1).astype(jnp.int32)


def levels(own_key, extent, pieces, low, high):
    gain = 1.0
    for axis_at, blocks in pieces:
        steps = jax.random.uniform(jax.random.fold_in(jax.random.fold_in(own_key, 6), axis_at), (blocks,), jnp.float32, low / len(pieces), high / len(pieces))
        gain = gain * jnp.repeat(jnp.exp(steps), extent[axis_at] // blocks).reshape((-1,) + (1,) * (len(extent) - 1 - axis_at))
    return gain


def centred(own_key, shape, spread, most, cuts=(), held_as=jnp.bfloat16):
    result = spread * jax.random.normal(own_key, shape, jnp.float32)
    if cuts:
        result = result * levels(own_key, shape, cuts, -0.22, 0.18)
    return jnp.clip(result, -most, most).astype(held_as)


def setup_inputs(seed: int = 0) -> dict:
    keys = jax.random.split(jax.random.key(seed), 7)
    return {
        "diag_block": draw_diag_block(jax.random.fold_in(keys[6], 71), 0),
        "panel_rows": centred(keys[1], (2, PR * (BLOCK_SIZE // 2), 2 * W), 1.0, 6.0, ((0, 2), (1, 16)), jnp.float32),
        "row_ids": draw_row_ids(jax.random.fold_in(keys[6], 71), 0),
        "col_ids": draw_col_ids(jax.random.fold_in(keys[6], 71), 0),
        "block_rows": draw_block_rows(jax.random.fold_in(keys[6], 71), 0),
        "blocks": centred(keys[5], (SLOT_COUNT, STORED_BLOCKS, BLOCK_SIZE, BLOCK_SIZE), 1.0, 6.0, ((0, 16), (2, 2)), jnp.float32),
    }


def right_solve(lower_factor, right_side):
    return lax.linalg.triangular_solve(lower_factor, right_side, left_side=False, lower=True, transpose_a=True)

def reference(diag_block, panel_rows, row_ids, col_ids, block_rows, blocks):
    diag_first = diag_block[:W, :W]
    coupling = diag_block[W:, :W]
    diag_second = diag_block[W:, W:]
    factor_first = jnp.linalg.cholesky(diag_first)
    stacked_rows = panel_rows.reshape(2 * PR * (BLOCK_SIZE // 2), 2 * W)
    left_part = right_solve(factor_first, stacked_rows[:, :W])
    coupled = right_solve(factor_first, coupling)
    schur_second = diag_second - jnp.dot(coupled, coupled.T, precision=lax.Precision.HIGHEST)
    factor_second = jnp.linalg.cholesky(schur_second)
    right_rows = stacked_rows[:, W:] - jnp.dot(left_part, coupled.T, precision=lax.Precision.HIGHEST)
    right_part = right_solve(factor_second, right_rows)
    factor_rows = jnp.concatenate([left_part, right_part], axis=1).reshape(2, PR * (BLOCK_SIZE // 2), 2 * W)
    rounded = factor_rows.astype(jnp.bfloat16)
    whole_blocks = rounded.reshape(2, PR, BLOCK_SIZE // 2, 2 * W).transpose(1, 0, 2, 3).reshape(PR, BLOCK_SIZE, 2 * W)
    positions = jnp.arange(PR, dtype=jnp.int32)

    def update(slot_data):
        column, rows_of, stored = slot_data
        col_match = (row_ids == column) & (column >= 0)
        col_index = jnp.sum(jnp.where(col_match, positions, 0)).astype(jnp.int32)
        col_valid = jnp.any(col_match)
        row_match = (row_ids[None, :] == rows_of[:, None]) & (rows_of[:, None] >= 0)
        row_index = jnp.sum(jnp.where(row_match, positions[None, :], 0), axis=1).astype(jnp.int32)
        row_valid = jnp.any(row_match, axis=1) & col_valid
        col_factor = whole_blocks[col_index].astype(jnp.float32)
        row_factor = whole_blocks[row_index].astype(jnp.float32)
        product = jnp.einsum('rab,jb->raj', row_factor, col_factor)
        return stored - jnp.where(row_valid[:, None, None], product, jnp.float32(0.0))
    new_blocks = lax.map(update, (col_ids, block_rows, blocks))
    return (factor_rows, new_blocks)
```

```python
import functools

import jax
import jax.numpy as jnp
from jax import lax
from jax.experimental import pallas as pl
from jax.experimental.pallas import tpu as pltpu
from jax.sharding import PartitionSpec as P

BLOCK = 128
PANEL = 32
STEP = 8
F32 = jnp.float32
BF16 = jnp.bfloat16
TN = (((0,), (0,)), ((), ()))
NT = (((1,), (1,)), ((), ()))


def halves(value):
    high = value.astype(BF16)
    return high, (value - high.astype(F32)).astype(BF16)


def eliminate(columns, tiles, scratch_diag, scratch_below):
    groups = PANEL // STEP
    sublane = lax.broadcasted_iota(jnp.int32, (STEP, BLOCK), 0)
    for s in range(groups):
        first = s * STEP
        for c in range(STEP):
            scratch_diag[s, c] = columns[first + c][s]
        square = [
            [
                jnp.broadcast_to(scratch_diag[s, c, k : k + 1, :], (STEP, BLOCK)) if k <= c else None
                for c in range(STEP)
            ]
            for k in range(STEP)
        ]
        inverse = []
        for k in range(STEP):
            inverse.append(pl.reciprocal(square[k][k], approx=True))
            for c in range(k + 1, STEP):
                ratio = square[k][c] * inverse[k]
                for d in range(c, STEP):
                    square[c][d] = square[c][d] - ratio * square[k][d]
        ratios = []
        for k in range(STEP):
            now = [None] * groups
            for g in range(s, groups):
                now[g] = columns[first + k][g] * inverse[k]
            now[s] = jnp.where(sublane > k, now[s], 0.0)
            for c in range(k + 1, STEP):
                for g in range(s, groups):
                    columns[first + c][g] = columns[first + c][g] - now[g] * square[k][c]
            ratios.append(now)
            for g in range(s + 1, groups):
                scratch_below[s, k, (g - 1) * STEP : g * STEP, :] = columns[first + k][g]
        for c in range(first + STEP, PANEL):
            for k in range(STEP):
                entry = jnp.broadcast_to(
                    scratch_below[s, k, c - STEP : c - STEP + 1, :], (STEP, BLOCK)
                )
                for g in range(c // STEP, groups):
                    columns[c][g] = columns[c][g] - ratios[k][g] * entry
        pivots = square[0][0]
        for k in range(1, STEP):
            pivots = jnp.where(sublane == k, square[k][k], pivots)
        for t in range(len(tiles[s])):
            for k in range(STEP):
                row = jnp.broadcast_to(tiles[s][t][k : k + 1, :], (STEP, BLOCK))
                for g in range(s, groups):
                    if g == s and k == STEP - 1:
                        continue
                    tiles[g][t] = tiles[g][t] - ratios[k][g] * row
        scale = lax.rsqrt(pivots)
        tiles[s] = [tile * scale for tile in tiles[s]]


def factor_kernel(
    core_ref, own_ref, other_ref, blocks_ref, high_ref, low_ref, copied_ref,
    matrix, work, diag, ahead, scratch_diag, scratch_below, sems,
):
    order = matrix.shape[0]
    half = order // 2
    count = order // BLOCK
    core = core_ref[0]
    copy_blocks = pltpu.make_async_copy(blocks_ref, copied_ref, sems.at[0])
    copy_blocks.start()
    copy_own = pltpu.make_async_copy(own_ref, matrix.at[pl.ds(core * half, half)], sems.at[1])
    copy_other = pltpu.make_async_copy(
        other_ref, matrix.at[pl.ds((1 - core) * half, half)], sems.at[2]
    )
    copy_own.start()
    copy_other.start()
    high_ref[...] = jnp.zeros(high_ref.shape, BF16)
    low_ref[...] = jnp.zeros(low_ref.shape, BF16)
    copy_own.wait()
    copy_other.wait()

    rows_at = lax.broadcasted_iota(jnp.int32, (BLOCK, BLOCK), 0)
    lanes_at = lax.broadcasted_iota(jnp.int32, (BLOCK, BLOCK), 1)
    identity = (rows_at == lanes_at).astype(F32)

    work[...] = matrix[0:BLOCK, :]
    diag[...] = matrix[0:BLOCK, 0:BLOCK]
    work[:, 0:BLOCK] = identity

    def block_step(b, carry):
        nxt = jnp.minimum(b + 1, count - 1)
        next_at = pl.multiple_of(nxt * BLOCK, BLOCK)
        here = pl.multiple_of(b * BLOCK, BLOCK)
        high_ref[:, pl.ds(here, BLOCK)] = jnp.zeros((order, BLOCK), BF16)
        low_ref[:, pl.ds(here, BLOCK)] = jnp.zeros((order, BLOCK), BF16)
        left_high = high_ref[:, pl.ds(next_at, BLOCK)]
        left_low = low_ref[:, pl.ds(next_at, BLOCK)]
        earlier = lax.dot_general(left_high, high_ref[...], TN, preferred_element_type=F32)
        earlier += lax.dot_general(left_low, high_ref[...], TN, preferred_element_type=F32)
        earlier += lax.dot_general(left_high, low_ref[...], TN, preferred_element_type=F32)
        ahead[...] = earlier

        for q in range(BLOCK // PANEL):
            top = q * PANEL
            groups = range(PANEL // STEP)
            tile = diag[top : top + PANEL, :]
            columns = [
                [
                    jnp.broadcast_to(
                        tile[g * STEP : (g + 1) * STEP, top + c : top + c + 1], (STEP, BLOCK)
                    )
                    if g >= c // STEP
                    else None
                    for g in groups
                ]
                for c in range(PANEL)
            ]
            tiles = []
            for g in groups:
                rows = slice(top + g * STEP, top + (g + 1) * STEP)
                tiles.append(
                    [work[rows, t * BLOCK : (t + 1) * BLOCK] for t in range(count)] + [diag[rows, :]]
                )
            eliminate(columns, tiles, scratch_diag, scratch_below)
            for g in groups:
                rows = slice(top + g * STEP, top + (g + 1) * STEP)
                for t in range(count):
                    work[rows, t * BLOCK : (t + 1) * BLOCK] = tiles[g][t]
                diag[rows, :] = tiles[g][count]
            rest = top + PANEL
            if rest < BLOCK:
                left_high, left_low = halves(diag[top:rest, :])
                left = jnp.concatenate([left_high, left_low, left_high], axis=0)
                for target in (diag, work):
                    right_high, right_low = halves(target[top:rest, :])
                    right = jnp.concatenate([right_high, right_high, right_low], axis=0)
                    change = lax.dot_general(left, right, TN, preferred_element_type=F32)
                    target[rest:, :] = target[rest:, :] - change[rest:, :]

        new_high, new_low = halves(work[...])
        high_ref[pl.ds(here, BLOCK), :] = new_high
        low_ref[pl.ds(here, BLOCK), :] = new_low
        left_high = high_ref[pl.ds(here, BLOCK), pl.ds(next_at, BLOCK)]
        left_low = low_ref[pl.ds(here, BLOCK), pl.ds(next_at, BLOCK)]
        left = jnp.concatenate([left_high, left_low, left_high], axis=0)
        right = jnp.concatenate([new_high, new_high, new_low], axis=0)
        latest = lax.dot_general(left, right, TN, preferred_element_type=F32)
        for t in range(count):
            lanes = slice(t * BLOCK, (t + 1) * BLOCK)
            kept = jnp.where(t >= nxt, matrix[pl.ds(next_at, BLOCK), lanes], 0.0)
            work[:, lanes] = kept - ahead[:, lanes] - latest[:, lanes]
        diag[...] = work[:, pl.ds(next_at, BLOCK)]
        work[:, pl.ds(next_at, BLOCK)] = identity
        return carry

    lax.fori_loop(0, count, block_step, 0)
    copy_blocks.wait()


def factor(core, own, other, blocks):
    order = own.shape[1]
    vmem = pl.BlockSpec(memory_space=pltpu.VMEM)
    hbm = pl.BlockSpec(memory_space=pl.ANY)
    return pl.pallas_call(
        factor_kernel,
        out_shape=[
            jax.ShapeDtypeStruct((order, order), BF16),
            jax.ShapeDtypeStruct((order, order), BF16),
            jax.ShapeDtypeStruct(blocks.shape, F32),
        ],
        in_specs=[pl.BlockSpec(memory_space=pltpu.SMEM), hbm, hbm, hbm],
        out_specs=[vmem, vmem, hbm],
        scratch_shapes=[
            pltpu.VMEM((order, order), F32),
            pltpu.VMEM((BLOCK, order), F32),
            pltpu.VMEM((BLOCK, BLOCK), F32),
            pltpu.VMEM((BLOCK, order), F32),
            pltpu.VMEM((PANEL // STEP, STEP, STEP, BLOCK), F32),
            pltpu.VMEM((PANEL // STEP, STEP, PANEL - STEP, BLOCK), F32),
            pltpu.SemaphoreType.DMA((3,)),
        ],
        compiler_params=pltpu.CompilerParams(vmem_limit_bytes=48 * 1024 * 1024),
        cost_estimate=pl.CostEstimate(
            flops=8 * order**3, bytes_accessed=200_000_000, transcendentals=0
        ),
        name="factor",
    )(core, own, other, blocks)


def update_kernel(
    place_ref, row_ids_ref, col_ids_ref, block_rows_ref,
    high_ref, low_ref, rows_ref, blocks_ref, copied_ref,
    own_ref, out_ref,
    rows, rows_high, rows_low, solved, rounded, held, found, row_sems, in_sems, out_sems,
):
    del copied_ref
    blk, core = place_ref[0], place_ref[1]
    n_blk, _, part, order = rows_ref.shape
    chunk = rows.shape[1]
    chunk_rows = chunk * part
    chunks = n_blk // chunk
    slots, stored = block_rows_ref.shape
    pieces = row_ids_ref.shape[0]
    half_rows = blocks_ref.shape[2]

    def load(at, h):
        return pltpu.make_async_copy(
            rows_ref.at[pl.ds(at * chunk, chunk), h], rows.at[h], row_sems.at[h]
        )

    for h in range(2):
        load(0, h).start()

    def fetch(n, slot, r):
        return pltpu.make_async_copy(blocks_ref.at[slot, r], held.at[n], in_sems.at[n])

    def place_of(wanted):
        def look(p, at):
            return jnp.where(row_ids_ref[p] == wanted, p, at)

        return jnp.where(wanted >= 0, lax.fori_loop(0, pieces, look, jnp.int32(-1)), -1)

    def scan_slot(slot, n):
        a = place_of(col_ids_ref[slot])

        def scan_stored(r, n):
            b = jnp.where(a >= 0, place_of(block_rows_ref[slot, r]), -1)

            @pl.when(b >= 0)
            def _():
                found[0, n] = slot
                found[1, n] = r
                found[2, n] = a
                found[3, n] = b
                fetch(n, slot, r).start()

            return jnp.where(b >= 0, n + 1, n)

        return lax.fori_loop(0, jnp.where(a >= 0, stored, 0), scan_stored, n)

    total = lax.fori_loop(0, slots, scan_slot, jnp.int32(0))

    def solve_chunk(at, carry):
        for h in range(2):
            load(at, h).wait()
        high, low = halves(rows[...].reshape(2 * chunk_rows, order))
        rows_high[...] = high
        rows_low[...] = low

        @pl.when(at + 1 < chunks)
        def _():
            for h in range(2):
                load(at + 1, h).start()

        width = 256
        for n in range(order // width):
            cut = slice(n * width, (n + 1) * width)
            deep = (n + 1) * width
            x = lax.dot_general(
                rows_high[:, :deep], high_ref[cut, :deep], NT, preferred_element_type=F32
            )
            x += lax.dot_general(
                rows_low[:, :deep], high_ref[cut, :deep], NT, preferred_element_type=F32
            )
            x += lax.dot_general(
                rows_high[:, :deep], low_ref[cut, :deep], NT, preferred_element_type=F32
            )
            solved[:, cut] = x
            for h in range(2):
                rounded[h, pl.ds(pl.multiple_of(at * chunk_rows, chunk_rows), chunk_rows), cut] = x[
                    h * chunk_rows : (h + 1) * chunk_rows
                ].astype(BF16)

        @pl.when(blk // chunk == at)
        def _():
            start = pl.multiple_of(core * chunk_rows + (blk % chunk) * part, part)
            own_ref[...] = solved[pl.ds(start, part), :]

        return carry

    lax.fori_loop(0, chunks, solve_chunk, 0)

    def store(n):
        return pltpu.make_async_copy(
            held.at[n], out_ref.at[found[0, n], found[1, n]], out_sems.at[n]
        )

    def apply(n, carry):
        fetch(n, found[0, n], found[1, n]).wait()
        a_at = pl.multiple_of(found[2, n] * half_rows, half_rows)
        b_at = pl.multiple_of(found[3, n] * half_rows, half_rows)
        column = rounded[:, pl.ds(a_at, half_rows), :].reshape(2 * half_rows, order)
        row = rounded[core, pl.ds(b_at, half_rows), :]
        held[n] = held[n] - lax.dot_general(row, column, NT, preferred_element_type=F32)
        store(n).start()
        return carry

    lax.fori_loop(0, total, apply, 0)

    def finish(n, carry):
        store(n).wait()
        return carry

    lax.fori_loop(0, total, finish, 0)


def update(place, row_ids, col_ids, block_rows, high, low, gathered, blocks, copied):
    order = high.shape[0]
    n_blk, _, part, _ = gathered.shape
    chunk = min(n_blk, max(1, 512 // part))
    slots, stored = block_rows.shape
    smem = pl.BlockSpec(memory_space=pltpu.SMEM)
    vmem = pl.BlockSpec(memory_space=pltpu.VMEM)
    hbm = pl.BlockSpec(memory_space=pl.ANY)
    return pl.pallas_call(
        update_kernel,
        out_shape=[
            jax.ShapeDtypeStruct((part, order), F32),
            jax.ShapeDtypeStruct(blocks.shape, F32),
        ],
        in_specs=[smem, smem, smem, smem, vmem, vmem, hbm, hbm, hbm],
        out_specs=[vmem, hbm],
        input_output_aliases={8: 1},
        scratch_shapes=[
            pltpu.VMEM((2, chunk, part, order), F32),
            pltpu.VMEM((2 * chunk * part, order), BF16),
            pltpu.VMEM((2 * chunk * part, order), BF16),
            pltpu.VMEM((2 * chunk * part, order), F32),
            pltpu.VMEM((2, n_blk * part, order), BF16),
            pltpu.VMEM((slots * stored,) + blocks.shape[2:], F32),
            pltpu.SMEM((4, slots * stored), jnp.int32),
            pltpu.SemaphoreType.DMA((2,)),
            pltpu.SemaphoreType.DMA((slots * stored,)),
            pltpu.SemaphoreType.DMA((slots * stored,)),
        ],
        compiler_params=pltpu.CompilerParams(vmem_limit_bytes=56 * 1024 * 1024),
        name="update",
    )(place, row_ids, col_ids, block_rows, high, low, gathered, blocks, copied)


def local(diag_block, panel_rows, row_ids, col_ids, block_rows, blocks):
    blk = lax.axis_index("blk").astype(jnp.int32)
    core = lax.axis_index("row").astype(jnp.int32)
    other = lax.ppermute(diag_block, "row", [(0, 1), (1, 0)])
    gathered = lax.all_gather(panel_rows, ("blk", "row"), axis=0, tiled=True)
    n_blk = gathered.shape[0] // 2
    gathered = gathered.reshape((n_blk, 2) + gathered.shape[1:])
    high, low, copied = factor(core[None], diag_block, other, blocks)
    own, new_blocks = update(
        jnp.stack([blk, core]), row_ids, col_ids, block_rows, high, low, gathered, blocks, copied
    )
    return own[None], new_blocks


def solution(mesh):
    return jax.shard_map(
        local,
        mesh=mesh,
        in_specs=(
            P("row", None),
            P("row", "blk", None),
            P(),
            P("blk"),
            P("blk", None),
            P("blk", None, "row", None),
        ),
        out_specs=(P("row", "blk", None), P("blk", None, "row", None)),
        check_vma=False,
    )
```

```python
import functools

import jax
import jax.numpy as jnp
from jax import lax
from jax.experimental import pallas as pl
from jax.experimental.pallas import tpu as pltpu
from jax.sharding import PartitionSpec as P

BLOCK = 128
PANEL = 32
STEP = 8
F32 = jnp.float32
BF16 = jnp.bfloat16
TN = (((0,), (0,)), ((), ()))
NT = (((1,), (1,)), ((), ()))


def halves(value):
    high = value.astype(BF16)
    return high, (value - high.astype(F32)).astype(BF16)


def in_hbm(value):
    return pltpu.with_memory_space_constraint(value, pltpu.HBM)


def repeated(ref, *index):
    *lead, row, lanes = index
    return ref[(*lead, pl.ds(row, STEP, stride=0), lanes)]


def eliminate(columns, tiles, scratch_diag, scratch_below, scratch_rows):
    groups = PANEL // STEP
    sublane = lax.broadcasted_iota(jnp.int32, (STEP, BLOCK), 0)
    for s in range(groups):
        first = s * STEP
        for c in range(STEP):
            scratch_diag[s, c] = columns[first + c][s]
        square = [
            [
                repeated(scratch_diag, s, c, k, slice(None)) if k <= c else None
                for c in range(STEP)
            ]
            for k in range(STEP)
        ]
        inverse = []
        for k in range(STEP):
            inverse.append(pl.reciprocal(square[k][k], approx=True))
            for c in range(k + 1, STEP):
                ratio = square[k][c] * inverse[k]
                for d in range(c, STEP):
                    square[c][d] = square[c][d] - ratio * square[k][d]
        ratios = []
        for k in range(STEP):
            now = [None] * groups
            for g in range(s, groups):
                now[g] = columns[first + k][g] * inverse[k]
            now[s] = jnp.where(sublane > k, now[s], 0.0)
            for c in range(k + 1, STEP):
                for g in range(s, groups):
                    columns[first + c][g] = columns[first + c][g] - now[g] * square[k][c]
            ratios.append(now)
            for g in range(s + 1, groups):
                scratch_below[s, k, (g - 1) * STEP : g * STEP, :] = columns[first + k][g]
        for c in range(first + STEP, PANEL):
            for k in range(STEP):
                entry = repeated(scratch_below, s, k, c - STEP, slice(None))
                for g in range(c // STEP, groups):
                    columns[c][g] = columns[c][g] - ratios[k][g] * entry
        pivots = square[0][0]
        for k in range(1, STEP):
            pivots = jnp.where(sublane == k, square[k][k], pivots)
        for t in range(len(tiles[s])):
            for k in range(STEP):
                scratch_rows[s, t, k % 2] = tiles[s][t]
                row = repeated(scratch_rows, s, t, k % 2, k, slice(None))
                for g in range(s, groups):
                    if g == s and k == STEP - 1:
                        continue
                    tiles[g][t] = tiles[g][t] - ratios[k][g] * row
        scale = lax.rsqrt(pivots)
        tiles[s] = [tile * scale for tile in tiles[s]]


def factor_kernel(
    core_ref, own_ref, other_ref, blocks_ref, high_ref, low_ref, copied_ref,
    work, diag, ahead, scratch_diag, scratch_below, scratch_rows, sem,
):
    order = own_ref.shape[1]
    count = order // BLOCK
    core = core_ref[0]
    copy_blocks = pltpu.make_async_copy(blocks_ref, copied_ref, sem)
    copy_blocks.start()
    high_ref[...] = jnp.zeros(high_ref.shape, BF16)
    low_ref[...] = jnp.zeros(low_ref.shape, BF16)

    def matrix(b, lanes):
        at = pl.multiple_of(b % (count // 2) * BLOCK, BLOCK)
        mine = b // (count // 2) == core
        return jnp.where(mine, own_ref[pl.ds(at, BLOCK), lanes], other_ref[pl.ds(at, BLOCK), lanes])

    rows_at = lax.broadcasted_iota(jnp.int32, (BLOCK, BLOCK), 0)
    lanes_at = lax.broadcasted_iota(jnp.int32, (BLOCK, BLOCK), 1)
    identity = (rows_at == lanes_at).astype(F32)

    work[...] = matrix(0, slice(None))
    diag[...] = work[:, 0:BLOCK]
    work[:, 0:BLOCK] = identity

    def block_step(b, carry):
        nxt = jnp.minimum(b + 1, count - 1)
        next_at = pl.multiple_of(nxt * BLOCK, BLOCK)
        here = pl.multiple_of(b * BLOCK, BLOCK)
        high_ref[:, pl.ds(here, BLOCK)] = jnp.zeros((order, BLOCK), BF16)
        low_ref[:, pl.ds(here, BLOCK)] = jnp.zeros((order, BLOCK), BF16)
        left_high = high_ref[:, pl.ds(next_at, BLOCK)]
        left_low = low_ref[:, pl.ds(next_at, BLOCK)]
        earlier = lax.dot_general(left_high, high_ref[...], TN, preferred_element_type=F32)
        earlier += lax.dot_general(left_low, high_ref[...], TN, preferred_element_type=F32)
        earlier += lax.dot_general(left_high, low_ref[...], TN, preferred_element_type=F32)
        ahead[...] = earlier

        for q in range(BLOCK // PANEL):
            top = q * PANEL
            groups = range(PANEL // STEP)
            tile = diag[top : top + PANEL, :]
            columns = [
                [
                    jnp.broadcast_to(
                        tile[g * STEP : (g + 1) * STEP, top + c : top + c + 1], (STEP, BLOCK)
                    )
                    if g >= c // STEP
                    else None
                    for g in groups
                ]
                for c in range(PANEL)
            ]
            tiles = []
            for g in groups:
                rows = slice(top + g * STEP, top + (g + 1) * STEP)
                tiles.append(
                    [work[rows, t * BLOCK : (t + 1) * BLOCK] for t in range(count)] + [diag[rows, :]]
                )
            eliminate(columns, tiles, scratch_diag, scratch_below, scratch_rows)
            for g in groups:
                rows = slice(top + g * STEP, top + (g + 1) * STEP)
                for t in range(count):
                    work[rows, t * BLOCK : (t + 1) * BLOCK] = tiles[g][t]
                diag[rows, :] = tiles[g][count]
            rest = top + PANEL
            if rest < BLOCK:
                left_high, left_low = halves(diag[top:rest, :])
                left = jnp.concatenate([left_high, left_low, left_high], axis=0)
                for target in (diag, work):
                    right_high, right_low = halves(target[top:rest, :])
                    right = jnp.concatenate([right_high, right_high, right_low], axis=0)
                    change = lax.dot_general(left, right, TN, preferred_element_type=F32)
                    target[rest:, :] = target[rest:, :] - change[rest:, :]

        new_high, new_low = halves(work[...])
        high_ref[pl.ds(here, BLOCK), :] = new_high
        low_ref[pl.ds(here, BLOCK), :] = new_low
        left_high = high_ref[pl.ds(here, BLOCK), pl.ds(next_at, BLOCK)]
        left_low = low_ref[pl.ds(here, BLOCK), pl.ds(next_at, BLOCK)]
        left = jnp.concatenate([left_high, left_low, left_high], axis=0)
        right = jnp.concatenate([new_high, new_high, new_low], axis=0)
        latest = lax.dot_general(left, right, TN, preferred_element_type=F32)
        for t in range(count):
            lanes = slice(t * BLOCK, (t + 1) * BLOCK)
            kept = jnp.where(t >= nxt, matrix(nxt, lanes), 0.0)
            work[:, lanes] = kept - ahead[:, lanes] - latest[:, lanes]
        diag[...] = work[:, pl.ds(next_at, BLOCK)]
        work[:, pl.ds(next_at, BLOCK)] = identity
        return carry

    lax.fori_loop(0, count, block_step, 0)
    copy_blocks.wait()


def factor(core, own, other, blocks):
    order = own.shape[1]
    vmem = pl.BlockSpec(memory_space=pltpu.VMEM)
    hbm = pl.BlockSpec(memory_space=pltpu.HBM)
    return pl.pallas_call(
        factor_kernel,
        out_shape=[
            jax.ShapeDtypeStruct((order, order), BF16),
            jax.ShapeDtypeStruct((order, order), BF16),
            jax.ShapeDtypeStruct(blocks.shape, F32),
        ],
        in_specs=[pl.BlockSpec(memory_space=pltpu.SMEM), vmem, vmem, hbm],
        out_specs=[vmem, vmem, hbm],
        scratch_shapes=[
            pltpu.VMEM((BLOCK, order), F32),
            pltpu.VMEM((BLOCK, BLOCK), F32),
            pltpu.VMEM((BLOCK, order), F32),
            pltpu.VMEM((PANEL // STEP, STEP, STEP, BLOCK), F32),
            pltpu.VMEM((PANEL // STEP, STEP, PANEL - STEP, BLOCK), F32),
            pltpu.VMEM((PANEL // STEP, order // BLOCK + 1, 2, STEP, BLOCK), F32),
            pltpu.SemaphoreType.DMA,
        ],
        compiler_params=pltpu.CompilerParams(vmem_limit_bytes=20 * 1024 * 1024),
        cost_estimate=pl.CostEstimate(
            flops=8 * order**3, bytes_accessed=200_000_000, transcendentals=0
        ),
        name="factor",
    )(core, own, other, in_hbm(blocks))


def update_kernel(
    place_ref, row_ids_ref, col_ids_ref, block_rows_ref,
    high_ref, low_ref, rows_ref, blocks_ref, copied_ref,
    own_ref, out_ref,
    rows, rows_high, rows_low, solved, rounded, held, found, row_sems, in_sems, out_sems,
):
    del copied_ref
    blk, core = place_ref[0], place_ref[1]
    n_blk, _, part, order = rows_ref.shape
    chunk = rows.shape[1]
    chunk_rows = chunk * part
    chunks = n_blk // chunk
    slots, stored = block_rows_ref.shape
    pieces = row_ids_ref.shape[0]
    half_rows = blocks_ref.shape[2]

    def load(at, h):
        return pltpu.make_async_copy(
            rows_ref.at[pl.ds(at * chunk, chunk), h], rows.at[h], row_sems.at[h]
        )

    for h in range(2):
        load(0, h).start()

    def fetch(n, slot, r):
        return pltpu.make_async_copy(blocks_ref.at[slot, r], held.at[n], in_sems.at[n])

    def place_of(wanted):
        def look(p, at):
            return jnp.where(row_ids_ref[p] == wanted, p, at)

        return jnp.where(wanted >= 0, lax.fori_loop(0, pieces, look, jnp.int32(-1)), -1)

    def scan_slot(slot, n):
        a = place_of(col_ids_ref[slot])

        def scan_stored(r, n):
            b = jnp.where(a >= 0, place_of(block_rows_ref[slot, r]), -1)

            @pl.when(b >= 0)
            def _():
                found[0, n] = slot
                found[1, n] = r
                found[2, n] = a
                found[3, n] = b
                fetch(n, slot, r).start()

            return jnp.where(b >= 0, n + 1, n)

        return lax.fori_loop(0, jnp.where(a >= 0, stored, 0), scan_stored, n)

    total = lax.fori_loop(0, slots, scan_slot, jnp.int32(0))

    def solve_chunk(at, carry):
        for h in range(2):
            load(at, h).wait()
        high, low = halves(rows[...].reshape(2 * chunk_rows, order))
        rows_high[...] = high
        rows_low[...] = low

        @pl.when(at + 1 < chunks)
        def _():
            for h in range(2):
                load(at + 1, h).start()

        width = 256
        for n in range(order // width):
            cut = slice(n * width, (n + 1) * width)
            deep = (n + 1) * width
            x = lax.dot_general(
                rows_high[:, :deep], high_ref[cut, :deep], NT, preferred_element_type=F32
            )
            x += lax.dot_general(
                rows_low[:, :deep], high_ref[cut, :deep], NT, preferred_element_type=F32
            )
            x += lax.dot_general(
                rows_high[:, :deep], low_ref[cut, :deep], NT, preferred_element_type=F32
            )
            solved[:, cut] = x
            for h in range(2):
                rounded[h, pl.ds(pl.multiple_of(at * chunk_rows, chunk_rows), chunk_rows), cut] = x[
                    h * chunk_rows : (h + 1) * chunk_rows
                ].astype(BF16)

        @pl.when(blk // chunk == at)
        def _():
            start = pl.multiple_of(core * chunk_rows + (blk % chunk) * part, part)
            own_ref[...] = solved[pl.ds(start, part), :]

        return carry

    lax.fori_loop(0, chunks, solve_chunk, 0)

    def store(n):
        return pltpu.make_async_copy(
            held.at[n], out_ref.at[found[0, n], found[1, n]], out_sems.at[n]
        )

    def apply(n, carry):
        fetch(n, found[0, n], found[1, n]).wait()
        a_at = pl.multiple_of(found[2, n] * half_rows, half_rows)
        b_at = pl.multiple_of(found[3, n] * half_rows, half_rows)
        column = rounded[:, pl.ds(a_at, half_rows), :].reshape(2 * half_rows, order)
        row = rounded[core, pl.ds(b_at, half_rows), :]
        held[n] = held[n] - lax.dot_general(row, column, NT, preferred_element_type=F32)
        store(n).start()
        return carry

    lax.fori_loop(0, total, apply, 0)

    def finish(n, carry):
        store(n).wait()
        return carry

    lax.fori_loop(0, total, finish, 0)


def update(place, row_ids, col_ids, block_rows, high, low, gathered, blocks, copied):
    order = high.shape[0]
    n_blk, _, part, _ = gathered.shape
    chunk = min(n_blk, max(1, 512 // part))
    slots, stored = block_rows.shape
    vmem_bytes = 4 * 5 * chunk * part * order * 2 + 4 * n_blk * part * order
    vmem_bytes += blocks.size * 4 + 8 * order * order + 4 * 1024 * 1024
    smem = pl.BlockSpec(memory_space=pltpu.SMEM)
    vmem = pl.BlockSpec(memory_space=pltpu.VMEM)
    hbm = pl.BlockSpec(memory_space=pltpu.HBM)
    return pl.pallas_call(
        update_kernel,
        out_shape=[
            jax.ShapeDtypeStruct((part, order), F32),
            jax.ShapeDtypeStruct(blocks.shape, F32),
        ],
        in_specs=[smem, smem, smem, smem, vmem, vmem, hbm, hbm, hbm],
        out_specs=[vmem, hbm],
        input_output_aliases={8: 1},
        scratch_shapes=[
            pltpu.VMEM((2, chunk, part, order), F32),
            pltpu.VMEM((2 * chunk * part, order), BF16),
            pltpu.VMEM((2 * chunk * part, order), BF16),
            pltpu.VMEM((2 * chunk * part, order), F32),
            pltpu.VMEM((2, n_blk * part, order), BF16),
            pltpu.VMEM((slots * stored,) + blocks.shape[2:], F32),
            pltpu.SMEM((4, slots * stored), jnp.int32),
            pltpu.SemaphoreType.DMA((2,)),
            pltpu.SemaphoreType.DMA((slots * stored,)),
            pltpu.SemaphoreType.DMA((slots * stored,)),
        ],
        compiler_params=pltpu.CompilerParams(vmem_limit_bytes=min(vmem_bytes, 60 * 1024 * 1024)),
        name="update",
    )(place, row_ids, col_ids, block_rows, high, low, in_hbm(gathered), in_hbm(blocks), in_hbm(copied))


def local(diag_block, panel_rows, row_ids, col_ids, block_rows, blocks):
    blk = lax.axis_index("blk").astype(jnp.int32)
    core = lax.axis_index("row").astype(jnp.int32)
    other = lax.ppermute(diag_block, "row", [(0, 1), (1, 0)])
    gathered = lax.all_gather(panel_rows, ("blk", "row"), axis=0, tiled=True)
    n_blk = gathered.shape[0] // 2
    gathered = gathered.reshape((n_blk, 2) + gathered.shape[1:])
    high, low, copied = factor(core[None], diag_block, other, blocks)
    own, new_blocks = update(
        jnp.stack([blk, core]), row_ids, col_ids, block_rows, high, low, gathered, blocks, copied
    )
    return own[None], new_blocks


def solution(mesh):
    return jax.shard_map(
        local,
        mesh=mesh,
        in_specs=(
            P("row", None),
            P("row", "blk", None),
            P(),
            P("blk"),
            P("blk", None),
            P("blk", None, "row", None),
        ),
        out_specs=(P("row", "blk", None), P("blk", None, "row", None)),
        check_vma=False,
    )
```

```python
import functools

import jax
import jax.numpy as jnp
from jax import lax
from jax.experimental import pallas as pl
from jax.experimental.pallas import tpu as pltpu
from jax.sharding import PartitionSpec as P

BLOCK = 128
PANEL = 32
STEP = 8
F32 = jnp.float32
BF16 = jnp.bfloat16
TN = (((0,), (0,)), ((), ()))
NT = (((1,), (1,)), ((), ()))


def halves(value):
    high = value.astype(BF16)
    return high, (value - high.astype(F32)).astype(BF16)


def in_hbm(value):
    return pltpu.with_memory_space_constraint(value, pltpu.HBM)


def repeated(ref, *index):
    *lead, row, lanes = index
    return ref[(*lead, pl.ds(row, STEP, stride=0), lanes)]


def eliminate(columns, tiles, scratch_diag, scratch_below, scratch_rows):
    groups = PANEL // STEP
    sublane = lax.broadcasted_iota(jnp.int32, (STEP, BLOCK), 0)
    for s in range(groups):
        first = s * STEP
        for c in range(STEP):
            scratch_diag[s, c] = columns[first + c][s]
        square = [
            [
                repeated(scratch_diag, s, c, k, slice(None)) if k <= c else None
                for c in range(STEP)
            ]
            for k in range(STEP)
        ]
        inverse = []
        for k in range(STEP):
            inverse.append(pl.reciprocal(square[k][k], approx=True))
            for c in range(k + 1, STEP):
                ratio = square[k][c] * inverse[k]
                for d in range(c, STEP):
                    square[c][d] = square[c][d] - ratio * square[k][d]
        ratios = []
        for k in range(STEP):
            now = [None] * groups
            for g in range(s, groups):
                now[g] = columns[first + k][g] * inverse[k]
            now[s] = jnp.where(sublane > k, now[s], 0.0)
            for c in range(k + 1, STEP):
                for g in range(s, groups):
                    columns[first + c][g] = columns[first + c][g] - now[g] * square[k][c]
            ratios.append(now)
            for g in range(s + 1, groups):
                scratch_below[s, k, (g - 1) * STEP : g * STEP, :] = columns[first + k][g]
        for c in range(first + STEP, PANEL):
            for k in range(STEP):
                entry = repeated(scratch_below, s, k, c - STEP, slice(None))
                for g in range(c // STEP, groups):
                    columns[c][g] = columns[c][g] - ratios[k][g] * entry
        pivots = square[0][0]
        for k in range(1, STEP):
            pivots = jnp.where(sublane == k, square[k][k], pivots)
        for t in range(len(tiles[s])):
            for k in range(STEP):
                scratch_rows[s, t, k % 2] = tiles[s][t]
                row = repeated(scratch_rows, s, t, k % 2, k, slice(None))
                for g in range(s, groups):
                    if g == s and k == STEP - 1:
                        continue
                    tiles[g][t] = tiles[g][t] - ratios[k][g] * row
        scale = lax.rsqrt(pivots)
        tiles[s] = [tile * scale for tile in tiles[s]]


def times_transposed(high, low, right_high, right_low):
    width = right_high.shape[0]
    both = lax.dot_general(
        high, jnp.concatenate([right_high, right_low], axis=0), NT, preferred_element_type=F32
    )
    return (
        both[:, :width]
        + both[:, width:]
        + lax.dot_general(low, right_high, NT, preferred_element_type=F32)
    )


def invert_diagonal(diag, unit, scratch_diag, scratch_below, scratch_rows):
    groups = range(PANEL // STEP)
    for q in range(BLOCK // PANEL):
        top = q * PANEL
        rest = top + PANEL
        tile = diag[top:rest, :]
        columns = [
            [
                jnp.broadcast_to(
                    tile[g * STEP : (g + 1) * STEP, top + c : top + c + 1], (STEP, BLOCK)
                )
                if g >= c // STEP
                else None
                for g in groups
            ]
            for c in range(PANEL)
        ]
        cuts = [slice(top + g * STEP, top + (g + 1) * STEP) for g in groups]
        tiles = [[diag[cut, :], unit[cut, :]] for cut in cuts]
        eliminate(columns, tiles, scratch_diag, scratch_below, scratch_rows)
        for g, cut in enumerate(cuts):
            diag[cut, :] = tiles[g][0]
            unit[cut, :] = tiles[g][1]
        if rest < BLOCK:
            left_high, left_low = halves(diag[top:rest, :])
            left = jnp.concatenate([left_high, left_low, left_high], axis=0)
            for target in (diag, unit):
                right_high, right_low = halves(target[top:rest, :])
                right = jnp.concatenate([right_high, right_high, right_low], axis=0)
                change = lax.dot_general(left, right, TN, preferred_element_type=F32)
                target[rest:, :] = target[rest:, :] - change[rest:, :]


def factor_kernel(
    core_ref, own_ref, other_ref, blocks_ref, high_ref, low_ref, copied_ref,
    base, ahead, diag, unit, scratch_diag, scratch_below, scratch_rows, sem,
):
    order = own_ref.shape[1]
    half = order // 2
    count = order // BLOCK
    core = core_ref[0]
    copy_blocks = pltpu.make_async_copy(blocks_ref, copied_ref, sem)
    copy_blocks.start()
    high_ref[...] = jnp.zeros(high_ref.shape, BF16)
    low_ref[...] = jnp.zeros(low_ref.shape, BF16)
    row_at = lax.broadcasted_iota(jnp.int32, (half, BLOCK), 0)
    identity = (
        lax.broadcasted_iota(jnp.int32, (BLOCK, BLOCK), 0)
        == lax.broadcasted_iota(jnp.int32, (BLOCK, BLOCK), 1)
    ).astype(F32)

    def matrix_column(at):
        mine, theirs = own_ref[:, pl.ds(at, BLOCK)], other_ref[:, pl.ds(at, BLOCK)]
        first = core == 0
        top = jnp.where(first, mine, theirs)
        bottom = jnp.where(first, theirs, mine)
        return jnp.where(row_at >= at, top, 0.0), jnp.where(row_at + half >= at, bottom, 0.0)

    base[:half], base[half:] = matrix_column(0)
    diag[...] = base[:BLOCK]
    base[:BLOCK] = identity

    def block_step(b, carry):
        here = pl.multiple_of(b * BLOCK, BLOCK)
        next_at = pl.multiple_of(jnp.minimum(b + 1, count - 1) * BLOCK, BLOCK)
        high_ref[pl.ds(here, BLOCK), :] = jnp.zeros((BLOCK, order), BF16)
        low_ref[pl.ds(here, BLOCK), :] = jnp.zeros((BLOCK, order), BF16)
        ahead[...] = times_transposed(
            high_ref[...],
            low_ref[...],
            high_ref[pl.ds(next_at, BLOCK), :],
            low_ref[pl.ds(next_at, BLOCK), :],
        )

        unit[...] = identity
        invert_diagonal(diag, unit, scratch_diag, scratch_below, scratch_rows)

        new_high, new_low = halves(times_transposed(*halves(base[...]), *halves(unit[...])))
        high_ref[:, pl.ds(here, BLOCK)] = new_high
        low_ref[:, pl.ds(here, BLOCK)] = new_low
        latest = times_transposed(
            new_high,
            new_low,
            high_ref[pl.ds(next_at, BLOCK), pl.ds(here, BLOCK)],
            low_ref[pl.ds(next_at, BLOCK), pl.ds(here, BLOCK)],
        )
        top, bottom = matrix_column(next_at)
        base[:half] = top - ahead[:half] - latest[:half]
        base[half:] = bottom - ahead[half:] - latest[half:]
        diag[...] = base[pl.ds(next_at, BLOCK), :]
        base[pl.ds(next_at, BLOCK), :] = identity
        return carry

    lax.fori_loop(0, count, block_step, 0)
    copy_blocks.wait()


def factor(core, own, other, blocks):
    order = own.shape[1]
    vmem = pl.BlockSpec(memory_space=pltpu.VMEM)
    hbm = pl.BlockSpec(memory_space=pltpu.HBM)
    return pl.pallas_call(
        factor_kernel,
        out_shape=[
            jax.ShapeDtypeStruct((order, order), BF16),
            jax.ShapeDtypeStruct((order, order), BF16),
            jax.ShapeDtypeStruct(blocks.shape, F32),
        ],
        in_specs=[pl.BlockSpec(memory_space=pltpu.SMEM), vmem, vmem, hbm],
        out_specs=[vmem, vmem, hbm],
        scratch_shapes=[
            pltpu.VMEM((order, BLOCK), F32),
            pltpu.VMEM((order, BLOCK), F32),
            pltpu.VMEM((BLOCK, BLOCK), F32),
            pltpu.VMEM((BLOCK, BLOCK), F32),
            pltpu.VMEM((PANEL // STEP, STEP, STEP, BLOCK), F32),
            pltpu.VMEM((PANEL // STEP, STEP, PANEL - STEP, BLOCK), F32),
            pltpu.VMEM((PANEL // STEP, 2, 2, STEP, BLOCK), F32),
            pltpu.SemaphoreType.DMA,
        ],
        compiler_params=pltpu.CompilerParams(vmem_limit_bytes=20 * 1024 * 1024),
        cost_estimate=pl.CostEstimate(
            flops=8 * order**3, bytes_accessed=200_000_000, transcendentals=0
        ),
        name="factor",
    )(core, own, other, in_hbm(blocks))


def update_kernel(
    place_ref, row_ids_ref, col_ids_ref, block_rows_ref,
    high_ref, low_ref, rows_ref, blocks_ref, copied_ref,
    own_ref, out_ref,
    rows, rows_high, rows_low, solved, rounded, held, found, row_sems, in_sems, out_sems,
):
    del copied_ref
    blk, core = place_ref[0], place_ref[1]
    n_blk, _, part, order = rows_ref.shape
    chunk = rows.shape[1]
    chunk_rows = chunk * part
    chunks = n_blk // chunk
    slots, stored = block_rows_ref.shape
    pieces = row_ids_ref.shape[0]
    half_rows = blocks_ref.shape[2]

    def load(at, h):
        return pltpu.make_async_copy(
            rows_ref.at[pl.ds(at * chunk, chunk), h], rows.at[h], row_sems.at[h]
        )

    for h in range(2):
        load(0, h).start()

    def fetch(n, slot, r):
        return pltpu.make_async_copy(blocks_ref.at[slot, r], held.at[n], in_sems.at[n])

    def place_of(wanted):
        def look(p, at):
            return jnp.where(row_ids_ref[p] == wanted, p, at)

        return jnp.where(wanted >= 0, lax.fori_loop(0, pieces, look, jnp.int32(-1)), -1)

    def scan_slot(slot, n):
        a = place_of(col_ids_ref[slot])

        def scan_stored(r, n):
            b = jnp.where(a >= 0, place_of(block_rows_ref[slot, r]), -1)

            @pl.when(b >= 0)
            def _():
                found[0, n] = slot
                found[1, n] = r
                found[2, n] = a
                found[3, n] = b
                fetch(n, slot, r).start()

            return jnp.where(b >= 0, n + 1, n)

        return lax.fori_loop(0, jnp.where(a >= 0, stored, 0), scan_stored, n)

    total = lax.fori_loop(0, slots, scan_slot, jnp.int32(0))

    def solve_chunk(at, carry):
        for h in range(2):
            load(at, h).wait()
        high, low = halves(rows[...].reshape(2 * chunk_rows, order))
        rows_high[...] = high
        rows_low[...] = low

        @pl.when(at + 1 < chunks)
        def _():
            for h in range(2):
                load(at + 1, h).start()

        width = 256
        for n in range(order // width):
            cut = slice(n * width, (n + 1) * width)
            deep = (n + 1) * width
            x = jnp.dot(
                rows_high[:, :deep], high_ref[:deep, cut], preferred_element_type=F32
            )
            x += jnp.dot(rows_low[:, :deep], high_ref[:deep, cut], preferred_element_type=F32)
            x += jnp.dot(rows_high[:, :deep], low_ref[:deep, cut], preferred_element_type=F32)
            solved[:, cut] = x
            for h in range(2):
                rounded[h, pl.ds(pl.multiple_of(at * chunk_rows, chunk_rows), chunk_rows), cut] = x[
                    h * chunk_rows : (h + 1) * chunk_rows
                ].astype(BF16)

        @pl.when(blk // chunk == at)
        def _():
            start = pl.multiple_of(core * chunk_rows + (blk % chunk) * part, part)
            own_ref[...] = solved[pl.ds(start, part), :]

        return carry

    lax.fori_loop(0, chunks, solve_chunk, 0)

    def store(n):
        return pltpu.make_async_copy(
            held.at[n], out_ref.at[found[0, n], found[1, n]], out_sems.at[n]
        )

    def apply(n, carry):
        fetch(n, found[0, n], found[1, n]).wait()
        a_at = pl.multiple_of(found[2, n] * half_rows, half_rows)
        b_at = pl.multiple_of(found[3, n] * half_rows, half_rows)
        column = rounded[:, pl.ds(a_at, half_rows), :].reshape(2 * half_rows, order)
        row = rounded[core, pl.ds(b_at, half_rows), :]
        held[n] = held[n] - lax.dot_general(row, column, NT, preferred_element_type=F32)
        store(n).start()
        return carry

    lax.fori_loop(0, total, apply, 0)

    def finish(n, carry):
        store(n).wait()
        return carry

    lax.fori_loop(0, total, finish, 0)


def update(place, row_ids, col_ids, block_rows, high, low, gathered, blocks, copied):
    order = high.shape[0]
    n_blk, _, part, _ = gathered.shape
    chunk = min(n_blk, max(1, 512 // part))
    slots, stored = block_rows.shape
    vmem_bytes = 4 * 5 * chunk * part * order * 2 + 4 * n_blk * part * order
    vmem_bytes += blocks.size * 4 + 8 * order * order + 4 * 1024 * 1024
    smem = pl.BlockSpec(memory_space=pltpu.SMEM)
    vmem = pl.BlockSpec(memory_space=pltpu.VMEM)
    hbm = pl.BlockSpec(memory_space=pltpu.HBM)
    return pl.pallas_call(
        update_kernel,
        out_shape=[
            jax.ShapeDtypeStruct((part, order), F32),
            jax.ShapeDtypeStruct(blocks.shape, F32),
        ],
        in_specs=[smem, smem, smem, smem, vmem, vmem, hbm, hbm, hbm],
        out_specs=[vmem, hbm],
        input_output_aliases={8: 1},
        scratch_shapes=[
            pltpu.VMEM((2, chunk, part, order), F32),
            pltpu.VMEM((2 * chunk * part, order), BF16),
            pltpu.VMEM((2 * chunk * part, order), BF16),
            pltpu.VMEM((2 * chunk * part, order), F32),
            pltpu.VMEM((2, n_blk * part, order), BF16),
            pltpu.VMEM((slots * stored,) + blocks.shape[2:], F32),
            pltpu.SMEM((4, slots * stored), jnp.int32),
            pltpu.SemaphoreType.DMA((2,)),
            pltpu.SemaphoreType.DMA((slots * stored,)),
            pltpu.SemaphoreType.DMA((slots * stored,)),
        ],
        compiler_params=pltpu.CompilerParams(vmem_limit_bytes=min(vmem_bytes, 60 * 1024 * 1024)),
        name="update",
    )(place, row_ids, col_ids, block_rows, high, low, in_hbm(gathered), in_hbm(blocks), in_hbm(copied))


def local(diag_block, panel_rows, row_ids, col_ids, block_rows, blocks):
    blk = lax.axis_index("blk").astype(jnp.int32)
    core = lax.axis_index("row").astype(jnp.int32)
    other = lax.ppermute(diag_block, "row", [(0, 1), (1, 0)])
    gathered = lax.all_gather(panel_rows, ("blk", "row"), axis=0, tiled=True)
    n_blk = gathered.shape[0] // 2
    gathered = gathered.reshape((n_blk, 2) + gathered.shape[1:])
    high, low, copied = factor(core[None], diag_block, other, blocks)
    own, new_blocks = update(
        jnp.stack([blk, core]), row_ids, col_ids, block_rows, high, low, gathered, blocks, copied
    )
    return own[None], new_blocks


def solution(mesh):
    return jax.shard_map(
        local,
        mesh=mesh,
        in_specs=(
            P("row", None),
            P("row", "blk", None),
            P(),
            P("blk"),
            P("blk", None),
            P("blk", None, "row", None),
        ),
        out_specs=(P("row", "blk", None), P("blk", None, "row", None)),
        check_vma=False,
    )
```

```python
import functools

import jax
import jax.numpy as jnp
from jax import lax
from jax.experimental import pallas as pl
from jax.experimental.pallas import tpu as pltpu
from jax.sharding import PartitionSpec as P

BLOCK = 128
PANEL = 32
STEP = 8
F32 = jnp.float32
BF16 = jnp.bfloat16
TN = (((0,), (0,)), ((), ()))
NT = (((1,), (1,)), ((), ()))


def halves(value):
    high = value.astype(BF16)
    return high, (value - high.astype(F32)).astype(BF16)


def in_hbm(value):
    return pltpu.with_memory_space_constraint(value, pltpu.HBM)


def repeated(ref, *index):
    *lead, row, lanes = index
    return ref[(*lead, pl.ds(row, STEP, stride=0), lanes)]


def eliminate(columns, tiles, scratch_diag, scratch_below, scratch_rows):
    groups = PANEL // STEP
    sublane = lax.broadcasted_iota(jnp.int32, (STEP, BLOCK), 0)
    for s in range(groups):
        first = s * STEP
        for c in range(STEP):
            scratch_diag[s, c] = columns[first + c][s]
        square = [
            [
                repeated(scratch_diag, s, c, k, slice(None)) if k <= c else None
                for c in range(STEP)
            ]
            for k in range(STEP)
        ]
        inverse = []
        for k in range(STEP):
            inverse.append(pl.reciprocal(square[k][k], approx=True))
            for c in range(k + 1, STEP):
                ratio = square[k][c] * inverse[k]
                for d in range(c, STEP):
                    square[c][d] = square[c][d] - ratio * square[k][d]
        ratios = []
        for k in range(STEP):
            now = [None] * groups
            for g in range(s, groups):
                now[g] = columns[first + k][g] * inverse[k]
            now[s] = jnp.where(sublane > k, now[s], 0.0)
            for c in range(k + 1, STEP):
                for g in range(s, groups):
                    columns[first + c][g] = columns[first + c][g] - now[g] * square[k][c]
            ratios.append(now)
            for g in range(s + 1, groups):
                scratch_below[s, k, (g - 1) * STEP : g * STEP, :] = columns[first + k][g]
        for c in range(first + STEP, PANEL):
            for k in range(STEP):
                entry = repeated(scratch_below, s, k, c - STEP, slice(None))
                for g in range(c // STEP, groups):
                    columns[c][g] = columns[c][g] - ratios[k][g] * entry
        pivots = square[0][0]
        for k in range(1, STEP):
            pivots = jnp.where(sublane == k, square[k][k], pivots)
        for t in range(len(tiles[s])):
            for k in range(STEP):
                scratch_rows[s, t, k % 2] = tiles[s][t]
                row = repeated(scratch_rows, s, t, k % 2, k, slice(None))
                for g in range(s, groups):
                    if g == s and k == STEP - 1:
                        continue
                    tiles[g][t] = tiles[g][t] - ratios[k][g] * row
        scale = lax.rsqrt(pivots)
        tiles[s] = [tile * scale for tile in tiles[s]]


def times_transposed(high, low, right_high, right_low):
    width = right_high.shape[0]
    both = lax.dot_general(
        high, jnp.concatenate([right_high, right_low], axis=0), NT, preferred_element_type=F32
    )
    return (
        both[:, :width]
        + both[:, width:]
        + lax.dot_general(low, right_high, NT, preferred_element_type=F32)
    )


def invert_diagonal(diag, unit, scratch_diag, scratch_below, scratch_rows):
    groups = range(PANEL // STEP)
    for q in range(BLOCK // PANEL):
        top = q * PANEL
        rest = top + PANEL
        tile = diag[top:rest, :]
        columns = [
            [
                jnp.broadcast_to(
                    tile[g * STEP : (g + 1) * STEP, top + c : top + c + 1], (STEP, BLOCK)
                )
                if g >= c // STEP
                else None
                for g in groups
            ]
            for c in range(PANEL)
        ]
        cuts = [slice(top + g * STEP, top + (g + 1) * STEP) for g in groups]
        tiles = [[diag[cut, :], unit[cut, :]] for cut in cuts]
        eliminate(columns, tiles, scratch_diag, scratch_below, scratch_rows)
        for g, cut in enumerate(cuts):
            diag[cut, :] = tiles[g][0]
            unit[cut, :] = tiles[g][1]
        if rest < BLOCK:
            left_high, left_low = halves(diag[top:rest, :])
            left = jnp.concatenate([left_high, left_low, left_high], axis=0)
            for target in (diag, unit):
                right_high, right_low = halves(target[top:rest, :])
                right = jnp.concatenate([right_high, right_high, right_low], axis=0)
                change = lax.dot_general(left, right, TN, preferred_element_type=F32)
                target[rest:, :] = target[rest:, :] - change[rest:, :]


def factor_kernel(
    core_ref, own_ref, other_ref, blocks_ref, high_ref, low_ref, copied_ref,
    base, ahead, diag, unit, scratch_diag, scratch_below, scratch_rows, held, sems,
):
    order = own_ref.shape[1]
    half = order // 2
    count = order // BLOCK
    core = core_ref[0]
    fetch_blocks = pltpu.make_async_copy(blocks_ref, held, sems.at[0])
    store_blocks = pltpu.make_async_copy(held, copied_ref, sems.at[1])
    fetch_blocks.start()
    high_ref[...] = jnp.zeros(high_ref.shape, BF16)
    low_ref[...] = jnp.zeros(low_ref.shape, BF16)
    row_at = lax.broadcasted_iota(jnp.int32, (half, BLOCK), 0)
    identity = (
        lax.broadcasted_iota(jnp.int32, (BLOCK, BLOCK), 0)
        == lax.broadcasted_iota(jnp.int32, (BLOCK, BLOCK), 1)
    ).astype(F32)

    def matrix_column(at):
        mine, theirs = own_ref[:, pl.ds(at, BLOCK)], other_ref[:, pl.ds(at, BLOCK)]
        first = core == 0
        top = jnp.where(first, mine, theirs)
        bottom = jnp.where(first, theirs, mine)
        return jnp.where(row_at >= at, top, 0.0), jnp.where(row_at + half >= at, bottom, 0.0)

    base[:half], base[half:] = matrix_column(0)
    diag[...] = base[:BLOCK]
    base[:BLOCK] = identity

    def block_step(b, carry):
        here = pl.multiple_of(b * BLOCK, BLOCK)
        next_at = pl.multiple_of(jnp.minimum(b + 1, count - 1) * BLOCK, BLOCK)
        @pl.when(b == 1)
        def _():
            fetch_blocks.wait()
            store_blocks.start()

        high_ref[pl.ds(here, BLOCK), :] = jnp.zeros((BLOCK, order), BF16)
        low_ref[pl.ds(here, BLOCK), :] = jnp.zeros((BLOCK, order), BF16)
        ahead[...] = times_transposed(
            high_ref[...],
            low_ref[...],
            high_ref[pl.ds(next_at, BLOCK), :],
            low_ref[pl.ds(next_at, BLOCK), :],
        )

        unit[...] = identity
        invert_diagonal(diag, unit, scratch_diag, scratch_below, scratch_rows)

        new_high, new_low = halves(times_transposed(*halves(base[...]), *halves(unit[...])))
        high_ref[:, pl.ds(here, BLOCK)] = new_high
        low_ref[:, pl.ds(here, BLOCK)] = new_low
        latest = times_transposed(
            new_high,
            new_low,
            high_ref[pl.ds(next_at, BLOCK), pl.ds(here, BLOCK)],
            low_ref[pl.ds(next_at, BLOCK), pl.ds(here, BLOCK)],
        )
        top, bottom = matrix_column(next_at)
        base[:half] = top - ahead[:half] - latest[:half]
        base[half:] = bottom - ahead[half:] - latest[half:]
        diag[...] = base[pl.ds(next_at, BLOCK), :]
        base[pl.ds(next_at, BLOCK), :] = identity
        return carry

    lax.fori_loop(0, count, block_step, 0)
    store_blocks.wait()


def factor(core, own, other, blocks):
    order = own.shape[1]
    vmem = pl.BlockSpec(memory_space=pltpu.VMEM)
    hbm = pl.BlockSpec(memory_space=pltpu.HBM)
    return pl.pallas_call(
        factor_kernel,
        out_shape=[
            jax.ShapeDtypeStruct((order, order), BF16),
            jax.ShapeDtypeStruct((order, order), BF16),
            jax.ShapeDtypeStruct(blocks.shape, F32),
        ],
        in_specs=[pl.BlockSpec(memory_space=pltpu.SMEM), vmem, vmem, hbm],
        out_specs=[vmem, vmem, hbm],
        scratch_shapes=[
            pltpu.VMEM((order, BLOCK), F32),
            pltpu.VMEM((order, BLOCK), F32),
            pltpu.VMEM((BLOCK, BLOCK), F32),
            pltpu.VMEM((BLOCK, BLOCK), F32),
            pltpu.VMEM((PANEL // STEP, STEP, STEP, BLOCK), F32),
            pltpu.VMEM((PANEL // STEP, STEP, PANEL - STEP, BLOCK), F32),
            pltpu.VMEM((PANEL // STEP, 2, 2, STEP, BLOCK), F32),
            pltpu.VMEM(blocks.shape, F32),
            pltpu.SemaphoreType.DMA((2,)),
        ],
        compiler_params=pltpu.CompilerParams(
            vmem_limit_bytes=20 * 1024 * 1024 + 4 * blocks.size
        ),
        cost_estimate=pl.CostEstimate(
            flops=8 * order**3, bytes_accessed=200_000_000, transcendentals=0
        ),
        name="factor",
    )(core, own, other, in_hbm(blocks))


def update_kernel(
    place_ref, row_ids_ref, col_ids_ref, block_rows_ref,
    high_ref, low_ref, rows_ref, blocks_ref, copied_ref,
    own_ref, out_ref,
    rows, rows_high, rows_low, solved, rounded, held, found, row_sems, in_sems, out_sems,
):
    del copied_ref
    blk, core = place_ref[0], place_ref[1]
    n_blk, _, part, order = rows_ref.shape
    chunk = rows.shape[1]
    chunk_rows = chunk * part
    chunks = n_blk // chunk
    slots, stored = block_rows_ref.shape
    pieces = row_ids_ref.shape[0]
    half_rows = blocks_ref.shape[2]

    def load(at, h):
        return pltpu.make_async_copy(
            rows_ref.at[pl.ds(at * chunk, chunk), h], rows.at[h], row_sems.at[h]
        )

    for h in range(2):
        load(0, h).start()

    def fetch(n, slot, r):
        return pltpu.make_async_copy(blocks_ref.at[slot, r], held.at[n], in_sems.at[n])

    def place_of(wanted):
        def look(p, at):
            return jnp.where(row_ids_ref[p] == wanted, p, at)

        return jnp.where(wanted >= 0, lax.fori_loop(0, pieces, look, jnp.int32(-1)), -1)

    def scan_slot(slot, n):
        a = place_of(col_ids_ref[slot])

        def scan_stored(r, n):
            b = jnp.where(a >= 0, place_of(block_rows_ref[slot, r]), -1)

            @pl.when(b >= 0)
            def _():
                found[0, n] = slot
                found[1, n] = r
                found[2, n] = a
                found[3, n] = b
                fetch(n, slot, r).start()

            return jnp.where(b >= 0, n + 1, n)

        return lax.fori_loop(0, jnp.where(a >= 0, stored, 0), scan_stored, n)

    total = lax.fori_loop(0, slots, scan_slot, jnp.int32(0))

    def solve_chunk(at, carry):
        for h in range(2):
            load(at, h).wait()
        high, low = halves(rows[...].reshape(2 * chunk_rows, order))
        rows_high[...] = high
        rows_low[...] = low

        @pl.when(at + 1 < chunks)
        def _():
            for h in range(2):
                load(at + 1, h).start()

        width = 256
        for n in range(order // width):
            cut = slice(n * width, (n + 1) * width)
            deep = (n + 1) * width
            x = jnp.dot(
                rows_high[:, :deep], high_ref[:deep, cut], preferred_element_type=F32
            )
            x += jnp.dot(rows_low[:, :deep], high_ref[:deep, cut], preferred_element_type=F32)
            x += jnp.dot(rows_high[:, :deep], low_ref[:deep, cut], preferred_element_type=F32)
            solved[:, cut] = x
            for h in range(2):
                rounded[h, pl.ds(pl.multiple_of(at * chunk_rows, chunk_rows), chunk_rows), cut] = x[
                    h * chunk_rows : (h + 1) * chunk_rows
                ].astype(BF16)

        @pl.when(blk // chunk == at)
        def _():
            start = pl.multiple_of(core * chunk_rows + (blk % chunk) * part, part)
            own_ref[...] = solved[pl.ds(start, part), :]

        return carry

    lax.fori_loop(0, chunks, solve_chunk, 0)

    def store(n):
        return pltpu.make_async_copy(
            held.at[n], out_ref.at[found[0, n], found[1, n]], out_sems.at[n]
        )

    def apply(n, carry):
        fetch(n, found[0, n], found[1, n]).wait()
        a_at = pl.multiple_of(found[2, n] * half_rows, half_rows)
        b_at = pl.multiple_of(found[3, n] * half_rows, half_rows)
        column = rounded[:, pl.ds(a_at, half_rows), :].reshape(2 * half_rows, order)
        row = rounded[core, pl.ds(b_at, half_rows), :]
        held[n] = held[n] - lax.dot_general(row, column, NT, preferred_element_type=F32)
        store(n).start()
        return carry

    lax.fori_loop(0, total, apply, 0)

    def finish(n, carry):
        store(n).wait()
        return carry

    lax.fori_loop(0, total, finish, 0)


def update(place, row_ids, col_ids, block_rows, high, low, gathered, blocks, copied):
    order = high.shape[0]
    n_blk, _, part, _ = gathered.shape
    chunk = min(n_blk, max(1, 512 // part))
    slots, stored = block_rows.shape
    vmem_bytes = 4 * 5 * chunk * part * order * 2 + 4 * n_blk * part * order
    vmem_bytes += blocks.size * 4 + 8 * order * order + 4 * 1024 * 1024
    smem = pl.BlockSpec(memory_space=pltpu.SMEM)
    vmem = pl.BlockSpec(memory_space=pltpu.VMEM)
    hbm = pl.BlockSpec(memory_space=pltpu.HBM)
    return pl.pallas_call(
        update_kernel,
        out_shape=[
            jax.ShapeDtypeStruct((part, order), F32),
            jax.ShapeDtypeStruct(blocks.shape, F32),
        ],
        in_specs=[smem, smem, smem, smem, vmem, vmem, hbm, hbm, hbm],
        out_specs=[vmem, hbm],
        input_output_aliases={8: 1},
        scratch_shapes=[
            pltpu.VMEM((2, chunk, part, order), F32),
            pltpu.VMEM((2 * chunk * part, order), BF16),
            pltpu.VMEM((2 * chunk * part, order), BF16),
            pltpu.VMEM((2 * chunk * part, order), F32),
            pltpu.VMEM((2, n_blk * part, order), BF16),
            pltpu.VMEM((slots * stored,) + blocks.shape[2:], F32),
            pltpu.SMEM((4, slots * stored), jnp.int32),
            pltpu.SemaphoreType.DMA((2,)),
            pltpu.SemaphoreType.DMA((slots * stored,)),
            pltpu.SemaphoreType.DMA((slots * stored,)),
        ],
        compiler_params=pltpu.CompilerParams(vmem_limit_bytes=min(vmem_bytes, 60 * 1024 * 1024)),
        name="update",
    )(place, row_ids, col_ids, block_rows, high, low, in_hbm(gathered), in_hbm(blocks), in_hbm(copied))


def local(diag_block, panel_rows, row_ids, col_ids, block_rows, blocks):
    blk = lax.axis_index("blk").astype(jnp.int32)
    core = lax.axis_index("row").astype(jnp.int32)
    other = lax.ppermute(diag_block, "row", [(0, 1), (1, 0)])
    gathered = lax.all_gather(panel_rows, ("blk", "row"), axis=0, tiled=True)
    n_blk = gathered.shape[0] // 2
    gathered = gathered.reshape((n_blk, 2) + gathered.shape[1:])
    high, low, copied = factor(core[None], diag_block, other, blocks)
    own, new_blocks = update(
        jnp.stack([blk, core]), row_ids, col_ids, block_rows, high, low, gathered, blocks, copied
    )
    return own[None], new_blocks


def solution(mesh):
    return jax.shard_map(
        local,
        mesh=mesh,
        in_specs=(
            P("row", None),
            P("row", "blk", None),
            P(),
            P("blk"),
            P("blk", None),
            P("blk", None, "row", None),
        ),
        out_specs=(P("row", "blk", None), P("blk", None, "row", None)),
        check_vma=False,
    )
```

```python
import functools

import jax
import jax.numpy as jnp
from jax import lax
from jax.experimental import pallas as pl
from jax.experimental.pallas import tpu as pltpu
from jax.sharding import PartitionSpec as P

BLOCK = 128
PANEL = 32
STEP = 8
F32 = jnp.float32
BF16 = jnp.bfloat16
TN = (((0,), (0,)), ((), ()))
NT = (((1,), (1,)), ((), ()))


def halves(value):
    high = value.astype(BF16)
    return high, (value - high.astype(F32)).astype(BF16)


def in_hbm(value):
    return pltpu.with_memory_space_constraint(value, pltpu.HBM)


def repeated(ref, *index):
    *lead, row, lanes = index
    return ref[(*lead, pl.ds(row, STEP, stride=0), lanes)]


def eliminate(columns, tiles, scratch_diag, scratch_below, scratch_rows):
    groups = PANEL // STEP
    sublane = lax.broadcasted_iota(jnp.int32, (STEP, BLOCK), 0)
    for s in range(groups):
        first = s * STEP
        for c in range(STEP):
            scratch_diag[s, c] = columns[first + c][s]
        square = [
            [
                repeated(scratch_diag, s, c, k, slice(None)) if k <= c else None
                for c in range(STEP)
            ]
            for k in range(STEP)
        ]
        inverse = []
        for k in range(STEP):
            inverse.append(pl.reciprocal(square[k][k], approx=True))
            for c in range(k + 1, STEP):
                ratio = square[k][c] * inverse[k]
                for d in range(c, STEP):
                    square[c][d] = square[c][d] - ratio * square[k][d]
        ratios = []
        for k in range(STEP):
            now = [None] * groups
            for g in range(s, groups):
                now[g] = columns[first + k][g] * inverse[k]
            now[s] = jnp.where(sublane > k, now[s], 0.0)
            for c in range(k + 1, STEP):
                for g in range(s, groups):
                    columns[first + c][g] = columns[first + c][g] - now[g] * square[k][c]
            ratios.append(now)
            for g in range(s + 1, groups):
                scratch_below[s, k, (g - 1) * STEP : g * STEP, :] = columns[first + k][g]
        for c in range(first + STEP, PANEL):
            for k in range(STEP):
                entry = repeated(scratch_below, s, k, c - STEP, slice(None))
                for g in range(c // STEP, groups):
                    columns[c][g] = columns[c][g] - ratios[k][g] * entry
        pivots = square[0][0]
        for k in range(1, STEP):
            pivots = jnp.where(sublane == k, square[k][k], pivots)
        for t in range(len(tiles[s])):
            for k in range(STEP):
                scratch_rows[s, t, k % 2] = tiles[s][t]
                row = repeated(scratch_rows, s, t, k % 2, k, slice(None))
                for g in range(s, groups):
                    if g == s and k == STEP - 1:
                        continue
                    tiles[g][t] = tiles[g][t] - ratios[k][g] * row
        scale = lax.rsqrt(pivots)
        tiles[s] = [tile * scale for tile in tiles[s]]


def times_transposed(high, low, right_high, right_low):
    width = right_high.shape[0]
    both = lax.dot_general(
        high, jnp.concatenate([right_high, right_low], axis=0), NT, preferred_element_type=F32
    )
    return (
        both[:, :width]
        + both[:, width:]
        + lax.dot_general(low, right_high, NT, preferred_element_type=F32)
    )


def invert_diagonal(diag, unit, scratch_diag, scratch_below, scratch_rows):
    groups = range(PANEL // STEP)
    for q in range(BLOCK // PANEL):
        top = q * PANEL
        rest = top + PANEL
        tile = diag[top:rest, :]
        columns = [
            [
                jnp.broadcast_to(
                    tile[g * STEP : (g + 1) * STEP, top + c : top + c + 1], (STEP, BLOCK)
                )
                if g >= c // STEP
                else None
                for g in groups
            ]
            for c in range(PANEL)
        ]
        cuts = [slice(top + g * STEP, top + (g + 1) * STEP) for g in groups]
        tiles = [[diag[cut, :], unit[cut, :]] for cut in cuts]
        eliminate(columns, tiles, scratch_diag, scratch_below, scratch_rows)
        for g, cut in enumerate(cuts):
            diag[cut, :] = tiles[g][0]
            unit[cut, :] = tiles[g][1]
        if rest < BLOCK:
            left_high, left_low = halves(diag[top:rest, :])
            left = jnp.concatenate([left_high, left_low, left_high], axis=0)
            for target in (diag, unit):
                right_high, right_low = halves(target[top:rest, :])
                right = jnp.concatenate([right_high, right_high, right_low], axis=0)
                change = lax.dot_general(left, right, TN, preferred_element_type=F32)
                target[rest:, :] = target[rest:, :] - change[rest:, :]


def factor_kernel(
    core_ref, own_ref, other_ref, blocks_ref, high_ref, low_ref, copied_ref,
    matrix, base, ahead, diag, unit, scratch_diag, scratch_below, scratch_rows, held, sems, tile_sems,
):
    order = own_ref.shape[1]
    half = order // 2
    count = order // BLOCK
    core = core_ref[0]
    fetch_blocks = pltpu.make_async_copy(blocks_ref, held, sems.at[0])
    store_blocks = pltpu.make_async_copy(held, copied_ref, sems.at[1])

    def fetch_tile(t, which):
        lanes = pl.ds(pl.multiple_of(t * BLOCK, BLOCK), BLOCK)
        source = (own_ref, other_ref)[which]
        at = pl.multiple_of((core if which == 0 else 1 - core) * half, half)
        return pltpu.make_async_copy(
            source.at[:, lanes], matrix.at[t, pl.ds(at, half), :], tile_sems.at[t, which]
        )

    for t in range(count):
        for which in range(2):
            fetch_tile(t, which).start()
    fetch_blocks.start()
    high_ref[...] = jnp.zeros(high_ref.shape, BF16)
    low_ref[...] = jnp.zeros(low_ref.shape, BF16)
    identity = (
        lax.broadcasted_iota(jnp.int32, (BLOCK, BLOCK), 0)
        == lax.broadcasted_iota(jnp.int32, (BLOCK, BLOCK), 1)
    ).astype(F32)

    row_at = lax.broadcasted_iota(jnp.int32, (order, BLOCK), 0)
    for which in range(2):
        fetch_tile(0, which).wait()
    base[...] = matrix[0]
    diag[...] = base[:BLOCK]
    base[:BLOCK] = identity

    def block_step(b, carry):
        here = pl.multiple_of(b * BLOCK, BLOCK)
        following = jnp.minimum(b + 1, count - 1)
        next_at = pl.multiple_of(following * BLOCK, BLOCK)

        @pl.when(b + 1 < count)
        def _():
            for which in range(2):
                fetch_tile(b + 1, which).wait()

        @pl.when(b == 1)
        def _():
            fetch_blocks.wait()
            store_blocks.start()

        high_ref[pl.ds(here, BLOCK), :] = jnp.zeros((BLOCK, order), BF16)
        low_ref[pl.ds(here, BLOCK), :] = jnp.zeros((BLOCK, order), BF16)
        ahead[...] = times_transposed(
            high_ref[...],
            low_ref[...],
            high_ref[pl.ds(next_at, BLOCK), :],
            low_ref[pl.ds(next_at, BLOCK), :],
        )

        unit[...] = identity
        invert_diagonal(diag, unit, scratch_diag, scratch_below, scratch_rows)

        new_high, new_low = halves(times_transposed(*halves(base[...]), *halves(unit[...])))
        high_ref[:, pl.ds(here, BLOCK)] = new_high
        low_ref[:, pl.ds(here, BLOCK)] = new_low
        latest = times_transposed(
            new_high,
            new_low,
            high_ref[pl.ds(next_at, BLOCK), pl.ds(here, BLOCK)],
            low_ref[pl.ds(next_at, BLOCK), pl.ds(here, BLOCK)],
        )
        kept = jnp.where(row_at >= next_at, matrix[following], 0.0)
        base[...] = kept - ahead[...] - latest
        diag[...] = base[pl.ds(next_at, BLOCK), :]
        base[pl.ds(next_at, BLOCK), :] = identity
        return carry

    lax.fori_loop(0, count, block_step, 0)
    store_blocks.wait()


def factor(core, own, other, blocks):
    order = own.shape[1]
    vmem = pl.BlockSpec(memory_space=pltpu.VMEM)
    hbm = pl.BlockSpec(memory_space=pltpu.HBM)
    return pl.pallas_call(
        factor_kernel,
        out_shape=[
            jax.ShapeDtypeStruct((order, order), BF16),
            jax.ShapeDtypeStruct((order, order), BF16),
            jax.ShapeDtypeStruct(blocks.shape, F32),
        ],
        in_specs=[
            pl.BlockSpec(memory_space=pltpu.SMEM), hbm, pl.BlockSpec(memory_space=pl.ANY), hbm
        ],
        out_specs=[vmem, vmem, hbm],
        scratch_shapes=[
            pltpu.VMEM((order // BLOCK, order, BLOCK), F32),
            pltpu.VMEM((order, BLOCK), F32),
            pltpu.VMEM((order, BLOCK), F32),
            pltpu.VMEM((BLOCK, BLOCK), F32),
            pltpu.VMEM((BLOCK, BLOCK), F32),
            pltpu.VMEM((PANEL // STEP, STEP, STEP, BLOCK), F32),
            pltpu.VMEM((PANEL // STEP, STEP, PANEL - STEP, BLOCK), F32),
            pltpu.VMEM((PANEL // STEP, 2, 2, STEP, BLOCK), F32),
            pltpu.VMEM(blocks.shape, F32),
            pltpu.SemaphoreType.DMA((2,)),
            pltpu.SemaphoreType.DMA((order // BLOCK, 2)),
        ],
        compiler_params=pltpu.CompilerParams(
            vmem_limit_bytes=16 * 1024 * 1024 + 4 * blocks.size
        ),
        cost_estimate=pl.CostEstimate(
            flops=8 * order**3, bytes_accessed=200_000_000, transcendentals=0
        ),
        name="factor",
    )(core, in_hbm(own), other, in_hbm(blocks))


def solve_kernel(
    blk_ref, high_ref, low_ref, rows_ref, own_ref, rounded_ref,
    rows, rows_high, rows_low, solved, row_sem,
):
    blk = blk_ref[0]
    n_blk, part, order = rows_ref.shape
    chunk = rows.shape[0]
    chunk_rows = chunk * part
    chunks = n_blk // chunk

    def load(at):
        return pltpu.make_async_copy(rows_ref.at[pl.ds(at * chunk, chunk)], rows, row_sem)

    load(0).start()

    def solve_chunk(at, carry):
        load(at).wait()
        rows_high[...], rows_low[...] = halves(rows[...].reshape(chunk_rows, order))

        @pl.when(at + 1 < chunks)
        def _():
            load(at + 1).start()

        width = 256
        for n in range(order // width):
            cut = slice(n * width, (n + 1) * width)
            deep = (n + 1) * width
            x = jnp.dot(
                rows_high[:, :deep], high_ref[:deep, cut], preferred_element_type=F32
            )
            x += jnp.dot(rows_low[:, :deep], high_ref[:deep, cut], preferred_element_type=F32)
            x += jnp.dot(rows_high[:, :deep], low_ref[:deep, cut], preferred_element_type=F32)
            solved[:, cut] = x
            rounded_ref[pl.ds(pl.multiple_of(at * chunk_rows, chunk_rows), chunk_rows), cut] = (
                x.astype(BF16)
            )

        @pl.when(blk // chunk == at)
        def _():
            own_ref[...] = solved[pl.ds(pl.multiple_of(blk % chunk * part, part), part), :]

        return carry

    lax.fori_loop(0, chunks, solve_chunk, 0)


def solve(blk, high, low, gathered):
    order = high.shape[0]
    n_blk, part, _ = gathered.shape
    chunk = min(n_blk, max(1, 512 // part))
    smem = pl.BlockSpec(memory_space=pltpu.SMEM)
    vmem = pl.BlockSpec(memory_space=pltpu.VMEM)
    hbm = pl.BlockSpec(memory_space=pltpu.HBM)
    return pl.pallas_call(
        solve_kernel,
        out_shape=[
            jax.ShapeDtypeStruct((part, order), F32),
            jax.ShapeDtypeStruct((n_blk * part, order), BF16),
        ],
        in_specs=[smem, vmem, vmem, hbm],
        out_specs=[vmem, vmem],
        scratch_shapes=[
            pltpu.VMEM((chunk, part, order), F32),
            pltpu.VMEM((chunk * part, order), BF16),
            pltpu.VMEM((chunk * part, order), BF16),
            pltpu.VMEM((chunk * part, order), F32),
            pltpu.SemaphoreType.DMA,
        ],
        compiler_params=pltpu.CompilerParams(vmem_limit_bytes=24 * 1024 * 1024),
        name="solve",
    )(blk, high, low, in_hbm(gathered))


def update_kernel(
    core_ref, row_ids_ref, col_ids_ref, block_rows_ref,
    mine_ref, theirs_ref, blocks_ref, copied_ref, out_ref,
    held, found, in_sems, out_sems,
):
    del copied_ref
    core = core_ref[0]
    slots, stored = block_rows_ref.shape
    pieces = row_ids_ref.shape[0]
    half_rows = blocks_ref.shape[2]

    def fetch(n, slot, r):
        return pltpu.make_async_copy(blocks_ref.at[slot, r], held.at[n], in_sems.at[n])

    def place_of(wanted):
        def look(p, at):
            return jnp.where(row_ids_ref[p] == wanted, p, at)

        return jnp.where(wanted >= 0, lax.fori_loop(0, pieces, look, jnp.int32(-1)), -1)

    def scan_slot(slot, n):
        a = place_of(col_ids_ref[slot])

        def scan_stored(r, n):
            b = jnp.where(a >= 0, place_of(block_rows_ref[slot, r]), -1)

            @pl.when(b >= 0)
            def _():
                found[0, n] = slot
                found[1, n] = r
                found[2, n] = a
                found[3, n] = b
                fetch(n, slot, r).start()

            return jnp.where(b >= 0, n + 1, n)

        return lax.fori_loop(0, jnp.where(a >= 0, stored, 0), scan_stored, n)

    total = lax.fori_loop(0, slots, scan_slot, jnp.int32(0))

    def store(n):
        return pltpu.make_async_copy(
            held.at[n], out_ref.at[found[0, n], found[1, n]], out_sems.at[n]
        )

    def apply(n, carry):
        a_rows = pl.ds(pl.multiple_of(found[2, n] * half_rows, half_rows), half_rows)
        b_rows = pl.ds(pl.multiple_of(found[3, n] * half_rows, half_rows), half_rows)
        row = mine_ref[b_rows, :]
        column = jnp.concatenate([mine_ref[a_rows, :], theirs_ref[a_rows, :]], axis=0)
        change = lax.dot_general(row, column, NT, preferred_element_type=F32)
        fetch(n, found[0, n], found[1, n]).wait()
        for which in range(2):
            at = (core if which == 0 else 1 - core) * half_rows
            lanes = pl.ds(pl.multiple_of(at, half_rows), half_rows)
            part = change[:, which * half_rows : (which + 1) * half_rows]
            held[n, :, lanes] = held[n, :, lanes] - part
        store(n).start()
        return carry

    lax.fori_loop(0, total, apply, 0)

    def finish(n, carry):
        store(n).wait()
        return carry

    lax.fori_loop(0, total, finish, 0)


def update(core, row_ids, col_ids, block_rows, mine, theirs, blocks, copied):
    slots, stored = block_rows.shape
    smem = pl.BlockSpec(memory_space=pltpu.SMEM)
    vmem = pl.BlockSpec(memory_space=pltpu.VMEM)
    hbm = pl.BlockSpec(memory_space=pltpu.HBM)
    return pl.pallas_call(
        update_kernel,
        out_shape=jax.ShapeDtypeStruct(blocks.shape, F32),
        in_specs=[smem, smem, smem, smem, vmem, vmem, hbm, hbm],
        out_specs=hbm,
        input_output_aliases={7: 0},
        scratch_shapes=[
            pltpu.VMEM((slots * stored,) + blocks.shape[2:], F32),
            pltpu.SMEM((4, slots * stored), jnp.int32),
            pltpu.SemaphoreType.DMA((slots * stored,)),
            pltpu.SemaphoreType.DMA((slots * stored,)),
        ],
        compiler_params=pltpu.CompilerParams(
            vmem_limit_bytes=8 * 1024 * 1024 + 4 * blocks.size + 4 * mine.size
        ),
        name="update",
    )(core, row_ids, col_ids, block_rows, mine, theirs, in_hbm(blocks), in_hbm(copied))


def local(diag_block, panel_rows, row_ids, col_ids, block_rows, blocks):
    blk = lax.axis_index("blk").astype(jnp.int32)[None]
    core = lax.axis_index("row").astype(jnp.int32)[None]
    swap = [(0, 1), (1, 0)]
    other = lax.ppermute(diag_block, "row", swap)
    gathered = lax.all_gather(panel_rows, "blk", axis=0, tiled=True)
    high, low, copied = factor(core, diag_block, other, blocks)
    own, mine = solve(blk, high, low, gathered)
    theirs = lax.ppermute(mine, "row", swap)
    new_blocks = update(core, row_ids, col_ids, block_rows, mine, theirs, blocks, copied)
    return own[None], new_blocks


def solution(mesh):
    return jax.shard_map(
        local,
        mesh=mesh,
        in_specs=(
            P("row", None),
            P("row", "blk", None),
            P(),
            P("blk"),
            P("blk", None),
            P("blk", None, "row", None),
        ),
        out_specs=(P("row", "blk", None), P("blk", None, "row", None)),
        check_vma=False,
    )
```

```python
import functools

import jax
import jax.numpy as jnp
from jax import lax
from jax.experimental import pallas as pl
from jax.experimental.pallas import tpu as pltpu
from jax.sharding import PartitionSpec as P

BLOCK = 128
PANEL = 32
STEP = 8
F32 = jnp.float32
BF16 = jnp.bfloat16
TN = (((0,), (0,)), ((), ()))
NT = (((1,), (1,)), ((), ()))


def halves(value):
    high = value.astype(BF16)
    return high, (value - high.astype(F32)).astype(BF16)


def in_hbm(value):
    return pltpu.with_memory_space_constraint(value, pltpu.HBM)


def in_vmem(value):
    return pltpu.with_memory_space_constraint(value, pltpu.VMEM)


def repeated(ref, *index):
    *lead, row, lanes = index
    return ref[(*lead, pl.ds(row, STEP, stride=0), lanes)]


def eliminate(columns, tiles, scratch_diag, scratch_below, scratch_rows):
    groups = PANEL // STEP
    sublane = lax.broadcasted_iota(jnp.int32, (STEP, BLOCK), 0)
    for s in range(groups):
        first = s * STEP
        for c in range(STEP):
            scratch_diag[s, c] = columns[first + c][s]
        square = [
            [
                repeated(scratch_diag, s, c, k, slice(None)) if k <= c else None
                for c in range(STEP)
            ]
            for k in range(STEP)
        ]
        inverse = []
        for k in range(STEP):
            inverse.append(pl.reciprocal(square[k][k], approx=True))
            for c in range(k + 1, STEP):
                ratio = square[k][c] * inverse[k]
                for d in range(c, STEP):
                    square[c][d] = square[c][d] - ratio * square[k][d]
        ratios = []
        for k in range(STEP):
            now = [None] * groups
            for g in range(s, groups):
                now[g] = columns[first + k][g] * inverse[k]
            now[s] = jnp.where(sublane > k, now[s], 0.0)
            for c in range(k + 1, STEP):
                for g in range(s, groups):
                    columns[first + c][g] = columns[first + c][g] - now[g] * square[k][c]
            ratios.append(now)
            for g in range(s + 1, groups):
                scratch_below[s, k, (g - 1) * STEP : g * STEP, :] = columns[first + k][g]
        for c in range(first + STEP, PANEL):
            for k in range(STEP):
                entry = repeated(scratch_below, s, k, c - STEP, slice(None))
                for g in range(c // STEP, groups):
                    columns[c][g] = columns[c][g] - ratios[k][g] * entry
        pivots = square[0][0]
        for k in range(1, STEP):
            pivots = jnp.where(sublane == k, square[k][k], pivots)
        for t in range(len(tiles[s])):
            for k in range(STEP):
                scratch_rows[s, t, k % 2] = tiles[s][t]
                row = repeated(scratch_rows, s, t, k % 2, k, slice(None))
                for g in range(s, groups):
                    if g == s and k == STEP - 1:
                        continue
                    tiles[g][t] = tiles[g][t] - ratios[k][g] * row
        scale = lax.rsqrt(pivots)
        tiles[s] = [tile * scale for tile in tiles[s]]


def times_transposed(high, low, right_high, right_low):
    width = right_high.shape[0]
    both = lax.dot_general(
        high, jnp.concatenate([right_high, right_low], axis=0), NT, preferred_element_type=F32
    )
    return (
        both[:, :width]
        + both[:, width:]
        + lax.dot_general(low, right_high, NT, preferred_element_type=F32)
    )


def invert_diagonal(diag, unit, scratch_diag, scratch_below, scratch_rows):
    groups = range(PANEL // STEP)
    for q in range(BLOCK // PANEL):
        top = q * PANEL
        rest = top + PANEL
        tile = diag[top:rest, :]
        columns = [
            [
                jnp.broadcast_to(
                    tile[g * STEP : (g + 1) * STEP, top + c : top + c + 1], (STEP, BLOCK)
                )
                if g >= c // STEP
                else None
                for g in groups
            ]
            for c in range(PANEL)
        ]
        cuts = [slice(top + g * STEP, top + (g + 1) * STEP) for g in groups]
        tiles = [[diag[cut, :], unit[cut, :]] for cut in cuts]
        eliminate(columns, tiles, scratch_diag, scratch_below, scratch_rows)
        for g, cut in enumerate(cuts):
            diag[cut, :] = tiles[g][0]
            unit[cut, :] = tiles[g][1]
        if rest < BLOCK:
            left_high, left_low = halves(diag[top:rest, :])
            left = jnp.concatenate([left_high, left_low, left_high], axis=0)
            for target in (diag, unit):
                right_high, right_low = halves(target[top:rest, :])
                right = jnp.concatenate([right_high, right_high, right_low], axis=0)
                change = lax.dot_general(left, right, TN, preferred_element_type=F32)
                target[rest:, :] = target[rest:, :] - change[rest:, :]


def factor_kernel(first, core_ref, own_ref, other_ref, *refs):
    refs = list(refs)
    state_refs = [refs.pop(0) for _ in range(4)] if first else []
    blocks_ref = refs.pop(0) if first else None
    high_ref, low_ref, base, diag = refs[:4]
    refs = refs[4:]
    copied_ref = refs.pop(0) if first else None
    matrix, ahead, unit, scratch_diag, scratch_below, scratch_rows, tile_sems = refs[:7]
    order = own_ref.shape[1]
    half = order // 2
    count = order // BLOCK
    last = high_ref.shape[1] // BLOCK
    core = core_ref[0]

    def fetch_tile(t, which):
        lanes = pl.ds(pl.multiple_of(t * BLOCK, BLOCK), BLOCK)
        source = (own_ref, other_ref)[which]
        at = pl.multiple_of((core if which == 0 else 1 - core) * half, half)
        return pltpu.make_async_copy(
            source.at[:, lanes], matrix.at[t, pl.ds(at, half), :], tile_sems.at[t, which]
        )

    for t in range(first + 1 if first else 0, min(last + 1, count)):
        for which in range(2):
            fetch_tile(t, which).start()
    if first:
        held, block_sems = refs[7:]
        fetch_blocks = pltpu.make_async_copy(blocks_ref, held, block_sems.at[0])
        store_blocks = pltpu.make_async_copy(held, copied_ref, block_sems.at[1])
        fetch_blocks.start()
    identity = (
        lax.broadcasted_iota(jnp.int32, (BLOCK, BLOCK), 0)
        == lax.broadcasted_iota(jnp.int32, (BLOCK, BLOCK), 1)
    ).astype(F32)
    row_at = lax.broadcasted_iota(jnp.int32, (order, BLOCK), 0)

    done = first * BLOCK
    high_ref[:, done:] = jnp.zeros((order, (last - first) * BLOCK), BF16)
    low_ref[:, done:] = jnp.zeros((order, (last - first) * BLOCK), BF16)
    if first:
        high_ref[:, :done] = state_refs[0][...]
        low_ref[:, :done] = state_refs[1][...]
        base[...] = state_refs[2][...]
        diag[...] = state_refs[3][...]
    else:
        for which in range(2):
            fetch_tile(0, which).wait()
        base[...] = matrix[0]
        diag[...] = base[:BLOCK]
        base[:BLOCK] = identity

    def block_step(b, carry):
        here = pl.multiple_of(b * BLOCK, BLOCK)
        following = jnp.minimum(b + 1, count - 1)
        next_at = pl.multiple_of(following * BLOCK, BLOCK)

        @pl.when(b + 1 < count)
        def _():
            for which in range(2):
                fetch_tile(b + 1, which).wait()

        if first:

            @pl.when(b == first + 1)
            def _():
                fetch_blocks.wait()
                store_blocks.start()

        high_ref[pl.ds(here, BLOCK), :] = jnp.zeros((BLOCK, high_ref.shape[1]), BF16)
        low_ref[pl.ds(here, BLOCK), :] = jnp.zeros((BLOCK, high_ref.shape[1]), BF16)
        ahead[...] = times_transposed(
            high_ref[...],
            low_ref[...],
            high_ref[pl.ds(next_at, BLOCK), :],
            low_ref[pl.ds(next_at, BLOCK), :],
        )

        unit[...] = identity
        invert_diagonal(diag, unit, scratch_diag, scratch_below, scratch_rows)

        new_high, new_low = halves(times_transposed(*halves(base[...]), *halves(unit[...])))
        high_ref[:, pl.ds(here, BLOCK)] = new_high
        low_ref[:, pl.ds(here, BLOCK)] = new_low
        latest = times_transposed(
            new_high,
            new_low,
            high_ref[pl.ds(next_at, BLOCK), pl.ds(here, BLOCK)],
            low_ref[pl.ds(next_at, BLOCK), pl.ds(here, BLOCK)],
        )
        kept = jnp.where(row_at >= next_at, matrix[following], 0.0)
        base[...] = kept - ahead[...] - latest
        diag[...] = base[pl.ds(next_at, BLOCK), :]
        base[pl.ds(next_at, BLOCK), :] = identity
        return carry

    lax.fori_loop(first, last, block_step, 0)
    if first:
        store_blocks.wait()


def factor(first, last, core, own, other, state, blocks):
    order = own.shape[1]
    count = order // BLOCK
    vmem = pl.BlockSpec(memory_space=pltpu.VMEM)
    hbm = pl.BlockSpec(memory_space=pltpu.HBM)
    out_shape = [
        pltpu.VMEM((order, last * BLOCK), BF16),
        pltpu.VMEM((order, last * BLOCK), BF16),
        pltpu.VMEM((order, BLOCK), F32),
        pltpu.VMEM((BLOCK, BLOCK), F32),
    ]
    scratch = [
        pltpu.VMEM((count, order, BLOCK), F32),
        pltpu.VMEM((order, BLOCK), F32),
        pltpu.VMEM((BLOCK, BLOCK), F32),
        pltpu.VMEM((PANEL // STEP, STEP, STEP, BLOCK), F32),
        pltpu.VMEM((PANEL // STEP, STEP, PANEL - STEP, BLOCK), F32),
        pltpu.VMEM((PANEL // STEP, 2, 2, STEP, BLOCK), F32),
        pltpu.SemaphoreType.DMA((count, 2)),
    ]
    in_specs = [pl.BlockSpec(memory_space=pltpu.SMEM), hbm, vmem]
    out_specs = [vmem] * 4
    operands = [core, in_hbm(own), in_vmem(other)]
    limit = 12 * 1024 * 1024
    if first:
        in_specs += [vmem] * 4 + [hbm]
        operands += [in_vmem(part) for part in state] + [in_hbm(blocks)]
        out_specs.append(hbm)
        out_shape.append(jax.ShapeDtypeStruct(blocks.shape, F32))
        scratch += [pltpu.VMEM(blocks.shape, F32), pltpu.SemaphoreType.DMA((2,))]
        limit += 4 * blocks.size + 4 * 1024 * 1024
    share = last - first
    return pl.pallas_call(
        functools.partial(factor_kernel, first),
        out_shape=out_shape,
        in_specs=in_specs,
        out_specs=out_specs,
        scratch_shapes=scratch,
        compiler_params=pltpu.CompilerParams(vmem_limit_bytes=limit),
        cost_estimate=pl.CostEstimate(
            flops=share * order**3, bytes_accessed=share * 20_000_000, transcendentals=0
        ),
        name="factor",
    )(*operands)


def solve_kernel(blk_ref, high_ref, low_ref, *refs):
    *piece_refs, own_ref, rounded_ref, rows, rows_high, rows_low, solved, row_sem = refs
    blk = blk_ref[0]
    held, part, order = piece_refs[0].shape
    n_blk = len(piece_refs) * held
    chunk_rows = rows_high.shape[0]
    chunk = chunk_rows // part
    chunks = n_blk // chunk

    def load(at):
        return pltpu.make_async_copy(piece_refs[0].at[pl.ds(at * chunk, chunk)], rows, row_sem)

    def solve_chunk(at, carry):
        if len(piece_refs) == 1:
            load(at).start()
            load(at).wait()
            rows_high[...], rows_low[...] = halves(rows[...].reshape(chunk_rows, order))
        else:
            for k, piece in enumerate(piece_refs):
                for j in range(held):
                    place = blk ^ (k + j * len(piece_refs))
                    here = pl.ds(pl.multiple_of(place * part, part), part)
                    rows_high[here, :], rows_low[here, :] = halves(piece[j])

        width = 256
        for n in range(order // width):
            cut = slice(n * width, (n + 1) * width)
            deep = (n + 1) * width
            x = jnp.dot(
                rows_high[:, :deep], high_ref[:deep, cut], preferred_element_type=F32
            )
            x += jnp.dot(rows_low[:, :deep], high_ref[:deep, cut], preferred_element_type=F32)
            x += jnp.dot(rows_high[:, :deep], low_ref[:deep, cut], preferred_element_type=F32)
            solved[:, cut] = x
            rounded_ref[pl.ds(pl.multiple_of(at * chunk_rows, chunk_rows), chunk_rows), cut] = (
                x.astype(BF16)
            )

        @pl.when(blk // chunk == at)
        def _():
            own_ref[...] = solved[pl.ds(pl.multiple_of(blk % chunk * part, part), part), :]

        return carry

    lax.fori_loop(0, chunks, solve_chunk, 0)


def solve(blk, high, low, pieces):
    order = high.shape[0]
    held, part, _ = pieces[0].shape
    n_blk = len(pieces) * held
    chunk = n_blk if len(pieces) > 1 else min(n_blk, max(1, 512 // part))
    smem = pl.BlockSpec(memory_space=pltpu.SMEM)
    vmem = pl.BlockSpec(memory_space=pltpu.VMEM)
    if len(pieces) > 1:
        piece_spec, row_shape = vmem, (1, 8, BLOCK)
        pieces = [in_vmem(piece) for piece in pieces]
    else:
        piece_spec, row_shape = pl.BlockSpec(memory_space=pltpu.HBM), (chunk, part, order)
        pieces = [in_hbm(piece) for piece in pieces]
    return pl.pallas_call(
        solve_kernel,
        out_shape=[
            jax.ShapeDtypeStruct((part, order), F32),
            pltpu.VMEM((n_blk * part, order), BF16),
        ],
        in_specs=[smem, vmem, vmem] + [piece_spec] * len(pieces),
        out_specs=[vmem, vmem],
        scratch_shapes=[
            pltpu.VMEM(row_shape, F32),
            pltpu.VMEM((chunk * part, order), BF16),
            pltpu.VMEM((chunk * part, order), BF16),
            pltpu.VMEM((chunk * part, order), F32),
            pltpu.SemaphoreType.DMA,
        ],
        compiler_params=pltpu.CompilerParams(vmem_limit_bytes=20 * 1024 * 1024),
        name="solve",
    )(blk, in_vmem(high), in_vmem(low), *pieces)


def pack_kernel(*refs):
    *parts, after_ref, out_ref = refs
    del after_ref
    for j, part in enumerate(parts):
        out_ref[j] = part[0]


def pack(parts, after):
    vmem = pl.BlockSpec(memory_space=pltpu.VMEM)
    return pl.pallas_call(
        pack_kernel,
        out_shape=pltpu.VMEM((len(parts),) + parts[0].shape[1:], parts[0].dtype),
        in_specs=[vmem] * (len(parts) + 1),
        out_specs=vmem,
        name="pack",
    )(*[in_vmem(part) for part in parts], in_vmem(after))


def update_kernel(
    core_ref, row_ids_ref, col_ids_ref, block_rows_ref,
    mine_ref, theirs_ref, blocks_ref, copied_ref, out_ref,
    held, found, in_sems, out_sems,
):
    del copied_ref
    core = core_ref[0]
    slots, stored = block_rows_ref.shape
    pieces = row_ids_ref.shape[0]
    half_rows = blocks_ref.shape[2]

    def fetch(n, slot, r):
        return pltpu.make_async_copy(blocks_ref.at[slot, r], held.at[n], in_sems.at[n])

    def place_of(wanted):
        def look(p, at):
            return jnp.where(row_ids_ref[p] == wanted, p, at)

        return jnp.where(wanted >= 0, lax.fori_loop(0, pieces, look, jnp.int32(-1)), -1)

    def scan_slot(slot, n):
        a = place_of(col_ids_ref[slot])

        def scan_stored(r, n):
            b = jnp.where(a >= 0, place_of(block_rows_ref[slot, r]), -1)

            @pl.when(b >= 0)
            def _():
                found[0, n] = slot
                found[1, n] = r
                found[2, n] = a
                found[3, n] = b
                fetch(n, slot, r).start()

            return jnp.where(b >= 0, n + 1, n)

        return lax.fori_loop(0, jnp.where(a >= 0, stored, 0), scan_stored, n)

    total = lax.fori_loop(0, slots, scan_slot, jnp.int32(0))

    def store(n):
        return pltpu.make_async_copy(
            held.at[n], out_ref.at[found[0, n], found[1, n]], out_sems.at[n]
        )

    def apply(n, carry):
        a_rows = pl.ds(pl.multiple_of(found[2, n] * half_rows, half_rows), half_rows)
        b_rows = pl.ds(pl.multiple_of(found[3, n] * half_rows, half_rows), half_rows)
        row = mine_ref[b_rows, :]
        column = jnp.concatenate([mine_ref[a_rows, :], theirs_ref[a_rows, :]], axis=0)
        change = lax.dot_general(row, column, NT, preferred_element_type=F32)
        fetch(n, found[0, n], found[1, n]).wait()
        for which in range(2):
            at = (core if which == 0 else 1 - core) * half_rows
            lanes = pl.ds(pl.multiple_of(at, half_rows), half_rows)
            part = change[:, which * half_rows : (which + 1) * half_rows]
            held[n, :, lanes] = held[n, :, lanes] - part
        store(n).start()
        return carry

    lax.fori_loop(0, total, apply, 0)

    def finish(n, carry):
        store(n).wait()
        return carry

    lax.fori_loop(0, total, finish, 0)


def update(core, row_ids, col_ids, block_rows, mine, theirs, blocks, copied):
    slots, stored = block_rows.shape
    smem = pl.BlockSpec(memory_space=pltpu.SMEM)
    vmem = pl.BlockSpec(memory_space=pltpu.VMEM)
    hbm = pl.BlockSpec(memory_space=pltpu.HBM)
    return pl.pallas_call(
        update_kernel,
        out_shape=jax.ShapeDtypeStruct(blocks.shape, F32),
        in_specs=[smem, smem, smem, smem, vmem, vmem, hbm, hbm],
        out_specs=hbm,
        input_output_aliases={7: 0},
        scratch_shapes=[
            pltpu.VMEM((slots * stored,) + blocks.shape[2:], F32),
            pltpu.SMEM((4, slots * stored), jnp.int32),
            pltpu.SemaphoreType.DMA((slots * stored,)),
            pltpu.SemaphoreType.DMA((slots * stored,)),
        ],
        compiler_params=pltpu.CompilerParams(
            vmem_limit_bytes=8 * 1024 * 1024 + 4 * blocks.size + 4 * mine.size
        ),
        name="update",
    )(
        core, row_ids, col_ids, block_rows, in_vmem(mine), in_vmem(theirs),
        in_hbm(blocks), in_hbm(copied),
    )


def local(diag_block, panel_rows, row_ids, col_ids, block_rows, blocks):
    blk = lax.axis_index("blk").astype(jnp.int32)[None]
    core = lax.axis_index("row").astype(jnp.int32)[None]
    swap = [(0, 1), (1, 0)]
    n_blk = lax.axis_size("blk")
    count = diag_block.shape[1] // BLOCK
    other = lax.ppermute(diag_block, "row", swap)

    def from_partner(value, k):
        return lax.ppermute(value, "blk", [(i, i ^ k) for i in range(n_blk)])

    in_stages = n_blk in (8, 16)
    near = n_blk // 4
    if in_stages:
        arrived = [from_partner(panel_rows, j * near) for j in range(1, 4)]
    else:
        pieces = [lax.all_gather(panel_rows, "blk", axis=0, tiled=True)]
    state = factor(0, 2, core, diag_block, other, [], blocks)
    if in_stages:
        group = pack([panel_rows] + arrived, state[3])
        pieces = [group] + [from_partner(group, k) for k in range(1, near)]
    high, low, _, _, copied = factor(2, count, core, diag_block, other, state, blocks)
    own, mine = solve(blk, high, low, pieces)
    theirs = lax.ppermute(mine, "row", swap)
    new_blocks = update(core, row_ids, col_ids, block_rows, mine, theirs, blocks, copied)
    return own[None], new_blocks


def solution(mesh):
    return jax.shard_map(
        local,
        mesh=mesh,
        in_specs=(
            P("row", None),
            P("row", "blk", None),
            P(),
            P("blk"),
            P("blk", None),
            P("blk", None, "row", None),
        ),
        out_specs=(P("row", "blk", None), P("blk", None, "row", None)),
        check_vma=False,
    )
```

```python
import functools

import jax
import jax.numpy as jnp
from jax import lax
from jax.experimental import pallas as pl
from jax.experimental.pallas import tpu as pltpu
from jax.sharding import PartitionSpec as P

BLOCK = 128
PANEL = 32
STEP = 8
F32 = jnp.float32
BF16 = jnp.bfloat16
TN = (((0,), (0,)), ((), ()))
NT = (((1,), (1,)), ((), ()))


def halves(value):
    high = value.astype(BF16)
    return high, (value - high.astype(F32)).astype(BF16)


def in_hbm(value):
    return pltpu.with_memory_space_constraint(value, pltpu.HBM)


def in_vmem(value):
    return pltpu.with_memory_space_constraint(value, pltpu.VMEM)


def repeated(ref, *index):
    *lead, row, lanes = index
    return ref[(*lead, pl.ds(row, STEP, stride=0), lanes)]


def eliminate(columns, tiles, scratch_diag, scratch_below, scratch_rows):
    groups = PANEL // STEP
    sublane = lax.broadcasted_iota(jnp.int32, (STEP, BLOCK), 0)
    for s in range(groups):
        first = s * STEP
        for c in range(STEP):
            scratch_diag[s, c] = columns[first + c][s]
        square = [
            [
                repeated(scratch_diag, s, c, k, slice(None)) if k <= c else None
                for c in range(STEP)
            ]
            for k in range(STEP)
        ]
        inverse = []
        for k in range(STEP):
            inverse.append(pl.reciprocal(square[k][k], approx=True))
            for c in range(k + 1, STEP):
                ratio = square[k][c] * inverse[k]
                for d in range(c, STEP):
                    square[c][d] = square[c][d] - ratio * square[k][d]
        ratios = []
        for k in range(STEP):
            now = [None] * groups
            for g in range(s, groups):
                now[g] = columns[first + k][g] * inverse[k]
            now[s] = jnp.where(sublane > k, now[s], 0.0)
            for c in range(k + 1, STEP):
                for g in range(s, groups):
                    columns[first + c][g] = columns[first + c][g] - now[g] * square[k][c]
            ratios.append(now)
            for g in range(s + 1, groups):
                scratch_below[s, k, (g - 1) * STEP : g * STEP, :] = columns[first + k][g]
        for c in range(first + STEP, PANEL):
            for k in range(STEP):
                entry = repeated(scratch_below, s, k, c - STEP, slice(None))
                for g in range(c // STEP, groups):
                    columns[c][g] = columns[c][g] - ratios[k][g] * entry
        pivots = square[0][0]
        for k in range(1, STEP):
            pivots = jnp.where(sublane == k, square[k][k], pivots)
        for t in range(len(tiles[s])):
            for k in range(STEP):
                scratch_rows[s, t, k % 2] = tiles[s][t]
                row = repeated(scratch_rows, s, t, k % 2, k, slice(None))
                for g in range(s, groups):
                    if g == s and k == STEP - 1:
                        continue
                    tiles[g][t] = tiles[g][t] - ratios[k][g] * row
        scale = lax.rsqrt(pivots)
        tiles[s] = [tile * scale for tile in tiles[s]]


def times_transposed(high, low, right_high, right_low):
    width = right_high.shape[0]
    both = lax.dot_general(
        high, jnp.concatenate([right_high, right_low], axis=0), NT, preferred_element_type=F32
    )
    return (
        both[:, :width]
        + both[:, width:]
        + lax.dot_general(low, right_high, NT, preferred_element_type=F32)
    )


def invert_diagonal(diag, unit, scratch_diag, scratch_below, scratch_rows):
    groups = range(PANEL // STEP)
    for q in range(BLOCK // PANEL):
        top = q * PANEL
        rest = top + PANEL
        tile = diag[top:rest, :]
        columns = [
            [
                jnp.broadcast_to(
                    tile[g * STEP : (g + 1) * STEP, top + c : top + c + 1], (STEP, BLOCK)
                )
                if g >= c // STEP
                else None
                for g in groups
            ]
            for c in range(PANEL)
        ]
        cuts = [slice(top + g * STEP, top + (g + 1) * STEP) for g in groups]
        tiles = [[diag[cut, :], unit[cut, :]] for cut in cuts]
        eliminate(columns, tiles, scratch_diag, scratch_below, scratch_rows)
        for g, cut in enumerate(cuts):
            diag[cut, :] = tiles[g][0]
            unit[cut, :] = tiles[g][1]
        if rest < BLOCK:
            left_high, left_low = halves(diag[top:rest, :])
            left = jnp.concatenate([left_high, left_low, left_high], axis=0)
            for target in (diag, unit):
                right_high, right_low = halves(target[top:rest, :])
                right = jnp.concatenate([right_high, right_high, right_low], axis=0)
                change = lax.dot_general(left, right, TN, preferred_element_type=F32)
                target[rest:, :] = target[rest:, :] - change[rest:, :]


def factor_kernel(first, last, core_ref, own_ref, other_ref, *refs):
    refs = list(refs)
    state_refs = [refs.pop(0) for _ in range(6)] if first else []
    blocks_ref = refs.pop(0) if first else None
    high_ref, low_ref, base, prev_high, prev_low, diag = refs[:6]
    refs = refs[6:]
    copied_ref = refs.pop(0) if first else None
    matrix, unit, scratch_diag, scratch_below, scratch_rows, tile_sems = refs[:6]
    order = own_ref.shape[1]
    half = order // 2
    count = order // BLOCK
    width = high_ref.shape[1]
    core = core_ref[0]

    def fetch_tile(t, which):
        lanes = pl.ds(pl.multiple_of(t * BLOCK, BLOCK), BLOCK)
        source = (own_ref, other_ref)[which]
        at = pl.multiple_of((core if which == 0 else 1 - core) * half, half)
        return pltpu.make_async_copy(
            source.at[:, lanes], matrix.at[t, pl.ds(at, half), :], tile_sems.at[t, which]
        )

    for t in range(first, min(last + 1, count)):
        for which in range(2):
            fetch_tile(t, which).start()
    if first:
        held, block_sems = refs[6:]
        fetch_blocks = pltpu.make_async_copy(blocks_ref, held, block_sems.at[0])
        store_blocks = pltpu.make_async_copy(held, copied_ref, block_sems.at[1])
        fetch_blocks.start()
    identity = (
        lax.broadcasted_iota(jnp.int32, (BLOCK, BLOCK), 0)
        == lax.broadcasted_iota(jnp.int32, (BLOCK, BLOCK), 1)
    ).astype(F32)
    row_at = lax.broadcasted_iota(jnp.int32, (order, BLOCK), 0)

    if first:
        done = (first - 1) * BLOCK
        high_ref[:, done:] = jnp.zeros((order, width - done), BF16)
        low_ref[:, done:] = jnp.zeros((order, width - done), BF16)
        high_ref[:, :done] = state_refs[0][...]
        low_ref[:, :done] = state_refs[1][...]
        for into, out_of in zip((base, prev_high, prev_low, diag), state_refs[2:]):
            into[...] = out_of[...]
        for which in range(2):
            fetch_tile(first, which).wait()
    else:
        for ref in (high_ref, low_ref, base, prev_high, prev_low):
            ref[...] = jnp.zeros(ref.shape, ref.dtype)
        for which in range(2):
            fetch_tile(0, which).wait()
        diag[...] = matrix[0, :BLOCK, :]

    def store_previous(b):
        before = pl.multiple_of(jnp.maximum(b - 1, 0) * BLOCK, BLOCK)
        high_ref[pl.ds(before, BLOCK), :] = jnp.zeros((BLOCK, width), BF16)
        low_ref[pl.ds(before, BLOCK), :] = jnp.zeros((BLOCK, width), BF16)
        column = times_transposed(*halves(base[...]), prev_high[...], prev_low[...])
        high, low = halves(column)
        high_ref[:, pl.ds(before, BLOCK)] = high
        low_ref[:, pl.ds(before, BLOCK)] = low

    def block_step(b, carry):
        here = pl.multiple_of(b * BLOCK, BLOCK)
        following = jnp.minimum(b + 1, count - 1)
        next_at = pl.multiple_of(following * BLOCK, BLOCK)

        @pl.when(b + 1 < count)
        def _():
            for which in range(2):
                fetch_tile(b + 1, which).wait()

        if first:

            @pl.when(b == first + 1)
            def _():
                fetch_blocks.wait()
                store_blocks.start()

        store_previous(b)
        earlier = times_transposed(
            high_ref[...],
            low_ref[...],
            high_ref[pl.ds(here, BLOCK), :],
            low_ref[pl.ds(here, BLOCK), :],
        )
        base[...] = jnp.where(row_at >= here, matrix[b], 0.0) - earlier
        base[pl.ds(here, BLOCK), :] = identity
        next_high, next_low = high_ref[pl.ds(next_at, BLOCK), :], low_ref[pl.ds(next_at, BLOCK), :]
        next_diag = matrix[following, pl.ds(next_at, BLOCK), :] - times_transposed(
            next_high, next_low, next_high, next_low
        )

        unit[...] = identity
        invert_diagonal(diag, unit, scratch_diag, scratch_below, scratch_rows)

        high, low = halves(unit[...])
        prev_high[...] = high
        prev_low[...] = low
        below = times_transposed(*halves(base[pl.ds(next_at, BLOCK), :]), high, low)
        high, low = halves(below)
        diag[...] = next_diag - times_transposed(high, low, high, low)
        return carry

    lax.fori_loop(first, last, block_step, 0)
    if last == count:
        store_previous(count)
    if first:
        store_blocks.wait()


def factor(first, last, core, own, other, state, blocks):
    order = own.shape[1]
    count = order // BLOCK
    vmem = pl.BlockSpec(memory_space=pltpu.VMEM)
    hbm = pl.BlockSpec(memory_space=pltpu.HBM)
    columns = (last if last == count else last - 1) * BLOCK
    out_shape = [
        pltpu.VMEM((order, columns), BF16),
        pltpu.VMEM((order, columns), BF16),
        pltpu.VMEM((order, BLOCK), F32),
        pltpu.VMEM((BLOCK, BLOCK), BF16),
        pltpu.VMEM((BLOCK, BLOCK), BF16),
        pltpu.VMEM((BLOCK, BLOCK), F32),
    ]
    scratch = [
        pltpu.VMEM((count, order, BLOCK), F32),
        pltpu.VMEM((BLOCK, BLOCK), F32),
        pltpu.VMEM((PANEL // STEP, STEP, STEP, BLOCK), F32),
        pltpu.VMEM((PANEL // STEP, STEP, PANEL - STEP, BLOCK), F32),
        pltpu.VMEM((PANEL // STEP, 2, 2, STEP, BLOCK), F32),
        pltpu.SemaphoreType.DMA((count, 2)),
    ]
    in_specs = [pl.BlockSpec(memory_space=pltpu.SMEM), hbm, vmem]
    out_specs = [vmem] * len(out_shape)
    operands = [core, in_hbm(own), in_vmem(other)]
    limit = 12 * 1024 * 1024
    if first:
        in_specs += [vmem] * len(state) + [hbm]
        operands += [in_vmem(part) for part in state] + [in_hbm(blocks)]
        out_specs.append(hbm)
        out_shape.append(jax.ShapeDtypeStruct(blocks.shape, F32))
        scratch += [pltpu.VMEM(blocks.shape, F32), pltpu.SemaphoreType.DMA((2,))]
        limit += 4 * blocks.size + 4 * 1024 * 1024
    share = last - first
    return pl.pallas_call(
        functools.partial(factor_kernel, first, last),
        out_shape=out_shape,
        in_specs=in_specs,
        out_specs=out_specs,
        scratch_shapes=scratch,
        compiler_params=pltpu.CompilerParams(vmem_limit_bytes=limit),
        cost_estimate=pl.CostEstimate(
            flops=share * order**3, bytes_accessed=share * 20_000_000, transcendentals=0
        ),
        name="factor",
    )(*operands)


def solve_kernel(blk_ref, high_ref, low_ref, *refs):
    *piece_refs, own_ref, rounded_ref, rows, rows_high, rows_low, solved, row_sem = refs
    blk = blk_ref[0]
    held, part, order = piece_refs[0].shape
    n_blk = len(piece_refs) * held
    chunk_rows = rows_high.shape[0]
    chunk = chunk_rows // part
    chunks = n_blk // chunk

    def load(at):
        return pltpu.make_async_copy(piece_refs[0].at[pl.ds(at * chunk, chunk)], rows, row_sem)

    def solve_chunk(at, carry):
        if len(piece_refs) == 1:
            load(at).start()
            load(at).wait()
            rows_high[...], rows_low[...] = halves(rows[...].reshape(chunk_rows, order))
        else:
            for k, piece in enumerate(piece_refs):
                for j in range(held):
                    place = blk ^ (k + j * len(piece_refs))
                    here = pl.ds(pl.multiple_of(place * part, part), part)
                    rows_high[here, :], rows_low[here, :] = halves(piece[j])

        width = 256
        for n in range(order // width):
            cut = slice(n * width, (n + 1) * width)
            deep = (n + 1) * width
            x = jnp.dot(
                rows_high[:, :deep], high_ref[:deep, cut], preferred_element_type=F32
            )
            x += jnp.dot(rows_low[:, :deep], high_ref[:deep, cut], preferred_element_type=F32)
            x += jnp.dot(rows_high[:, :deep], low_ref[:deep, cut], preferred_element_type=F32)
            solved[:, cut] = x
            rounded_ref[pl.ds(pl.multiple_of(at * chunk_rows, chunk_rows), chunk_rows), cut] = (
                x.astype(BF16)
            )

        @pl.when(blk // chunk == at)
        def _():
            own_ref[...] = solved[pl.ds(pl.multiple_of(blk % chunk * part, part), part), :]

        return carry

    lax.fori_loop(0, chunks, solve_chunk, 0)


def solve(blk, high, low, pieces):
    order = high.shape[0]
    held, part, _ = pieces[0].shape
    n_blk = len(pieces) * held
    chunk = n_blk if len(pieces) > 1 else min(n_blk, max(1, 512 // part))
    smem = pl.BlockSpec(memory_space=pltpu.SMEM)
    vmem = pl.BlockSpec(memory_space=pltpu.VMEM)
    if len(pieces) > 1:
        piece_spec, row_shape = vmem, (1, 8, BLOCK)
        pieces = [in_vmem(piece) for piece in pieces]
    else:
        piece_spec, row_shape = pl.BlockSpec(memory_space=pltpu.HBM), (chunk, part, order)
        pieces = [in_hbm(piece) for piece in pieces]
    return pl.pallas_call(
        solve_kernel,
        out_shape=[
            jax.ShapeDtypeStruct((part, order), F32),
            pltpu.VMEM((n_blk * part, order), BF16),
        ],
        in_specs=[smem, vmem, vmem] + [piece_spec] * len(pieces),
        out_specs=[vmem, vmem],
        scratch_shapes=[
            pltpu.VMEM(row_shape, F32),
            pltpu.VMEM((chunk * part, order), BF16),
            pltpu.VMEM((chunk * part, order), BF16),
            pltpu.VMEM((chunk * part, order), F32),
            pltpu.SemaphoreType.DMA,
        ],
        compiler_params=pltpu.CompilerParams(vmem_limit_bytes=20 * 1024 * 1024),
        name="solve",
    )(blk, in_vmem(high), in_vmem(low), *pieces)


def pack_kernel(count, *refs):
    out_ref = refs[-1]
    for j in range(count):
        out_ref[j] = refs[j][0]


def pack(parts, after):
    vmem = pl.BlockSpec(memory_space=pltpu.VMEM)
    return pl.pallas_call(
        functools.partial(pack_kernel, len(parts)),
        out_shape=pltpu.VMEM((len(parts),) + parts[0].shape[1:], parts[0].dtype),
        in_specs=[vmem] * (len(parts) + len(after)),
        out_specs=vmem,
        name="pack",
    )(*[in_vmem(value) for value in list(parts) + list(after)])


def update_kernel(
    core_ref, row_ids_ref, col_ids_ref, block_rows_ref,
    mine_ref, theirs_ref, blocks_ref, copied_ref, out_ref,
    held, found, in_sems, out_sems,
):
    del copied_ref
    core = core_ref[0]
    slots, stored = block_rows_ref.shape
    pieces = row_ids_ref.shape[0]
    half_rows = blocks_ref.shape[2]

    def fetch(n, slot, r):
        return pltpu.make_async_copy(blocks_ref.at[slot, r], held.at[n], in_sems.at[n])

    def place_of(wanted):
        def look(p, at):
            return jnp.where(row_ids_ref[p] == wanted, p, at)

        return jnp.where(wanted >= 0, lax.fori_loop(0, pieces, look, jnp.int32(-1)), -1)

    def scan_slot(slot, n):
        a = place_of(col_ids_ref[slot])

        def scan_stored(r, n):
            b = jnp.where(a >= 0, place_of(block_rows_ref[slot, r]), -1)

            @pl.when(b >= 0)
            def _():
                found[0, n] = slot
                found[1, n] = r
                found[2, n] = a
                found[3, n] = b
                fetch(n, slot, r).start()

            return jnp.where(b >= 0, n + 1, n)

        return lax.fori_loop(0, jnp.where(a >= 0, stored, 0), scan_stored, n)

    total = lax.fori_loop(0, slots, scan_slot, jnp.int32(0))

    def store(n):
        return pltpu.make_async_copy(
            held.at[n], out_ref.at[found[0, n], found[1, n]], out_sems.at[n]
        )

    def apply(n, carry):
        a_rows = pl.ds(pl.multiple_of(found[2, n] * half_rows, half_rows), half_rows)
        b_rows = pl.ds(pl.multiple_of(found[3, n] * half_rows, half_rows), half_rows)
        row = mine_ref[b_rows, :]
        column = jnp.concatenate([mine_ref[a_rows, :], theirs_ref[a_rows, :]], axis=0)
        change = lax.dot_general(row, column, NT, preferred_element_type=F32)
        fetch(n, found[0, n], found[1, n]).wait()
        for which in range(2):
            at = (core if which == 0 else 1 - core) * half_rows
            lanes = pl.ds(pl.multiple_of(at, half_rows), half_rows)
            part = change[:, which * half_rows : (which + 1) * half_rows]
            held[n, :, lanes] = held[n, :, lanes] - part
        store(n).start()
        return carry

    lax.fori_loop(0, total, apply, 0)

    def finish(n, carry):
        store(n).wait()
        return carry

    lax.fori_loop(0, total, finish, 0)


def update(core, row_ids, col_ids, block_rows, mine, theirs, blocks, copied):
    slots, stored = block_rows.shape
    smem = pl.BlockSpec(memory_space=pltpu.SMEM)
    vmem = pl.BlockSpec(memory_space=pltpu.VMEM)
    hbm = pl.BlockSpec(memory_space=pltpu.HBM)
    return pl.pallas_call(
        update_kernel,
        out_shape=jax.ShapeDtypeStruct(blocks.shape, F32),
        in_specs=[smem, smem, smem, smem, vmem, vmem, hbm, hbm],
        out_specs=hbm,
        input_output_aliases={7: 0},
        scratch_shapes=[
            pltpu.VMEM((slots * stored,) + blocks.shape[2:], F32),
            pltpu.SMEM((4, slots * stored), jnp.int32),
            pltpu.SemaphoreType.DMA((slots * stored,)),
            pltpu.SemaphoreType.DMA((slots * stored,)),
        ],
        compiler_params=pltpu.CompilerParams(
            vmem_limit_bytes=8 * 1024 * 1024 + 4 * blocks.size + 4 * mine.size
        ),
        name="update",
    )(
        core, row_ids, col_ids, block_rows, in_vmem(mine), in_vmem(theirs),
        in_hbm(blocks), in_hbm(copied),
    )


def local(diag_block, panel_rows, row_ids, col_ids, block_rows, blocks):
    blk = lax.axis_index("blk").astype(jnp.int32)[None]
    core = lax.axis_index("row").astype(jnp.int32)[None]
    swap = [(0, 1), (1, 0)]
    n_blk = lax.axis_size("blk")
    count = diag_block.shape[1] // BLOCK
    other = lax.ppermute(diag_block, "row", swap)

    def from_partner(value, k):
        return lax.ppermute(value, "blk", [(i, i ^ k) for i in range(n_blk)])

    in_stages = n_blk in (8, 16)
    near = n_blk // 4
    if in_stages:
        arrived = [from_partner(panel_rows, j * near) for j in range(1, 4)]
    else:
        pieces = [lax.all_gather(panel_rows, "blk", axis=0, tiled=True)]
    state = factor(0, 2, core, diag_block, other, [], blocks)
    if in_stages:
        group = pack([panel_rows] + arrived, state)
        pieces = [group] + [from_partner(group, k) for k in range(1, near)]
    high, low, *_, copied = factor(2, count, core, diag_block, other, state, blocks)
    own, mine = solve(blk, high, low, pieces)
    theirs = lax.ppermute(mine, "row", swap)
    new_blocks = update(core, row_ids, col_ids, block_rows, mine, theirs, blocks, copied)
    return own[None], new_blocks


def solution(mesh):
    return jax.shard_map(
        local,
        mesh=mesh,
        in_specs=(
            P("row", None),
            P("row", "blk", None),
            P(),
            P("blk"),
            P("blk", None),
            P("blk", None, "row", None),
        ),
        out_specs=(P("row", "blk", None), P("blk", None, "row", None)),
        check_vma=False,
    )
```

```python
import functools

import jax
import jax.numpy as jnp
from jax import lax
from jax.experimental import pallas as pl
from jax.experimental.pallas import tpu as pltpu
from jax.sharding import PartitionSpec as P

BLOCK = 128
PANEL = 32
STEP = 8
F32 = jnp.float32
BF16 = jnp.bfloat16
TN = (((0,), (0,)), ((), ()))
NT = (((1,), (1,)), ((), ()))


def halves(value):
    high = value.astype(BF16)
    return high, (value - high.astype(F32)).astype(BF16)


def in_hbm(value):
    return pltpu.with_memory_space_constraint(value, pltpu.HBM)


def in_vmem(value):
    return pltpu.with_memory_space_constraint(value, pltpu.VMEM)


def repeated(ref, *index):
    *lead, row, lanes = index
    return ref[(*lead, pl.ds(row, STEP, stride=0), lanes)]


def eliminate(columns, tiles, scratch_diag, scratch_below, scratch_rows):
    groups = PANEL // STEP
    sublane = lax.broadcasted_iota(jnp.int32, (STEP, BLOCK), 0)
    for s in range(groups):
        first = s * STEP
        for c in range(STEP):
            scratch_diag[s, c] = columns[first + c][s]
        square = [
            [
                repeated(scratch_diag, s, c, k, slice(None)) if k <= c else None
                for c in range(STEP)
            ]
            for k in range(STEP)
        ]
        inverse = []
        for k in range(STEP):
            inverse.append(pl.reciprocal(square[k][k], approx=True))
            for c in range(k + 1, STEP):
                ratio = square[k][c] * inverse[k]
                for d in range(c, STEP):
                    square[c][d] = square[c][d] - ratio * square[k][d]
        ratios = []
        for k in range(STEP):
            now = [None] * groups
            for g in range(s, groups):
                now[g] = columns[first + k][g] * inverse[k]
            now[s] = jnp.where(sublane > k, now[s], 0.0)
            for c in range(k + 1, STEP):
                for g in range(s, groups):
                    columns[first + c][g] = columns[first + c][g] - now[g] * square[k][c]
            ratios.append(now)
            for g in range(s + 1, groups):
                scratch_below[s, k, (g - 1) * STEP : g * STEP, :] = columns[first + k][g]
        for c in range(first + STEP, PANEL):
            for k in range(STEP):
                entry = repeated(scratch_below, s, k, c - STEP, slice(None))
                for g in range(c // STEP, groups):
                    columns[c][g] = columns[c][g] - ratios[k][g] * entry
        pivots = square[0][0]
        for k in range(1, STEP):
            pivots = jnp.where(sublane == k, square[k][k], pivots)
        for t in range(len(tiles[s])):
            for k in range(STEP):
                scratch_rows[s, t, k % 2] = tiles[s][t]
                row = repeated(scratch_rows, s, t, k % 2, k, slice(None))
                for g in range(s, groups):
                    if g == s and k == STEP - 1:
                        continue
                    tiles[g][t] = tiles[g][t] - ratios[k][g] * row
        scale = lax.rsqrt(pivots)
        tiles[s] = [tile * scale for tile in tiles[s]]


def times_transposed(high, low, right_high, right_low):
    width = right_high.shape[0]
    both = lax.dot_general(
        high, jnp.concatenate([right_high, right_low], axis=0), NT, preferred_element_type=F32
    )
    return (
        both[:, :width]
        + both[:, width:]
        + lax.dot_general(low, right_high, NT, preferred_element_type=F32)
    )


def invert_diagonal(diag, unit, scratch_diag, scratch_below, scratch_rows):
    groups = range(PANEL // STEP)
    for q in range(BLOCK // PANEL):
        top = q * PANEL
        rest = top + PANEL
        tile = diag[top:rest, :]
        columns = [
            [
                jnp.broadcast_to(
                    tile[g * STEP : (g + 1) * STEP, top + c : top + c + 1], (STEP, BLOCK)
                )
                if g >= c // STEP
                else None
                for g in groups
            ]
            for c in range(PANEL)
        ]
        cuts = [slice(top + g * STEP, top + (g + 1) * STEP) for g in groups]
        tiles = [[diag[cut, :], unit[cut, :]] for cut in cuts]
        eliminate(columns, tiles, scratch_diag, scratch_below, scratch_rows)
        for g, cut in enumerate(cuts):
            diag[cut, :] = tiles[g][0]
            unit[cut, :] = tiles[g][1]
        if rest < BLOCK:
            left_high, left_low = halves(diag[top:rest, :])
            left = jnp.concatenate([left_high, left_low, left_high], axis=0)
            for target in (diag, unit):
                right_high, right_low = halves(target[top:rest, :])
                right = jnp.concatenate([right_high, right_high, right_low], axis=0)
                change = lax.dot_general(left, right, TN, preferred_element_type=F32)
                target[rest:, :] = target[rest:, :] - change[rest:, :]


def factor_kernel(first, last, core_ref, own_ref, other_ref, *refs):
    refs = list(refs)
    state_refs = [refs.pop(0) for _ in range(6)] if first else []
    blocks_ref = refs.pop(0) if first else None
    high_ref, low_ref, base, prev_high, prev_low, diag = refs[:6]
    refs = refs[6:]
    copied_ref = refs.pop(0) if first else None
    matrix, unit, next_diag, column_high, column_low = refs[:5]
    scratch_diag, scratch_below, scratch_rows, tile_sems = refs[5:9]
    order = own_ref.shape[1]
    half = order // 2
    count = order // BLOCK
    width = high_ref.shape[1]
    core = core_ref[0]

    def fetch_tile(t, which):
        lanes = pl.ds(pl.multiple_of(t * BLOCK, BLOCK), BLOCK)
        source = (own_ref, other_ref)[which]
        at = pl.multiple_of((core if which == 0 else 1 - core) * half, half)
        return pltpu.make_async_copy(
            source.at[:, lanes], matrix.at[t, pl.ds(at, half), :], tile_sems.at[t, which]
        )

    for t in range(first, min(last + 1, count)):
        for which in range(2):
            fetch_tile(t, which).start()
    if first:
        held, block_sems = refs[9:]
        fetch_blocks = pltpu.make_async_copy(blocks_ref, held, block_sems.at[0])
        store_blocks = pltpu.make_async_copy(held, copied_ref, block_sems.at[1])
        fetch_blocks.start()
    identity = (
        lax.broadcasted_iota(jnp.int32, (BLOCK, BLOCK), 0)
        == lax.broadcasted_iota(jnp.int32, (BLOCK, BLOCK), 1)
    ).astype(F32)
    row_at = lax.broadcasted_iota(jnp.int32, (order, BLOCK), 0)
    lane_at = lax.broadcasted_iota(jnp.int32, (order, BLOCK), 1)

    if first:
        done = (first - 1) * BLOCK
        high_ref[:, done:] = jnp.zeros((order, width - done), BF16)
        low_ref[:, done:] = jnp.zeros((order, width - done), BF16)
        high_ref[:, :done] = state_refs[0][...]
        low_ref[:, :done] = state_refs[1][...]
        for into, out_of in zip((base, prev_high, prev_low, diag), state_refs[2:]):
            into[...] = out_of[...]
        for which in range(2):
            fetch_tile(first, which).wait()
    else:
        for ref in (high_ref, low_ref, base, prev_high, prev_low):
            ref[...] = jnp.zeros(ref.shape, ref.dtype)
        for which in range(2):
            fetch_tile(0, which).wait()
        diag[...] = matrix[0, :BLOCK, :]

    def previous_column():
        return halves(times_transposed(*halves(base[...]), prev_high[...], prev_low[...]))

    def block_step(b, carry):
        here = pl.multiple_of(b * BLOCK, BLOCK)
        before = pl.multiple_of(jnp.maximum(b - 1, 0) * BLOCK, BLOCK)
        following = jnp.minimum(b + 1, count - 1)
        next_at = pl.multiple_of(following * BLOCK, BLOCK)

        @pl.when(b + 1 < count)
        def _():
            for which in range(2):
                fetch_tile(b + 1, which).wait()

        if first:

            @pl.when(b == first + 1)
            def _():
                fetch_blocks.wait()
                store_blocks.start()

        column_high[...], column_low[...] = previous_column()

        def rows_of(at):
            rows = pl.ds(at, BLOCK)
            return (high_ref[rows, :], low_ref[rows, :]), (column_high[rows, :], column_low[rows, :])

        history, column = rows_of(here)
        earlier = times_transposed(high_ref[...], low_ref[...], *history)
        earlier += times_transposed(column_high[...], column_low[...], *column)
        fresh = jnp.where(row_at >= here, matrix[b], 0.0) - earlier
        in_diag = (row_at >= here) & (row_at < here + BLOCK)
        base[...] = jnp.where(in_diag, (row_at - here == lane_at).astype(F32), fresh)
        history, column = rows_of(next_at)
        next_diag[...] = (
            matrix[following, pl.ds(next_at, BLOCK), :]
            - times_transposed(*history, *history)
            - times_transposed(*column, *column)
        )

        unit[...] = identity
        invert_diagonal(diag, unit, scratch_diag, scratch_below, scratch_rows)

        high, low = halves(unit[...])
        prev_high[...] = high
        prev_low[...] = low
        below = times_transposed(*halves(base[pl.ds(next_at, BLOCK), :]), high, low)
        high, low = halves(below)
        diag[...] = next_diag[...] - times_transposed(high, low, high, low)

        for ref, column in ((high_ref, column_high), (low_ref, column_low)):
            ref[:, pl.ds(before, BLOCK)] = column[...]
            ref[pl.ds(here, BLOCK), :] = jnp.zeros((BLOCK, width), BF16)
        return carry

    lax.fori_loop(first, last, block_step, 0)
    if last == count:
        high_ref[:, order - BLOCK :], low_ref[:, order - BLOCK :] = previous_column()
    if first:
        store_blocks.wait()


def factor(first, last, core, own, other, state, blocks):
    order = own.shape[1]
    count = order // BLOCK
    vmem = pl.BlockSpec(memory_space=pltpu.VMEM)
    hbm = pl.BlockSpec(memory_space=pltpu.HBM)
    columns = (last if last == count else last - 1) * BLOCK
    out_shape = [
        pltpu.VMEM((order, columns), BF16),
        pltpu.VMEM((order, columns), BF16),
        pltpu.VMEM((order, BLOCK), F32),
        pltpu.VMEM((BLOCK, BLOCK), BF16),
        pltpu.VMEM((BLOCK, BLOCK), BF16),
        pltpu.VMEM((BLOCK, BLOCK), F32),
    ]
    scratch = [
        pltpu.VMEM((count, order, BLOCK), F32),
        pltpu.VMEM((BLOCK, BLOCK), F32),
        pltpu.VMEM((BLOCK, BLOCK), F32),
        pltpu.VMEM((order, BLOCK), BF16),
        pltpu.VMEM((order, BLOCK), BF16),
        pltpu.VMEM((PANEL // STEP, STEP, STEP, BLOCK), F32),
        pltpu.VMEM((PANEL // STEP, STEP, PANEL - STEP, BLOCK), F32),
        pltpu.VMEM((PANEL // STEP, 2, 2, STEP, BLOCK), F32),
        pltpu.SemaphoreType.DMA((count, 2)),
    ]
    in_specs = [pl.BlockSpec(memory_space=pltpu.SMEM), hbm, vmem]
    out_specs = [vmem] * len(out_shape)
    operands = [core, in_hbm(own), in_vmem(other)]
    limit = 12 * 1024 * 1024
    if first:
        in_specs += [vmem] * len(state) + [hbm]
        operands += [in_vmem(part) for part in state] + [in_hbm(blocks)]
        out_specs.append(hbm)
        out_shape.append(jax.ShapeDtypeStruct(blocks.shape, F32))
        scratch += [pltpu.VMEM(blocks.shape, F32), pltpu.SemaphoreType.DMA((2,))]
        limit += 4 * blocks.size + 4 * 1024 * 1024
    share = last - first
    return pl.pallas_call(
        functools.partial(factor_kernel, first, last),
        out_shape=out_shape,
        in_specs=in_specs,
        out_specs=out_specs,
        scratch_shapes=scratch,
        compiler_params=pltpu.CompilerParams(vmem_limit_bytes=limit),
        cost_estimate=pl.CostEstimate(
            flops=share * order**3, bytes_accessed=share * 20_000_000, transcendentals=0
        ),
        name="factor",
    )(*operands)


def solve_kernel(blk_ref, high_ref, low_ref, *refs):
    *piece_refs, own_ref, rounded_ref, rows, rows_high, rows_low, solved, row_sem = refs
    blk = blk_ref[0]
    held, part, order = piece_refs[0].shape
    n_blk = len(piece_refs) * held
    chunk_rows = rows_high.shape[0]
    chunk = chunk_rows // part
    chunks = n_blk // chunk

    def load(at):
        return pltpu.make_async_copy(piece_refs[0].at[pl.ds(at * chunk, chunk)], rows, row_sem)

    def solve_chunk(at, carry):
        if len(piece_refs) == 1:
            load(at).start()
            load(at).wait()
            rows_high[...], rows_low[...] = halves(rows[...].reshape(chunk_rows, order))
        else:
            for k, piece in enumerate(piece_refs):
                for j in range(held):
                    place = blk ^ (k + j * len(piece_refs))
                    here = pl.ds(pl.multiple_of(place * part, part), part)
                    rows_high[here, :], rows_low[here, :] = halves(piece[j])

        width = 256
        for n in range(order // width):
            cut = slice(n * width, (n + 1) * width)
            deep = (n + 1) * width
            x = jnp.dot(
                rows_high[:, :deep], high_ref[:deep, cut], preferred_element_type=F32
            )
            x += jnp.dot(rows_low[:, :deep], high_ref[:deep, cut], preferred_element_type=F32)
            x += jnp.dot(rows_high[:, :deep], low_ref[:deep, cut], preferred_element_type=F32)
            solved[:, cut] = x
            rounded_ref[pl.ds(pl.multiple_of(at * chunk_rows, chunk_rows), chunk_rows), cut] = (
                x.astype(BF16)
            )

        @pl.when(blk // chunk == at)
        def _():
            own_ref[...] = solved[pl.ds(pl.multiple_of(blk % chunk * part, part), part), :]

        return carry

    lax.fori_loop(0, chunks, solve_chunk, 0)


def solve(blk, high, low, pieces):
    order = high.shape[0]
    held, part, _ = pieces[0].shape
    n_blk = len(pieces) * held
    chunk = n_blk if len(pieces) > 1 else min(n_blk, max(1, 512 // part))
    smem = pl.BlockSpec(memory_space=pltpu.SMEM)
    vmem = pl.BlockSpec(memory_space=pltpu.VMEM)
    if len(pieces) > 1:
        piece_spec, row_shape = vmem, (1, 8, BLOCK)
        pieces = [in_vmem(piece) for piece in pieces]
    else:
        piece_spec, row_shape = pl.BlockSpec(memory_space=pltpu.HBM), (chunk, part, order)
        pieces = [in_hbm(piece) for piece in pieces]
    return pl.pallas_call(
        solve_kernel,
        out_shape=[
            jax.ShapeDtypeStruct((part, order), F32),
            pltpu.VMEM((n_blk * part, order), BF16),
        ],
        in_specs=[smem, vmem, vmem] + [piece_spec] * len(pieces),
        out_specs=[vmem, vmem],
        scratch_shapes=[
            pltpu.VMEM(row_shape, F32),
            pltpu.VMEM((chunk * part, order), BF16),
            pltpu.VMEM((chunk * part, order), BF16),
            pltpu.VMEM((chunk * part, order), F32),
            pltpu.SemaphoreType.DMA,
        ],
        compiler_params=pltpu.CompilerParams(vmem_limit_bytes=20 * 1024 * 1024),
        name="solve",
    )(blk, in_vmem(high), in_vmem(low), *pieces)


def pack_kernel(count, *refs):
    out_ref = refs[-1]
    for j in range(count):
        out_ref[j] = refs[j][0]


def pack(parts, after):
    vmem = pl.BlockSpec(memory_space=pltpu.VMEM)
    return pl.pallas_call(
        functools.partial(pack_kernel, len(parts)),
        out_shape=pltpu.VMEM((len(parts),) + parts[0].shape[1:], parts[0].dtype),
        in_specs=[vmem] * (len(parts) + len(after)),
        out_specs=vmem,
        name="pack",
    )(*[in_vmem(value) for value in list(parts) + list(after)])


def update_kernel(
    core_ref, row_ids_ref, col_ids_ref, block_rows_ref,
    mine_ref, theirs_ref, blocks_ref, copied_ref, out_ref,
    held, found, in_sems, out_sems,
):
    del copied_ref
    core = core_ref[0]
    slots, stored = block_rows_ref.shape
    pieces = row_ids_ref.shape[0]
    half_rows = blocks_ref.shape[2]

    def fetch(n, slot, r):
        return pltpu.make_async_copy(blocks_ref.at[slot, r], held.at[n], in_sems.at[n])

    def place_of(wanted):
        def look(p, at):
            return jnp.where(row_ids_ref[p] == wanted, p, at)

        return jnp.where(wanted >= 0, lax.fori_loop(0, pieces, look, jnp.int32(-1)), -1)

    def scan_slot(slot, n):
        a = place_of(col_ids_ref[slot])

        def scan_stored(r, n):
            b = jnp.where(a >= 0, place_of(block_rows_ref[slot, r]), -1)

            @pl.when(b >= 0)
            def _():
                found[0, n] = slot
                found[1, n] = r
                found[2, n] = a
                found[3, n] = b
                fetch(n, slot, r).start()

            return jnp.where(b >= 0, n + 1, n)

        return lax.fori_loop(0, jnp.where(a >= 0, stored, 0), scan_stored, n)

    total = lax.fori_loop(0, slots, scan_slot, jnp.int32(0))

    def store(n):
        return pltpu.make_async_copy(
            held.at[n], out_ref.at[found[0, n], found[1, n]], out_sems.at[n]
        )

    def apply(n, carry):
        a_rows = pl.ds(pl.multiple_of(found[2, n] * half_rows, half_rows), half_rows)
        b_rows = pl.ds(pl.multiple_of(found[3, n] * half_rows, half_rows), half_rows)
        row = mine_ref[b_rows, :]
        column = jnp.concatenate([mine_ref[a_rows, :], theirs_ref[a_rows, :]], axis=0)
        change = lax.dot_general(row, column, NT, preferred_element_type=F32)
        fetch(n, found[0, n], found[1, n]).wait()
        for which in range(2):
            at = (core if which == 0 else 1 - core) * half_rows
            lanes = pl.ds(pl.multiple_of(at, half_rows), half_rows)
            part = change[:, which * half_rows : (which + 1) * half_rows]
            held[n, :, lanes] = held[n, :, lanes] - part
        store(n).start()
        return carry

    lax.fori_loop(0, total, apply, 0)

    def finish(n, carry):
        store(n).wait()
        return carry

    lax.fori_loop(0, total, finish, 0)


def update(core, row_ids, col_ids, block_rows, mine, theirs, blocks, copied):
    slots, stored = block_rows.shape
    smem = pl.BlockSpec(memory_space=pltpu.SMEM)
    vmem = pl.BlockSpec(memory_space=pltpu.VMEM)
    hbm = pl.BlockSpec(memory_space=pltpu.HBM)
    return pl.pallas_call(
        update_kernel,
        out_shape=jax.ShapeDtypeStruct(blocks.shape, F32),
        in_specs=[smem, smem, smem, smem, vmem, vmem, hbm, hbm],
        out_specs=hbm,
        input_output_aliases={7: 0},
        scratch_shapes=[
            pltpu.VMEM((slots * stored,) + blocks.shape[2:], F32),
            pltpu.SMEM((4, slots * stored), jnp.int32),
            pltpu.SemaphoreType.DMA((slots * stored,)),
            pltpu.SemaphoreType.DMA((slots * stored,)),
        ],
        compiler_params=pltpu.CompilerParams(
            vmem_limit_bytes=8 * 1024 * 1024 + 4 * blocks.size + 4 * mine.size
        ),
        name="update",
    )(
        core, row_ids, col_ids, block_rows, in_vmem(mine), in_vmem(theirs),
        in_hbm(blocks), in_hbm(copied),
    )


def local(diag_block, panel_rows, row_ids, col_ids, block_rows, blocks):
    blk = lax.axis_index("blk").astype(jnp.int32)[None]
    core = lax.axis_index("row").astype(jnp.int32)[None]
    swap = [(0, 1), (1, 0)]
    n_blk = lax.axis_size("blk")
    count = diag_block.shape[1] // BLOCK
    other = lax.ppermute(diag_block, "row", swap)

    def from_partner(value, k):
        return lax.ppermute(value, "blk", [(i, i ^ k) for i in range(n_blk)])

    in_stages = n_blk in (8, 16)
    near = n_blk // 4
    if in_stages:
        arrived = [from_partner(panel_rows, j * near) for j in range(1, 4)]
    else:
        pieces = [lax.all_gather(panel_rows, "blk", axis=0, tiled=True)]
    state = factor(0, 2, core, diag_block, other, [], blocks)
    if in_stages:
        group = pack([panel_rows] + arrived, state)
        pieces = [group] + [from_partner(group, k) for k in range(1, near)]
    high, low, *_, copied = factor(2, count, core, diag_block, other, state, blocks)
    own, mine = solve(blk, high, low, pieces)
    theirs = lax.ppermute(mine, "row", swap)
    new_blocks = update(core, row_ids, col_ids, block_rows, mine, theirs, blocks, copied)
    return own[None], new_blocks


def solution(mesh):
    return jax.shard_map(
        local,
        mesh=mesh,
        in_specs=(
            P("row", None),
            P("row", "blk", None),
            P(),
            P("blk"),
            P("blk", None),
            P("blk", None, "row", None),
        ),
        out_specs=(P("row", "blk", None), P("blk", None, "row", None)),
        check_vma=False,
    )
```

```python
import functools

import jax
import jax.numpy as jnp
from jax import lax
from jax.experimental import pallas as pl
from jax.experimental.pallas import tpu as pltpu
from jax.sharding import PartitionSpec as P

BLOCK = 128
PANEL = 32
STEP = 8
F32 = jnp.float32
BF16 = jnp.bfloat16
TN = (((0,), (0,)), ((), ()))
NT = (((1,), (1,)), ((), ()))


def halves(value):
    high = value.astype(BF16)
    return high, (value - high.astype(F32)).astype(BF16)


def in_hbm(value):
    return pltpu.with_memory_space_constraint(value, pltpu.HBM)


def in_vmem(value):
    return pltpu.with_memory_space_constraint(value, pltpu.VMEM)


def repeated(ref, *index):
    *lead, row, lanes = index
    return ref[(*lead, pl.ds(row, STEP, stride=0), lanes)]


def eliminate(columns, tiles, scratch_diag, scratch_below, scratch_rows):
    groups = PANEL // STEP
    sublane = lax.broadcasted_iota(jnp.int32, (STEP, BLOCK), 0)
    for s in range(groups):
        first = s * STEP
        for c in range(STEP):
            scratch_diag[s, c] = columns[first + c][s]
        square = [
            [
                repeated(scratch_diag, s, c, k, slice(None)) if k <= c else None
                for c in range(STEP)
            ]
            for k in range(STEP)
        ]
        inverse = []
        for k in range(STEP):
            inverse.append(pl.reciprocal(square[k][k], approx=True))
            for c in range(k + 1, STEP):
                ratio = square[k][c] * inverse[k]
                for d in range(c, STEP):
                    square[c][d] = square[c][d] - ratio * square[k][d]
        ratios = []
        for k in range(STEP):
            now = [None] * groups
            for g in range(s, groups):
                now[g] = columns[first + k][g] * inverse[k]
            now[s] = jnp.where(sublane > k, now[s], 0.0)
            for c in range(k + 1, STEP):
                for g in range(s, groups):
                    columns[first + c][g] = columns[first + c][g] - now[g] * square[k][c]
            ratios.append(now)
            for g in range(s + 1, groups):
                scratch_below[s, k, (g - 1) * STEP : g * STEP, :] = columns[first + k][g]
        for c in range(first + STEP, PANEL):
            for k in range(STEP):
                entry = repeated(scratch_below, s, k, c - STEP, slice(None))
                for g in range(c // STEP, groups):
                    columns[c][g] = columns[c][g] - ratios[k][g] * entry
        pivots = square[0][0]
        for k in range(1, STEP):
            pivots = jnp.where(sublane == k, square[k][k], pivots)
        for t in range(len(tiles[s])):
            for k in range(STEP):
                scratch_rows[s, t, k % 2] = tiles[s][t]
                row = repeated(scratch_rows, s, t, k % 2, k, slice(None))
                for g in range(s, groups):
                    if g == s and k == STEP - 1:
                        continue
                    tiles[g][t] = tiles[g][t] - ratios[k][g] * row
        scale = lax.rsqrt(pivots)
        tiles[s] = [tile * scale for tile in tiles[s]]


def times_transposed(high, low, right_high, right_low):
    width = right_high.shape[0]
    if high.shape[1] <= BLOCK:
        return lax.dot_general(
            jnp.concatenate([high, low, high], axis=1),
            jnp.concatenate([right_high, right_high, right_low], axis=1),
            NT,
            preferred_element_type=F32,
        )
    both = lax.dot_general(
        high, jnp.concatenate([right_high, right_low], axis=0), NT, preferred_element_type=F32
    )
    return (
        both[:, :width]
        + both[:, width:]
        + lax.dot_general(low, right_high, NT, preferred_element_type=F32)
    )


def invert_diagonal(diag, unit, scratch_diag, scratch_below, scratch_rows):
    groups = range(PANEL // STEP)
    for q in range(BLOCK // PANEL):
        top = q * PANEL
        rest = top + PANEL
        tile = diag[top:rest, :]
        columns = [
            [
                jnp.broadcast_to(
                    tile[g * STEP : (g + 1) * STEP, top + c : top + c + 1], (STEP, BLOCK)
                )
                if g >= c // STEP
                else None
                for g in groups
            ]
            for c in range(PANEL)
        ]
        cuts = [slice(top + g * STEP, top + (g + 1) * STEP) for g in groups]
        tiles = [[diag[cut, :], unit[cut, :]] for cut in cuts]
        eliminate(columns, tiles, scratch_diag, scratch_below, scratch_rows)
        for g, cut in enumerate(cuts):
            diag[cut, :] = tiles[g][0]
            unit[cut, :] = tiles[g][1]
        if rest < BLOCK:
            left_high, left_low = halves(diag[top:rest, :])
            left = jnp.concatenate([left_high, left_low, left_high], axis=0)
            for target in (diag, unit):
                right_high, right_low = halves(target[top:rest, :])
                right = jnp.concatenate([right_high, right_high, right_low], axis=0)
                change = lax.dot_general(left, right, TN, preferred_element_type=F32)
                target[rest:, :] = target[rest:, :] - change[rest:, :]


def factor_kernel(first, last, core_ref, own_ref, other_ref, *refs):
    refs = list(refs)
    state_refs = [refs.pop(0) for _ in range(4)] if first else []
    blocks_ref = refs.pop(0) if first else None
    high_ref, low_ref, base, diag = refs[:4]
    refs = refs[4:]
    copied_ref = refs.pop(0) if first else None
    matrix, unit, scratch_diag, scratch_below, scratch_rows, tile_sems = refs[:6]
    order = own_ref.shape[1]
    half = order // 2
    count = order // BLOCK
    core = core_ref[0]

    def fetch_tile(t, which):
        source = (own_ref, other_ref)[which]
        at = pl.multiple_of((core if which == 0 else 1 - core) * half, half)
        return pltpu.make_async_copy(
            source.at[:, pl.ds(t * BLOCK, BLOCK)],
            matrix.at[t, pl.ds(at, half), :],
            tile_sems.at[t, which],
        )

    for t in range(first + 1 if first else 0, min(last + 1, count)):
        for which in range(2):
            fetch_tile(t, which).start()
    if first:
        held, block_sems = refs[6:]
        fetch_blocks = pltpu.make_async_copy(blocks_ref, held, block_sems.at[0])
        store_blocks = pltpu.make_async_copy(held, copied_ref, block_sems.at[1])
        fetch_blocks.start()
    identity = (
        lax.broadcasted_iota(jnp.int32, (BLOCK, BLOCK), 0)
        == lax.broadcasted_iota(jnp.int32, (BLOCK, BLOCK), 1)
    ).astype(F32)

    if first:
        done = first * BLOCK
        high_ref[:, :done] = state_refs[0][...]
        low_ref[:, :done] = state_refs[1][...]
        base[...] = state_refs[2][...]
        diag[...] = state_refs[3][...]
    else:
        for which in range(2):
            fetch_tile(0, which).wait()
        base[:BLOCK] = identity
        base[BLOCK:] = matrix[0, BLOCK:, :]
        diag[...] = matrix[0, :BLOCK, :]

    for b in range(first, last):
        unit[...] = identity
        invert_diagonal(diag, unit, scratch_diag, scratch_below, scratch_rows)
        if b == first + 1 and first:
            fetch_blocks.wait()
            store_blocks.start()
        here = slice(b * BLOCK, (b + 1) * BLOCK)
        high, low = halves(times_transposed(*halves(base[...]), *halves(unit[...])))
        high_ref[:, here] = high
        low_ref[:, here] = low
        if b + 1 == count:
            break
        done = (b + 1) * BLOCK
        following = slice(done, done + BLOCK)
        change = times_transposed(
            high_ref[:, :done], low_ref[:, :done], high_ref[following, :done], low_ref[following, :done]
        )
        for which in range(2):
            fetch_tile(b + 1, which).wait()
        diag[...] = matrix[b + 1, following, :] - change[following]
        base[:done] = -change[:done]
        base[following] = identity
        if done + BLOCK < order:
            base[done + BLOCK :] = matrix[b + 1, done + BLOCK :, :] - change[done + BLOCK :]
        high_ref[following, :done] = jnp.zeros((BLOCK, done), BF16)
        low_ref[following, :done] = jnp.zeros((BLOCK, done), BF16)

    if first:
        store_blocks.wait()


def factor(first, last, core, own, other, state, blocks):
    order = own.shape[1]
    count = order // BLOCK
    vmem = pl.BlockSpec(memory_space=pltpu.VMEM)
    hbm = pl.BlockSpec(memory_space=pltpu.HBM)
    columns = last * BLOCK
    out_shape = [
        pltpu.VMEM((order, columns), BF16),
        pltpu.VMEM((order, columns), BF16),
        pltpu.VMEM((order, BLOCK), F32),
        pltpu.VMEM((BLOCK, BLOCK), F32),
    ]
    scratch = [
        pltpu.VMEM((count, order, BLOCK), F32),
        pltpu.VMEM((BLOCK, BLOCK), F32),
        pltpu.VMEM((PANEL // STEP, STEP, STEP, BLOCK), F32),
        pltpu.VMEM((PANEL // STEP, STEP, PANEL - STEP, BLOCK), F32),
        pltpu.VMEM((PANEL // STEP, 2, 2, STEP, BLOCK), F32),
        pltpu.SemaphoreType.DMA((count, 2)),
    ]
    in_specs = [pl.BlockSpec(memory_space=pltpu.SMEM), hbm, vmem]
    out_specs = [vmem] * len(out_shape)
    operands = [core, in_hbm(own), in_vmem(other)]
    limit = 12 * 1024 * 1024
    if first:
        in_specs += [vmem] * len(state) + [hbm]
        operands += [in_vmem(part) for part in state] + [in_hbm(blocks)]
        out_specs.append(hbm)
        out_shape.append(jax.ShapeDtypeStruct(blocks.shape, F32))
        scratch += [pltpu.VMEM(blocks.shape, F32), pltpu.SemaphoreType.DMA((2,))]
        limit += 4 * blocks.size + 4 * 1024 * 1024
    share = last - first
    return pl.pallas_call(
        functools.partial(factor_kernel, first, last),
        out_shape=out_shape,
        in_specs=in_specs,
        out_specs=out_specs,
        scratch_shapes=scratch,
        compiler_params=pltpu.CompilerParams(vmem_limit_bytes=limit),
        cost_estimate=pl.CostEstimate(
            flops=share * order**3, bytes_accessed=share * 20_000_000, transcendentals=0
        ),
        name="factor",
    )(*operands)


def solve_kernel(blk_ref, high_ref, low_ref, *refs):
    *piece_refs, own_ref, rounded_ref, rows, rows_high, rows_low, solved, row_sem = refs
    blk = blk_ref[0]
    held, part, order = piece_refs[0].shape
    n_blk = len(piece_refs) * held
    chunk_rows = rows_high.shape[0]
    chunk = chunk_rows // part
    chunks = n_blk // chunk

    def load(at):
        return pltpu.make_async_copy(piece_refs[0].at[pl.ds(at * chunk, chunk)], rows, row_sem)

    def solve_chunk(at, carry):
        if len(piece_refs) == 1:
            load(at).start()
            load(at).wait()
            rows_high[...], rows_low[...] = halves(rows[...].reshape(chunk_rows, order))
        else:
            for k, piece in enumerate(piece_refs):
                for j in range(held):
                    place = blk ^ (k + j * len(piece_refs))
                    here = pl.ds(pl.multiple_of(place * part, part), part)
                    rows_high[here, :], rows_low[here, :] = halves(piece[j])

        width = 256
        for n in range(order // width):
            cut = slice(n * width, (n + 1) * width)
            deep = (n + 1) * width
            x = jnp.dot(
                rows_high[:, :deep], high_ref[:deep, cut], preferred_element_type=F32
            )
            x += jnp.dot(rows_low[:, :deep], high_ref[:deep, cut], preferred_element_type=F32)
            x += jnp.dot(rows_high[:, :deep], low_ref[:deep, cut], preferred_element_type=F32)
            solved[:, cut] = x
            rounded_ref[pl.ds(pl.multiple_of(at * chunk_rows, chunk_rows), chunk_rows), cut] = (
                x.astype(BF16)
            )

        @pl.when(blk // chunk == at)
        def _():
            own_ref[...] = solved[pl.ds(pl.multiple_of(blk % chunk * part, part), part), :]

        return carry

    lax.fori_loop(0, chunks, solve_chunk, 0)


def solve(blk, high, low, pieces):
    order = high.shape[0]
    held, part, _ = pieces[0].shape
    n_blk = len(pieces) * held
    chunk = n_blk if len(pieces) > 1 else min(n_blk, max(1, 512 // part))
    smem = pl.BlockSpec(memory_space=pltpu.SMEM)
    vmem = pl.BlockSpec(memory_space=pltpu.VMEM)
    if len(pieces) > 1:
        piece_spec, row_shape = vmem, (1, 8, BLOCK)
        pieces = [in_vmem(piece) for piece in pieces]
    else:
        piece_spec, row_shape = pl.BlockSpec(memory_space=pltpu.HBM), (chunk, part, order)
        pieces = [in_hbm(piece) for piece in pieces]
    return pl.pallas_call(
        solve_kernel,
        out_shape=[
            jax.ShapeDtypeStruct((part, order), F32),
            pltpu.VMEM((n_blk * part, order), BF16),
        ],
        in_specs=[smem, vmem, vmem] + [piece_spec] * len(pieces),
        out_specs=[vmem, vmem],
        scratch_shapes=[
            pltpu.VMEM(row_shape, F32),
            pltpu.VMEM((chunk * part, order), BF16),
            pltpu.VMEM((chunk * part, order), BF16),
            pltpu.VMEM((chunk * part, order), F32),
            pltpu.SemaphoreType.DMA,
        ],
        compiler_params=pltpu.CompilerParams(vmem_limit_bytes=20 * 1024 * 1024),
        name="solve",
    )(blk, in_vmem(high), in_vmem(low), *pieces)


def pack_kernel(count, *refs):
    out_ref = refs[-1]
    for j in range(count):
        out_ref[j] = refs[j][0]


def pack(parts, after):
    vmem = pl.BlockSpec(memory_space=pltpu.VMEM)
    return pl.pallas_call(
        functools.partial(pack_kernel, len(parts)),
        out_shape=pltpu.VMEM((len(parts),) + parts[0].shape[1:], parts[0].dtype),
        in_specs=[vmem] * (len(parts) + len(after)),
        out_specs=vmem,
        name="pack",
    )(*[in_vmem(value) for value in list(parts) + list(after)])


def update_kernel(
    core_ref, row_ids_ref, col_ids_ref, block_rows_ref,
    mine_ref, theirs_ref, blocks_ref, copied_ref, out_ref,
    held, found, in_sems, out_sems,
):
    del copied_ref
    core = core_ref[0]
    slots, stored = block_rows_ref.shape
    pieces = row_ids_ref.shape[0]
    half_rows = blocks_ref.shape[2]

    def fetch(n, slot, r):
        return pltpu.make_async_copy(blocks_ref.at[slot, r], held.at[n], in_sems.at[n])

    def place_of(wanted):
        def look(p, at):
            return jnp.where(row_ids_ref[p] == wanted, p, at)

        return jnp.where(wanted >= 0, lax.fori_loop(0, pieces, look, jnp.int32(-1)), -1)

    def scan_slot(slot, n):
        a = place_of(col_ids_ref[slot])

        def scan_stored(r, n):
            b = jnp.where(a >= 0, place_of(block_rows_ref[slot, r]), -1)

            @pl.when(b >= 0)
            def _():
                found[0, n] = slot
                found[1, n] = r
                found[2, n] = a
                found[3, n] = b
                fetch(n, slot, r).start()

            return jnp.where(b >= 0, n + 1, n)

        return lax.fori_loop(0, jnp.where(a >= 0, stored, 0), scan_stored, n)

    total = lax.fori_loop(0, slots, scan_slot, jnp.int32(0))

    def store(n):
        return pltpu.make_async_copy(
            held.at[n], out_ref.at[found[0, n], found[1, n]], out_sems.at[n]
        )

    def apply(n, carry):
        a_rows = pl.ds(pl.multiple_of(found[2, n] * half_rows, half_rows), half_rows)
        b_rows = pl.ds(pl.multiple_of(found[3, n] * half_rows, half_rows), half_rows)
        row = mine_ref[b_rows, :]
        column = jnp.concatenate([mine_ref[a_rows, :], theirs_ref[a_rows, :]], axis=0)
        change = lax.dot_general(row, column, NT, preferred_element_type=F32)
        fetch(n, found[0, n], found[1, n]).wait()
        for which in range(2):
            at = (core if which == 0 else 1 - core) * half_rows
            lanes = pl.ds(pl.multiple_of(at, half_rows), half_rows)
            part = change[:, which * half_rows : (which + 1) * half_rows]
            held[n, :, lanes] = held[n, :, lanes] - part
        store(n).start()
        return carry

    lax.fori_loop(0, total, apply, 0)

    def finish(n, carry):
        store(n).wait()
        return carry

    lax.fori_loop(0, total, finish, 0)


def update(core, row_ids, col_ids, block_rows, mine, theirs, blocks, copied):
    slots, stored = block_rows.shape
    smem = pl.BlockSpec(memory_space=pltpu.SMEM)
    vmem = pl.BlockSpec(memory_space=pltpu.VMEM)
    hbm = pl.BlockSpec(memory_space=pltpu.HBM)
    return pl.pallas_call(
        update_kernel,
        out_shape=jax.ShapeDtypeStruct(blocks.shape, F32),
        in_specs=[smem, smem, smem, smem, vmem, vmem, hbm, hbm],
        out_specs=hbm,
        input_output_aliases={7: 0},
        scratch_shapes=[
            pltpu.VMEM((slots * stored,) + blocks.shape[2:], F32),
            pltpu.SMEM((4, slots * stored), jnp.int32),
            pltpu.SemaphoreType.DMA((slots * stored,)),
            pltpu.SemaphoreType.DMA((slots * stored,)),
        ],
        compiler_params=pltpu.CompilerParams(
            vmem_limit_bytes=8 * 1024 * 1024 + 4 * blocks.size + 4 * mine.size
        ),
        name="update",
    )(
        core, row_ids, col_ids, block_rows, in_vmem(mine), in_vmem(theirs),
        in_hbm(blocks), in_hbm(copied),
    )


def local(diag_block, panel_rows, row_ids, col_ids, block_rows, blocks):
    blk = lax.axis_index("blk").astype(jnp.int32)[None]
    core = lax.axis_index("row").astype(jnp.int32)[None]
    swap = [(0, 1), (1, 0)]
    n_blk = lax.axis_size("blk")
    count = diag_block.shape[1] // BLOCK
    other = lax.ppermute(diag_block, "row", swap)

    def from_partner(value, k):
        return lax.ppermute(value, "blk", [(i, i ^ k) for i in range(n_blk)])

    in_stages = n_blk in (8, 16)
    near = n_blk // 4
    if in_stages:
        arrived = [from_partner(panel_rows, j * near) for j in range(1, 4)]
    else:
        pieces = [lax.all_gather(panel_rows, "blk", axis=0, tiled=True)]
    state = factor(0, 2, core, diag_block, other, [], blocks)
    if in_stages:
        group = pack([panel_rows] + arrived, state)
        pieces = [group] + [from_partner(group, k) for k in range(1, near)]
    high, low, *_, copied = factor(2, count, core, diag_block, other, state, blocks)
    own, mine = solve(blk, high, low, pieces)
    theirs = lax.ppermute(mine, "row", swap)
    new_blocks = update(core, row_ids, col_ids, block_rows, mine, theirs, blocks, copied)
    return own[None], new_blocks


def solution(mesh):
    return jax.shard_map(
        local,
        mesh=mesh,
        in_specs=(
            P("row", None),
            P("row", "blk", None),
            P(),
            P("blk"),
            P("blk", None),
            P("blk", None, "row", None),
        ),
        out_specs=(P("row", "blk", None), P("blk", None, "row", None)),
        check_vma=False,
    )
```

```python
import functools

import jax
import jax.numpy as jnp
from jax import lax
from jax.experimental import pallas as pl
from jax.experimental.pallas import tpu as pltpu
from jax.sharding import PartitionSpec as P

BLOCK = 128
PANEL = 32
STEP = 8
F32 = jnp.float32
BF16 = jnp.bfloat16
TN = (((0,), (0,)), ((), ()))
NT = (((1,), (1,)), ((), ()))


def halves(value):
    high = value.astype(BF16)
    return high, (value - high.astype(F32)).astype(BF16)


def in_hbm(value):
    return pltpu.with_memory_space_constraint(value, pltpu.HBM)


def in_vmem(value):
    return pltpu.with_memory_space_constraint(value, pltpu.VMEM)


def repeated(ref, *index):
    *lead, row, lanes = index
    return ref[(*lead, pl.ds(row, STEP, stride=0), lanes)]


def eliminate(columns, tiles, scratch_diag, scratch_below, scratch_rows):
    groups = PANEL // STEP
    sublane = lax.broadcasted_iota(jnp.int32, (STEP, BLOCK), 0)
    for s in range(groups):
        first = s * STEP
        for c in range(STEP):
            scratch_diag[s, c] = columns[first + c][s]
        square = [
            [
                repeated(scratch_diag, s, c, k, slice(None)) if k <= c else None
                for c in range(STEP)
            ]
            for k in range(STEP)
        ]
        inverse = []
        for k in range(STEP):
            inverse.append(pl.reciprocal(square[k][k], approx=True))
            for c in range(k + 1, STEP):
                ratio = square[k][c] * inverse[k]
                for d in range(c, STEP):
                    square[c][d] = square[c][d] - ratio * square[k][d]
        ratios = []
        for k in range(STEP):
            now = [None] * groups
            for g in range(s, groups):
                now[g] = columns[first + k][g] * inverse[k]
            now[s] = jnp.where(sublane > k, now[s], 0.0)
            for c in range(k + 1, STEP):
                for g in range(s, groups):
                    columns[first + c][g] = columns[first + c][g] - now[g] * square[k][c]
            ratios.append(now)
            for g in range(s + 1, groups):
                scratch_below[s, k, (g - 1) * STEP : g * STEP, :] = columns[first + k][g]
        for c in range(first + STEP, PANEL):
            for k in range(STEP):
                entry = repeated(scratch_below, s, k, c - STEP, slice(None))
                for g in range(c // STEP, groups):
                    columns[c][g] = columns[c][g] - ratios[k][g] * entry
        pivots = square[0][0]
        for k in range(1, STEP):
            pivots = jnp.where(sublane == k, square[k][k], pivots)
        for t in range(len(tiles[s])):
            for k in range(STEP):
                scratch_rows[s, t, k % 2] = tiles[s][t]
                row = repeated(scratch_rows, s, t, k % 2, k, slice(None))
                for g in range(s, groups):
                    if g == s and k == STEP - 1:
                        continue
                    tiles[g][t] = tiles[g][t] - ratios[k][g] * row
        scale = lax.rsqrt(pivots)
        tiles[s] = [tile * scale for tile in tiles[s]]


def times_transposed(high, low, right_high, right_low):
    width = right_high.shape[0]
    if high.shape[1] <= BLOCK:
        return lax.dot_general(
            jnp.concatenate([high, low, high], axis=1),
            jnp.concatenate([right_high, right_high, right_low], axis=1),
            NT,
            preferred_element_type=F32,
        )
    both = lax.dot_general(
        high, jnp.concatenate([right_high, right_low], axis=0), NT, preferred_element_type=F32
    )
    return (
        both[:, :width]
        + both[:, width:]
        + lax.dot_general(low, right_high, NT, preferred_element_type=F32)
    )


def invert_diagonal(diag, unit, scratch_diag, scratch_below, scratch_rows):
    groups = range(PANEL // STEP)
    for q in range(BLOCK // PANEL):
        top = q * PANEL
        rest = top + PANEL
        tile = diag[top:rest, :]
        columns = [
            [
                jnp.broadcast_to(
                    tile[g * STEP : (g + 1) * STEP, top + c : top + c + 1], (STEP, BLOCK)
                )
                if g >= c // STEP
                else None
                for g in groups
            ]
            for c in range(PANEL)
        ]
        cuts = [slice(top + g * STEP, top + (g + 1) * STEP) for g in groups]
        tiles = [[diag[cut, :], unit[cut, :]] for cut in cuts]
        eliminate(columns, tiles, scratch_diag, scratch_below, scratch_rows)
        for g, cut in enumerate(cuts):
            diag[cut, :] = tiles[g][0]
            unit[cut, :] = tiles[g][1]
        if rest < BLOCK:
            right_high, right_low = halves(
                jnp.concatenate([diag[top:rest, :], unit[top:rest, :]], axis=1)
            )
            left_high, left_low = right_high[:, :BLOCK], right_low[:, :BLOCK]
            change = lax.dot_general(
                jnp.concatenate([left_high, left_low, left_high], axis=0),
                jnp.concatenate([right_high, right_high, right_low], axis=0),
                TN,
                preferred_element_type=F32,
            )
            diag[rest:, :] = diag[rest:, :] - change[rest:, :BLOCK]
            unit[rest:, :] = unit[rest:, :] - change[rest:, BLOCK:]


def factor_kernel(first, last, core_ref, own_ref, other_ref, *refs):
    refs = list(refs)
    state_refs = [refs.pop(0) for _ in range(4)] if first else []
    blocks_ref = refs.pop(0) if first else None
    high_ref, low_ref, base, diag = refs[:4]
    refs = refs[4:]
    copied_ref = refs.pop(0) if first else None
    matrix, unit, scratch_diag, scratch_below, scratch_rows, tile_sems = refs[:6]
    order = own_ref.shape[1]
    half = order // 2
    count = order // BLOCK
    core = core_ref[0]

    def fetch_tile(t, which):
        source = (own_ref, other_ref)[which]
        at = pl.multiple_of((core if which == 0 else 1 - core) * half, half)
        return pltpu.make_async_copy(
            source.at[:, pl.ds(t * BLOCK, BLOCK)],
            matrix.at[t, pl.ds(at, half), :],
            tile_sems.at[t, which],
        )

    for t in range(first + 1 if first else 0, min(last + 1, count)):
        for which in range(2):
            fetch_tile(t, which).start()
    if first:
        held, block_sems = refs[6:]
        fetch_blocks = pltpu.make_async_copy(blocks_ref, held, block_sems.at[0])
        store_blocks = pltpu.make_async_copy(held, copied_ref, block_sems.at[1])
        fetch_blocks.start()
    identity = (
        lax.broadcasted_iota(jnp.int32, (BLOCK, BLOCK), 0)
        == lax.broadcasted_iota(jnp.int32, (BLOCK, BLOCK), 1)
    ).astype(F32)

    if first:
        done = first * BLOCK
        high_ref[:, :done] = state_refs[0][...]
        low_ref[:, :done] = state_refs[1][...]
        base[...] = state_refs[2][...]
        diag[...] = state_refs[3][...]
    else:
        for which in range(2):
            fetch_tile(0, which).wait()
        base[:BLOCK] = identity
        base[BLOCK:] = matrix[0, BLOCK:, :]
        diag[...] = matrix[0, :BLOCK, :]

    def prepare(b):
        done = (b + 1) * BLOCK
        following = slice(done, done + BLOCK)
        change = times_transposed(
            high_ref[:, :done], low_ref[:, :done], high_ref[following, :done], low_ref[following, :done]
        )
        for which in range(2):
            fetch_tile(b + 1, which).wait()
        diag[...] = matrix[b + 1, following, :] - change[following]
        base[:done] = -change[:done]
        base[following] = identity
        if done + BLOCK < order:
            base[done + BLOCK :] = matrix[b + 1, done + BLOCK :, :] - change[done + BLOCK :]
        high_ref[following, :done] = jnp.zeros((BLOCK, done), BF16)
        low_ref[following, :done] = jnp.zeros((BLOCK, done), BF16)
        if first and b == first:
            fetch_blocks.wait()
            store_blocks.start()

    def block_step(b, carry):
        unit[...] = identity
        invert_diagonal(diag, unit, scratch_diag, scratch_below, scratch_rows)
        here = pl.ds(pl.multiple_of(b * BLOCK, BLOCK), BLOCK)
        high, low = halves(times_transposed(*halves(base[...]), *halves(unit[...])))
        high_ref[:, here] = high
        low_ref[:, here] = low
        for at in range(first, min(last, count - 1)):
            pl.when(b == at)(functools.partial(prepare, at))
        return carry

    lax.fori_loop(first, last, block_step, 0)
    if first:
        store_blocks.wait()


def factor(first, last, core, own, other, state, blocks):
    order = own.shape[1]
    count = order // BLOCK
    vmem = pl.BlockSpec(memory_space=pltpu.VMEM)
    hbm = pl.BlockSpec(memory_space=pltpu.HBM)
    columns = last * BLOCK
    out_shape = [
        pltpu.VMEM((order, columns), BF16),
        pltpu.VMEM((order, columns), BF16),
        pltpu.VMEM((order, BLOCK), F32),
        pltpu.VMEM((BLOCK, BLOCK), F32),
    ]
    scratch = [
        pltpu.VMEM((count, order, BLOCK), F32),
        pltpu.VMEM((BLOCK, BLOCK), F32),
        pltpu.VMEM((PANEL // STEP, STEP, STEP, BLOCK), F32),
        pltpu.VMEM((PANEL // STEP, STEP, PANEL - STEP, BLOCK), F32),
        pltpu.VMEM((PANEL // STEP, 2, 2, STEP, BLOCK), F32),
        pltpu.SemaphoreType.DMA((count, 2)),
    ]
    in_specs = [pl.BlockSpec(memory_space=pltpu.SMEM), hbm, vmem]
    out_specs = [vmem] * len(out_shape)
    operands = [core, in_hbm(own), in_vmem(other)]
    limit = 12 * 1024 * 1024
    if first:
        in_specs += [vmem] * len(state) + [hbm]
        operands += [in_vmem(part) for part in state] + [in_hbm(blocks)]
        out_specs.append(hbm)
        out_shape.append(jax.ShapeDtypeStruct(blocks.shape, F32))
        scratch += [pltpu.VMEM(blocks.shape, F32), pltpu.SemaphoreType.DMA((2,))]
        limit += 4 * blocks.size + 4 * 1024 * 1024
    share = last - first
    return pl.pallas_call(
        functools.partial(factor_kernel, first, last),
        out_shape=out_shape,
        in_specs=in_specs,
        out_specs=out_specs,
        scratch_shapes=scratch,
        compiler_params=pltpu.CompilerParams(vmem_limit_bytes=limit),
        cost_estimate=pl.CostEstimate(
            flops=share * order**3, bytes_accessed=share * 20_000_000, transcendentals=0
        ),
        name="factor",
    )(*operands)


def solve_kernel(blk_ref, high_ref, low_ref, *refs):
    *piece_refs, own_ref, rounded_ref, rows, rows_high, rows_low, solved, row_sem = refs
    blk = blk_ref[0]
    held, part, order = piece_refs[0].shape
    n_blk = len(piece_refs) * held
    chunk_rows = rows_high.shape[0]
    chunk = chunk_rows // part
    chunks = n_blk // chunk

    def load(at):
        return pltpu.make_async_copy(piece_refs[0].at[pl.ds(at * chunk, chunk)], rows, row_sem)

    def solve_chunk(at, carry):
        if len(piece_refs) == 1:
            load(at).start()
            load(at).wait()
            rows_high[...], rows_low[...] = halves(rows[...].reshape(chunk_rows, order))
        else:
            for k, piece in enumerate(piece_refs):
                for j in range(held):
                    place = blk ^ (k + j * len(piece_refs))
                    here = pl.ds(pl.multiple_of(place * part, part), part)
                    rows_high[here, :], rows_low[here, :] = halves(piece[j])

        width = 256
        for n in range(order // width):
            cut = slice(n * width, (n + 1) * width)
            deep = (n + 1) * width
            x = jnp.dot(
                rows_high[:, :deep], high_ref[:deep, cut], preferred_element_type=F32
            )
            x += jnp.dot(rows_low[:, :deep], high_ref[:deep, cut], preferred_element_type=F32)
            x += jnp.dot(rows_high[:, :deep], low_ref[:deep, cut], preferred_element_type=F32)
            solved[:, cut] = x
            rounded_ref[pl.ds(pl.multiple_of(at * chunk_rows, chunk_rows), chunk_rows), cut] = (
                x.astype(BF16)
            )

        @pl.when(blk // chunk == at)
        def _():
            own_ref[...] = solved[pl.ds(pl.multiple_of(blk % chunk * part, part), part), :]

        return carry

    lax.fori_loop(0, chunks, solve_chunk, 0)


def solve(blk, high, low, pieces):
    order = high.shape[0]
    held, part, _ = pieces[0].shape
    n_blk = len(pieces) * held
    chunk = n_blk if len(pieces) > 1 else min(n_blk, max(1, 512 // part))
    smem = pl.BlockSpec(memory_space=pltpu.SMEM)
    vmem = pl.BlockSpec(memory_space=pltpu.VMEM)
    if len(pieces) > 1:
        piece_spec, row_shape = vmem, (1, 8, BLOCK)
        pieces = [in_vmem(piece) for piece in pieces]
    else:
        piece_spec, row_shape = pl.BlockSpec(memory_space=pltpu.HBM), (chunk, part, order)
        pieces = [in_hbm(piece) for piece in pieces]
    return pl.pallas_call(
        solve_kernel,
        out_shape=[
            jax.ShapeDtypeStruct((part, order), F32),
            pltpu.VMEM((n_blk * part, order), BF16),
        ],
        in_specs=[smem, vmem, vmem] + [piece_spec] * len(pieces),
        out_specs=[vmem, vmem],
        scratch_shapes=[
            pltpu.VMEM(row_shape, F32),
            pltpu.VMEM((chunk * part, order), BF16),
            pltpu.VMEM((chunk * part, order), BF16),
            pltpu.VMEM((chunk * part, order), F32),
            pltpu.SemaphoreType.DMA,
        ],
        compiler_params=pltpu.CompilerParams(vmem_limit_bytes=20 * 1024 * 1024),
        name="solve",
    )(blk, in_vmem(high), in_vmem(low), *pieces)


def pack_kernel(count, *refs):
    out_ref = refs[-1]
    for j in range(count):
        out_ref[j] = refs[j][0]


def pack(parts, after):
    vmem = pl.BlockSpec(memory_space=pltpu.VMEM)
    return pl.pallas_call(
        functools.partial(pack_kernel, len(parts)),
        out_shape=pltpu.VMEM((len(parts),) + parts[0].shape[1:], parts[0].dtype),
        in_specs=[vmem] * (len(parts) + len(after)),
        out_specs=vmem,
        name="pack",
    )(*[in_vmem(value) for value in list(parts) + list(after)])


def update_kernel(
    core_ref, row_ids_ref, col_ids_ref, block_rows_ref,
    mine_ref, theirs_ref, blocks_ref, copied_ref, out_ref,
    held, found, in_sems, out_sems,
):
    del copied_ref
    core = core_ref[0]
    slots, stored = block_rows_ref.shape
    pieces = row_ids_ref.shape[0]
    half_rows = blocks_ref.shape[2]

    def fetch(n, slot, r):
        return pltpu.make_async_copy(blocks_ref.at[slot, r], held.at[n], in_sems.at[n])

    def place_of(wanted):
        def look(p, at):
            return jnp.where(row_ids_ref[p] == wanted, p, at)

        return jnp.where(wanted >= 0, lax.fori_loop(0, pieces, look, jnp.int32(-1)), -1)

    def scan_slot(slot, n):
        a = place_of(col_ids_ref[slot])

        def scan_stored(r, n):
            b = jnp.where(a >= 0, place_of(block_rows_ref[slot, r]), -1)

            @pl.when(b >= 0)
            def _():
                found[0, n] = slot
                found[1, n] = r
                found[2, n] = a
                found[3, n] = b
                fetch(n, slot, r).start()

            return jnp.where(b >= 0, n + 1, n)

        return lax.fori_loop(0, jnp.where(a >= 0, stored, 0), scan_stored, n)

    total = lax.fori_loop(0, slots, scan_slot, jnp.int32(0))

    def store(n):
        return pltpu.make_async_copy(
            held.at[n], out_ref.at[found[0, n], found[1, n]], out_sems.at[n]
        )

    def apply(n, carry):
        a_rows = pl.ds(pl.multiple_of(found[2, n] * half_rows, half_rows), half_rows)
        b_rows = pl.ds(pl.multiple_of(found[3, n] * half_rows, half_rows), half_rows)
        row = mine_ref[b_rows, :]
        column = jnp.concatenate([mine_ref[a_rows, :], theirs_ref[a_rows, :]], axis=0)
        change = lax.dot_general(row, column, NT, preferred_element_type=F32)
        fetch(n, found[0, n], found[1, n]).wait()
        for which in range(2):
            at = (core if which == 0 else 1 - core) * half_rows
            lanes = pl.ds(pl.multiple_of(at, half_rows), half_rows)
            part = change[:, which * half_rows : (which + 1) * half_rows]
            held[n, :, lanes] = held[n, :, lanes] - part
        store(n).start()
        return carry

    lax.fori_loop(0, total, apply, 0)

    def finish(n, carry):
        store(n).wait()
        return carry

    lax.fori_loop(0, total, finish, 0)


def update(core, row_ids, col_ids, block_rows, mine, theirs, blocks, copied):
    slots, stored = block_rows.shape
    smem = pl.BlockSpec(memory_space=pltpu.SMEM)
    vmem = pl.BlockSpec(memory_space=pltpu.VMEM)
    hbm = pl.BlockSpec(memory_space=pltpu.HBM)
    return pl.pallas_call(
        update_kernel,
        out_shape=jax.ShapeDtypeStruct(blocks.shape, F32),
        in_specs=[smem, smem, smem, smem, vmem, vmem, hbm, hbm],
        out_specs=hbm,
        input_output_aliases={7: 0},
        scratch_shapes=[
            pltpu.VMEM((slots * stored,) + blocks.shape[2:], F32),
            pltpu.SMEM((4, slots * stored), jnp.int32),
            pltpu.SemaphoreType.DMA((slots * stored,)),
            pltpu.SemaphoreType.DMA((slots * stored,)),
        ],
        compiler_params=pltpu.CompilerParams(
            vmem_limit_bytes=8 * 1024 * 1024 + 4 * blocks.size + 4 * mine.size
        ),
        name="update",
    )(
        core, row_ids, col_ids, block_rows, in_vmem(mine), in_vmem(theirs),
        in_hbm(blocks), in_hbm(copied),
    )


def local(diag_block, panel_rows, row_ids, col_ids, block_rows, blocks):
    blk = lax.axis_index("blk").astype(jnp.int32)[None]
    core = lax.axis_index("row").astype(jnp.int32)[None]
    swap = [(0, 1), (1, 0)]
    n_blk = lax.axis_size("blk")
    count = diag_block.shape[1] // BLOCK
    other = lax.ppermute(diag_block, "row", swap)

    def from_partner(value, k):
        return lax.ppermute(value, "blk", [(i, i ^ k) for i in range(n_blk)])

    in_stages = n_blk in (8, 16)
    near = n_blk // 4
    if in_stages:
        arrived = [from_partner(panel_rows, j * near) for j in range(1, 4)]
    else:
        pieces = [lax.all_gather(panel_rows, "blk", axis=0, tiled=True)]
    state = factor(0, 2, core, diag_block, other, [], blocks)
    if in_stages:
        group = pack([panel_rows] + arrived, state)
        pieces = [group] + [from_partner(group, k) for k in range(1, near)]
    high, low, *_, copied = factor(2, count, core, diag_block, other, state, blocks)
    own, mine = solve(blk, high, low, pieces)
    theirs = lax.ppermute(mine, "row", swap)
    new_blocks = update(core, row_ids, col_ids, block_rows, mine, theirs, blocks, copied)
    return own[None], new_blocks


def solution(mesh):
    return jax.shard_map(
        local,
        mesh=mesh,
        in_specs=(
            P("row", None),
            P("row", "blk", None),
            P(),
            P("blk"),
            P("blk", None),
            P("blk", None, "row", None),
        ),
        out_specs=(P("row", "blk", None), P("blk", None, "row", None)),
        check_vma=False,
    )
```

```python
import functools

import jax
import jax.numpy as jnp
from jax import lax
from jax.experimental import pallas as pl
from jax.experimental.pallas import tpu as pltpu
from jax.sharding import PartitionSpec as P

BLOCK = 128
PANEL = 32
STEP = 8
F32 = jnp.float32
BF16 = jnp.bfloat16
TN = (((0,), (0,)), ((), ()))
NT = (((1,), (1,)), ((), ()))


def halves(value):
    high = value.astype(BF16)
    return high, (value - high.astype(F32)).astype(BF16)


def in_hbm(value):
    return pltpu.with_memory_space_constraint(value, pltpu.HBM)


def in_vmem(value):
    return pltpu.with_memory_space_constraint(value, pltpu.VMEM)


def repeated(ref, *index):
    *lead, row, lanes = index
    return ref[(*lead, pl.ds(row, STEP, stride=0), lanes)]


def eliminate(columns, tiles, scratch_diag, scratch_below, scratch_rows):
    groups = PANEL // STEP
    sublane = lax.broadcasted_iota(jnp.int32, (STEP, BLOCK), 0)
    for s in range(groups):
        first = s * STEP
        for c in range(STEP):
            scratch_diag[s, c] = columns[first + c][s]
        square = [
            [
                repeated(scratch_diag, s, c, k, slice(None)) if k <= c else None
                for c in range(STEP)
            ]
            for k in range(STEP)
        ]
        inverse = []
        for k in range(STEP):
            inverse.append(pl.reciprocal(square[k][k], approx=True))
            for c in range(k + 1, STEP):
                ratio = square[k][c] * inverse[k]
                for d in range(c, STEP):
                    square[c][d] = square[c][d] - ratio * square[k][d]
        ratios = []
        for k in range(STEP):
            now = [None] * groups
            for g in range(s, groups):
                now[g] = columns[first + k][g] * inverse[k]
            now[s] = jnp.where(sublane > k, now[s], 0.0)
            for c in range(k + 1, STEP):
                for g in range(s, groups):
                    columns[first + c][g] = columns[first + c][g] - now[g] * square[k][c]
            ratios.append(now)
            for g in range(s + 1, groups):
                scratch_below[s, k, (g - 1) * STEP : g * STEP, :] = columns[first + k][g]
        for c in range(first + STEP, PANEL):
            for k in range(STEP):
                entry = repeated(scratch_below, s, k, c - STEP, slice(None))
                for g in range(c // STEP, groups):
                    columns[c][g] = columns[c][g] - ratios[k][g] * entry
        pivots = square[0][0]
        for k in range(1, STEP):
            pivots = jnp.where(sublane == k, square[k][k], pivots)
        for t in range(len(tiles[s])):
            for k in range(STEP):
                scratch_rows[s, t, k % 2] = tiles[s][t]
                row = repeated(scratch_rows, s, t, k % 2, k, slice(None))
                for g in range(s, groups):
                    if g == s and k == STEP - 1:
                        continue
                    tiles[g][t] = tiles[g][t] - ratios[k][g] * row
        scale = lax.rsqrt(pivots)
        tiles[s] = [tile * scale for tile in tiles[s]]


def times_transposed(high, low, right_high, right_low):
    width = right_high.shape[0]
    both = lax.dot_general(
        high, jnp.concatenate([right_high, right_low], axis=0), NT, preferred_element_type=F32
    )
    return (
        both[:, :width]
        + both[:, width:]
        + lax.dot_general(low, right_high, NT, preferred_element_type=F32)
    )


def invert_diagonal(diag, unit, scratch_diag, scratch_below, scratch_rows):
    groups = range(PANEL // STEP)
    for q in range(BLOCK // PANEL):
        top = q * PANEL
        rest = top + PANEL
        tile = diag[top:rest, :]
        columns = [
            [
                jnp.broadcast_to(
                    tile[g * STEP : (g + 1) * STEP, top + c : top + c + 1], (STEP, BLOCK)
                )
                if g >= c // STEP
                else None
                for g in groups
            ]
            for c in range(PANEL)
        ]
        cuts = [slice(top + g * STEP, top + (g + 1) * STEP) for g in groups]
        tiles = [[diag[cut, :], unit[cut, :]] for cut in cuts]
        eliminate(columns, tiles, scratch_diag, scratch_below, scratch_rows)
        for g, cut in enumerate(cuts):
            diag[cut, :] = tiles[g][0]
            unit[cut, :] = tiles[g][1]
        if rest < BLOCK:
            right_high, right_low = halves(
                jnp.concatenate([diag[top:rest, :], unit[top:rest, :]], axis=1)
            )
            left_high, left_low = right_high[:, :BLOCK], right_low[:, :BLOCK]
            change = lax.dot_general(
                jnp.concatenate([left_high, left_low, left_high], axis=0),
                jnp.concatenate([right_high, right_high, right_low], axis=0),
                TN,
                preferred_element_type=F32,
            )
            diag[rest:, :] = diag[rest:, :] - change[rest:, :BLOCK]
            unit[rest:, :] = unit[rest:, :] - change[rest:, BLOCK:]


def factor_kernel(first, last, core_ref, own_ref, other_ref, *refs):
    refs = list(refs)
    state_refs = [refs.pop(0) for _ in range(4)] if first else []
    blocks_ref = refs.pop(0) if first else None
    high_ref, low_ref, base, diag = refs[:4]
    refs = refs[4:]
    copied_ref = refs.pop(0) if first else None
    matrix, unit, scratch_diag, scratch_below, scratch_rows, tile_sems = refs[:6]
    order = own_ref.shape[1]
    half = order // 2
    count = order // BLOCK
    core = core_ref[0]

    def fetch_tile(t, which):
        source = (own_ref, other_ref)[which]
        at = pl.multiple_of((core if which == 0 else 1 - core) * half, half)
        return pltpu.make_async_copy(
            source.at[:, pl.ds(t * BLOCK, BLOCK)],
            matrix.at[t, pl.ds(at, half), :],
            tile_sems.at[t, which],
        )

    for t in range(first + 1 if first else 0, min(last + 1, count)):
        for which in range(2):
            fetch_tile(t, which).start()
    if first:
        held, block_sems = refs[6:]
        fetch_blocks = pltpu.make_async_copy(blocks_ref, held, block_sems.at[0])
        store_blocks = pltpu.make_async_copy(held, copied_ref, block_sems.at[1])
        fetch_blocks.start()
    identity = (
        lax.broadcasted_iota(jnp.int32, (BLOCK, BLOCK), 0)
        == lax.broadcasted_iota(jnp.int32, (BLOCK, BLOCK), 1)
    ).astype(F32)

    if first:
        done = first * BLOCK
        high_ref[:, :done] = state_refs[0][...]
        low_ref[:, :done] = state_refs[1][...]
        base[...] = state_refs[2][...]
        diag[...] = state_refs[3][...]
    else:
        for which in range(2):
            fetch_tile(0, which).wait()
        base[:BLOCK] = identity
        base[BLOCK:] = matrix[0, BLOCK:, :]
        diag[...] = matrix[0, :BLOCK, :]

    def prepare(b):
        done = (b + 1) * BLOCK
        following = slice(done, done + BLOCK)
        change = times_transposed(
            high_ref[:, :done], low_ref[:, :done], high_ref[following, :done], low_ref[following, :done]
        )
        for which in range(2):
            fetch_tile(b + 1, which).wait()
        diag[...] = matrix[b + 1, following, :] - change[following]
        base[:done] = -change[:done]
        base[following] = identity
        if done + BLOCK < order:
            base[done + BLOCK :] = matrix[b + 1, done + BLOCK :, :] - change[done + BLOCK :]
        high_ref[following, :done] = jnp.zeros((BLOCK, done), BF16)
        low_ref[following, :done] = jnp.zeros((BLOCK, done), BF16)
        if first and b == first:
            fetch_blocks.wait()
            store_blocks.start()

    def block_step(b, carry):
        unit[...] = identity
        invert_diagonal(diag, unit, scratch_diag, scratch_below, scratch_rows)
        here = pl.ds(pl.multiple_of(b * BLOCK, BLOCK), BLOCK)
        high, low = halves(times_transposed(*halves(base[...]), *halves(unit[...])))
        high_ref[:, here] = high
        low_ref[:, here] = low
        for at in range(first, min(last, count - 1)):
            pl.when(b == at)(functools.partial(prepare, at))
        return carry

    lax.fori_loop(first, last, block_step, 0)
    if first:
        store_blocks.wait()


def factor(first, last, core, own, other, state, blocks):
    order = own.shape[1]
    count = order // BLOCK
    vmem = pl.BlockSpec(memory_space=pltpu.VMEM)
    hbm = pl.BlockSpec(memory_space=pltpu.HBM)
    columns = last * BLOCK
    out_shape = [
        pltpu.VMEM((order, columns), BF16),
        pltpu.VMEM((order, columns), BF16),
        pltpu.VMEM((order, BLOCK), F32),
        pltpu.VMEM((BLOCK, BLOCK), F32),
    ]
    scratch = [
        pltpu.VMEM((count, order, BLOCK), F32),
        pltpu.VMEM((BLOCK, BLOCK), F32),
        pltpu.VMEM((PANEL // STEP, STEP, STEP, BLOCK), F32),
        pltpu.VMEM((PANEL // STEP, STEP, PANEL - STEP, BLOCK), F32),
        pltpu.VMEM((PANEL // STEP, 2, 2, STEP, BLOCK), F32),
        pltpu.SemaphoreType.DMA((count, 2)),
    ]
    in_specs = [pl.BlockSpec(memory_space=pltpu.SMEM), hbm, vmem]
    out_specs = [vmem] * len(out_shape)
    operands = [core, in_hbm(own), in_vmem(other)]
    limit = 12 * 1024 * 1024
    if first:
        in_specs += [vmem] * len(state) + [hbm]
        operands += [in_vmem(part) for part in state] + [in_hbm(blocks)]
        out_specs.append(hbm)
        out_shape.append(jax.ShapeDtypeStruct(blocks.shape, F32))
        scratch += [pltpu.VMEM(blocks.shape, F32), pltpu.SemaphoreType.DMA((2,))]
        limit += 4 * blocks.size + 4 * 1024 * 1024
    share = last - first
    return pl.pallas_call(
        functools.partial(factor_kernel, first, last),
        out_shape=out_shape,
        in_specs=in_specs,
        out_specs=out_specs,
        scratch_shapes=scratch,
        compiler_params=pltpu.CompilerParams(vmem_limit_bytes=limit),
        cost_estimate=pl.CostEstimate(
            flops=share * order**3, bytes_accessed=share * 20_000_000, transcendentals=0
        ),
        name="factor",
    )(*operands)


def solve_kernel(blk_ref, high_ref, low_ref, *refs):
    *piece_refs, own_ref, rounded_ref, rows, rows_high, rows_low, solved, row_sem = refs
    blk = blk_ref[0]
    held, part, order = piece_refs[0].shape
    n_blk = len(piece_refs) * held
    chunk_rows = rows_high.shape[0]
    chunk = chunk_rows // part
    chunks = n_blk // chunk

    def load(at):
        return pltpu.make_async_copy(piece_refs[0].at[pl.ds(at * chunk, chunk)], rows, row_sem)

    def solve_chunk(at, carry):
        if len(piece_refs) == 1:
            load(at).start()
            load(at).wait()
            rows_high[...], rows_low[...] = halves(rows[...].reshape(chunk_rows, order))
        else:
            for k, piece in enumerate(piece_refs):
                for j in range(held):
                    place = blk ^ (k + j * len(piece_refs))
                    here = pl.ds(pl.multiple_of(place * part, part), part)
                    rows_high[here, :], rows_low[here, :] = halves(piece[j])

        width = 256
        for n in range(order // width):
            cut = slice(n * width, (n + 1) * width)
            deep = (n + 1) * width
            x = jnp.dot(
                rows_high[:, :deep], high_ref[:deep, cut], preferred_element_type=F32
            )
            x += jnp.dot(rows_low[:, :deep], high_ref[:deep, cut], preferred_element_type=F32)
            x += jnp.dot(rows_high[:, :deep], low_ref[:deep, cut], preferred_element_type=F32)
            solved[:, cut] = x
            rounded_ref[pl.ds(pl.multiple_of(at * chunk_rows, chunk_rows), chunk_rows), cut] = (
                x.astype(BF16)
            )

        @pl.when(blk // chunk == at)
        def _():
            own_ref[...] = solved[pl.ds(pl.multiple_of(blk % chunk * part, part), part), :]

        return carry

    lax.fori_loop(0, chunks, solve_chunk, 0)


def solve(blk, high, low, pieces):
    order = high.shape[0]
    held, part, _ = pieces[0].shape
    n_blk = len(pieces) * held
    chunk = n_blk if len(pieces) > 1 else min(n_blk, max(1, 512 // part))
    smem = pl.BlockSpec(memory_space=pltpu.SMEM)
    vmem = pl.BlockSpec(memory_space=pltpu.VMEM)
    if len(pieces) > 1:
        piece_spec, row_shape = vmem, (1, 8, BLOCK)
        pieces = [in_vmem(piece) for piece in pieces]
    else:
        piece_spec, row_shape = pl.BlockSpec(memory_space=pltpu.HBM), (chunk, part, order)
        pieces = [in_hbm(piece) for piece in pieces]
    return pl.pallas_call(
        solve_kernel,
        out_shape=[
            jax.ShapeDtypeStruct((part, order), F32),
            pltpu.VMEM((n_blk * part, order), BF16),
        ],
        in_specs=[smem, vmem, vmem] + [piece_spec] * len(pieces),
        out_specs=[vmem, vmem],
        scratch_shapes=[
            pltpu.VMEM(row_shape, F32),
            pltpu.VMEM((chunk * part, order), BF16),
            pltpu.VMEM((chunk * part, order), BF16),
            pltpu.VMEM((chunk * part, order), F32),
            pltpu.SemaphoreType.DMA,
        ],
        compiler_params=pltpu.CompilerParams(vmem_limit_bytes=20 * 1024 * 1024),
        name="solve",
    )(blk, in_vmem(high), in_vmem(low), *pieces)


def pack_kernel(count, *refs):
    out_ref = refs[-1]
    for j in range(count):
        out_ref[j] = refs[j][0]


def pack(parts, after):
    vmem = pl.BlockSpec(memory_space=pltpu.VMEM)
    return pl.pallas_call(
        functools.partial(pack_kernel, len(parts)),
        out_shape=pltpu.VMEM((len(parts),) + parts[0].shape[1:], parts[0].dtype),
        in_specs=[vmem] * (len(parts) + len(after)),
        out_specs=vmem,
        name="pack",
    )(*[in_vmem(value) for value in list(parts) + list(after)])


def update_kernel(
    core_ref, row_ids_ref, col_ids_ref, block_rows_ref,
    mine_ref, theirs_ref, blocks_ref, copied_ref, out_ref,
    held, found, in_sems, out_sems,
):
    del copied_ref
    core = core_ref[0]
    slots, stored = block_rows_ref.shape
    pieces = row_ids_ref.shape[0]
    half_rows = blocks_ref.shape[2]

    def fetch(n, slot, r):
        return pltpu.make_async_copy(blocks_ref.at[slot, r], held.at[n], in_sems.at[n])

    def place_of(wanted):
        def look(p, at):
            return jnp.where(row_ids_ref[p] == wanted, p, at)

        return jnp.where(wanted >= 0, lax.fori_loop(0, pieces, look, jnp.int32(-1)), -1)

    def scan_slot(slot, n):
        a = place_of(col_ids_ref[slot])

        def scan_stored(r, n):
            b = jnp.where(a >= 0, place_of(block_rows_ref[slot, r]), -1)

            @pl.when(b >= 0)
            def _():
                found[0, n] = slot
                found[1, n] = r
                found[2, n] = a
                found[3, n] = b
                fetch(n, slot, r).start()

            return jnp.where(b >= 0, n + 1, n)

        return lax.fori_loop(0, jnp.where(a >= 0, stored, 0), scan_stored, n)

    total = lax.fori_loop(0, slots, scan_slot, jnp.int32(0))

    def store(n):
        return pltpu.make_async_copy(
            held.at[n], out_ref.at[found[0, n], found[1, n]], out_sems.at[n]
        )

    def apply(n, carry):
        a_rows = pl.ds(pl.multiple_of(found[2, n] * half_rows, half_rows), half_rows)
        b_rows = pl.ds(pl.multiple_of(found[3, n] * half_rows, half_rows), half_rows)
        row = mine_ref[b_rows, :]
        column = jnp.concatenate([mine_ref[a_rows, :], theirs_ref[a_rows, :]], axis=0)
        change = lax.dot_general(row, column, NT, preferred_element_type=F32)
        fetch(n, found[0, n], found[1, n]).wait()
        for which in range(2):
            at = (core if which == 0 else 1 - core) * half_rows
            lanes = pl.ds(pl.multiple_of(at, half_rows), half_rows)
            part = change[:, which * half_rows : (which + 1) * half_rows]
            held[n, :, lanes] = held[n, :, lanes] - part
        store(n).start()
        return carry

    lax.fori_loop(0, total, apply, 0)

    def finish(n, carry):
        store(n).wait()
        return carry

    lax.fori_loop(0, total, finish, 0)


def update(core, row_ids, col_ids, block_rows, mine, theirs, blocks, copied):
    slots, stored = block_rows.shape
    smem = pl.BlockSpec(memory_space=pltpu.SMEM)
    vmem = pl.BlockSpec(memory_space=pltpu.VMEM)
    hbm = pl.BlockSpec(memory_space=pltpu.HBM)
    return pl.pallas_call(
        update_kernel,
        out_shape=jax.ShapeDtypeStruct(blocks.shape, F32),
        in_specs=[smem, smem, smem, smem, vmem, vmem, hbm, hbm],
        out_specs=hbm,
        input_output_aliases={7: 0},
        scratch_shapes=[
            pltpu.VMEM((slots * stored,) + blocks.shape[2:], F32),
            pltpu.SMEM((4, slots * stored), jnp.int32),
            pltpu.SemaphoreType.DMA((slots * stored,)),
            pltpu.SemaphoreType.DMA((slots * stored,)),
        ],
        compiler_params=pltpu.CompilerParams(
            vmem_limit_bytes=8 * 1024 * 1024 + 4 * blocks.size + 4 * mine.size
        ),
        name="update",
    )(
        core, row_ids, col_ids, block_rows, in_vmem(mine), in_vmem(theirs),
        in_hbm(blocks), in_hbm(copied),
    )


def local(diag_block, panel_rows, row_ids, col_ids, block_rows, blocks):
    blk = lax.axis_index("blk").astype(jnp.int32)[None]
    core = lax.axis_index("row").astype(jnp.int32)[None]
    swap = [(0, 1), (1, 0)]
    n_blk = lax.axis_size("blk")
    count = diag_block.shape[1] // BLOCK
    other = lax.ppermute(diag_block, "row", swap)

    def from_partner(value, k):
        return lax.ppermute(value, "blk", [(i, i ^ k) for i in range(n_blk)])

    in_stages = n_blk in (8, 16)
    near = n_blk // 4
    if in_stages:
        arrived = [from_partner(panel_rows, j * near) for j in range(1, 4)]
    else:
        pieces = [lax.all_gather(panel_rows, "blk", axis=0, tiled=True)]
    state = factor(0, 2, core, diag_block, other, [], blocks)
    if in_stages:
        group = pack([panel_rows] + arrived, state)
        pieces = [group] + [from_partner(group, k) for k in range(1, near)]
    high, low, *_, copied = factor(2, count, core, diag_block, other, state, blocks)
    own, mine = solve(blk, high, low, pieces)
    theirs = lax.ppermute(mine, "row", swap)
    new_blocks = update(core, row_ids, col_ids, block_rows, mine, theirs, blocks, copied)
    return own[None], new_blocks


def solution(mesh):
    return jax.shard_map(
        local,
        mesh=mesh,
        in_specs=(
            P("row", None),
            P("row", "blk", None),
            P(),
            P("blk"),
            P("blk", None),
            P("blk", None, "row", None),
        ),
        out_specs=(P("row", "blk", None), P("blk", None, "row", None)),
        check_vma=False,
    )
```

```python
import functools

import jax
import jax.numpy as jnp
from jax import lax
from jax.experimental import pallas as pl
from jax.experimental.pallas import tpu as pltpu
from jax.sharding import PartitionSpec as P

BLOCK = 128
PANEL = 32
STEP = 8
F32 = jnp.float32
BF16 = jnp.bfloat16
TN = (((0,), (0,)), ((), ()))
NT = (((1,), (1,)), ((), ()))


def halves(value):
    high = value.astype(BF16)
    return high, (value - high.astype(F32)).astype(BF16)


def in_hbm(value):
    return pltpu.with_memory_space_constraint(value, pltpu.HBM)


def in_vmem(value):
    return pltpu.with_memory_space_constraint(value, pltpu.VMEM)


def repeated(ref, *index):
    *lead, row, lanes = index
    return ref[(*lead, pl.ds(row, STEP, stride=0), lanes)]


def eliminate(columns, tiles, scratch_diag, scratch_below, scratch_rows):
    groups = PANEL // STEP
    sublane = lax.broadcasted_iota(jnp.int32, (STEP, BLOCK), 0)
    for s in range(groups):
        first = s * STEP
        for c in range(STEP):
            scratch_diag[s, c] = columns[first + c][s]
        square = [
            [
                repeated(scratch_diag, s, c, k, slice(None)) if k <= c else None
                for c in range(STEP)
            ]
            for k in range(STEP)
        ]
        inverse = []
        for k in range(STEP):
            inverse.append(pl.reciprocal(square[k][k], approx=True))
            for c in range(k + 1, STEP):
                ratio = square[k][c] * inverse[k]
                for d in range(c, STEP):
                    square[c][d] = square[c][d] - ratio * square[k][d]
        ratios = []
        for k in range(STEP):
            now = [None] * groups
            for g in range(s, groups):
                now[g] = columns[first + k][g] * inverse[k]
            now[s] = jnp.where(sublane > k, now[s], 0.0)
            for c in range(k + 1, STEP):
                for g in range(s, groups):
                    columns[first + c][g] = columns[first + c][g] - now[g] * square[k][c]
            ratios.append(now)
            for g in range(s + 1, groups):
                scratch_below[s, k, (g - 1) * STEP : g * STEP, :] = columns[first + k][g]
        for c in range(first + STEP, PANEL):
            for k in range(STEP):
                entry = repeated(scratch_below, s, k, c - STEP, slice(None))
                for g in range(c // STEP, groups):
                    columns[c][g] = columns[c][g] - ratios[k][g] * entry
        pivots = square[0][0]
        for k in range(1, STEP):
            pivots = jnp.where(sublane == k, square[k][k], pivots)
        for t in range(len(tiles[s])):
            for k in range(STEP):
                scratch_rows[s, t, k % 2] = tiles[s][t]
                row = repeated(scratch_rows, s, t, k % 2, k, slice(None))
                for g in range(s, groups):
                    if g == s and k == STEP - 1:
                        continue
                    tiles[g][t] = tiles[g][t] - ratios[k][g] * row
        scale = lax.rsqrt(pivots)
        tiles[s] = [tile * scale for tile in tiles[s]]


def times_transposed(high, low, right_high, right_low):
    width = right_high.shape[0]
    both = lax.dot_general(
        high, jnp.concatenate([right_high, right_low], axis=0), NT, preferred_element_type=F32
    )
    return (
        both[:, :width]
        + both[:, width:]
        + lax.dot_general(low, right_high, NT, preferred_element_type=F32)
    )


def invert_diagonal(diag, unit, scratch_diag, scratch_below, scratch_rows):
    groups = range(PANEL // STEP)
    for q in range(BLOCK // PANEL):
        top = q * PANEL
        rest = top + PANEL
        tile = diag[top:rest, :]
        columns = [
            [
                jnp.broadcast_to(
                    tile[g * STEP : (g + 1) * STEP, top + c : top + c + 1], (STEP, BLOCK)
                )
                if g >= c // STEP
                else None
                for g in groups
            ]
            for c in range(PANEL)
        ]
        cuts = [slice(top + g * STEP, top + (g + 1) * STEP) for g in groups]
        tiles = [[diag[cut, :], unit[cut, :]] for cut in cuts]
        eliminate(columns, tiles, scratch_diag, scratch_below, scratch_rows)
        for g, cut in enumerate(cuts):
            diag[cut, :] = tiles[g][0]
            unit[cut, :] = tiles[g][1]
        if rest < BLOCK:
            left_high, left_low = halves(diag[top:rest, :])
            left = jnp.concatenate([left_high, left_low, left_high], axis=0)
            for target in (diag, unit):
                right_high, right_low = halves(target[top:rest, :])
                right = jnp.concatenate([right_high, right_high, right_low], axis=0)
                change = lax.dot_general(left, right, TN, preferred_element_type=F32)
                target[rest:, :] = target[rest:, :] - change[rest:, :]


def factor_kernel(first, last, core_ref, own_ref, other_ref, *refs):
    refs = list(refs)
    state_refs = [refs.pop(0) for _ in range(4)] if first else []
    blocks_ref = refs.pop(0) if first else None
    high_ref, low_ref, base, diag = refs[:4]
    refs = refs[4:]
    copied_ref = refs.pop(0) if first else None
    matrix, unit, ahead, scratch_diag, scratch_below, scratch_rows, tile_sems = refs[:7]
    order = own_ref.shape[1]
    half = order // 2
    count = order // BLOCK
    core = core_ref[0]

    def fetch_tile(t, which):
        source = (own_ref, other_ref)[which]
        at = pl.multiple_of((core if which == 0 else 1 - core) * half, half)
        return pltpu.make_async_copy(
            source.at[:, pl.ds(pl.multiple_of(t * BLOCK, BLOCK), BLOCK)],
            matrix.at[t, pl.ds(at, half), :],
            tile_sems.at[t, which],
        )

    for t in range(first + 1 if first else 0, min(last + 1, count)):
        for which in range(2):
            fetch_tile(t, which).start()
    if first:
        held, block_sems = refs[7:]
        fetch_blocks = pltpu.make_async_copy(blocks_ref, held, block_sems.at[0])
        store_blocks = pltpu.make_async_copy(held, copied_ref, block_sems.at[1])
        fetch_blocks.start()
    identity = (
        lax.broadcasted_iota(jnp.int32, (BLOCK, BLOCK), 0)
        == lax.broadcasted_iota(jnp.int32, (BLOCK, BLOCK), 1)
    ).astype(F32)

    row_at = lax.broadcasted_iota(jnp.int32, (order, BLOCK), 0)

    done = first * BLOCK
    high_ref[:, done:] = jnp.zeros((order, (last - first) * BLOCK), BF16)
    low_ref[:, done:] = jnp.zeros((order, (last - first) * BLOCK), BF16)
    if first:
        high_ref[:, :done] = state_refs[0][...]
        low_ref[:, :done] = state_refs[1][...]
        base[...] = state_refs[2][...]
        diag[...] = state_refs[3][...]
    else:
        for which in range(2):
            fetch_tile(0, which).wait()
        base[...] = matrix[0]
        diag[...] = base[:BLOCK]
        base[:BLOCK] = identity

    def block_step(cleared, depth, b, carry):
        here = pl.multiple_of(b * BLOCK, BLOCK)
        following = jnp.minimum(b + 1, count - 1)
        next_at = pl.multiple_of(following * BLOCK, BLOCK)

        @pl.when(b + 1 < count)
        def _():
            for which in range(2):
                fetch_tile(following, which).wait()

        if first:

            @pl.when(b == first + 1)
            def _():
                fetch_blocks.wait()
                store_blocks.start()

        high_ref[pl.ds(here, BLOCK), :cleared] = jnp.zeros((BLOCK, cleared), BF16)
        low_ref[pl.ds(here, BLOCK), :cleared] = jnp.zeros((BLOCK, cleared), BF16)
        ahead[...] = times_transposed(
            high_ref[:, :depth],
            low_ref[:, :depth],
            high_ref[pl.ds(next_at, BLOCK), :depth],
            low_ref[pl.ds(next_at, BLOCK), :depth],
        )

        unit[...] = identity
        invert_diagonal(diag, unit, scratch_diag, scratch_below, scratch_rows)

        new_high, new_low = halves(times_transposed(*halves(base[...]), *halves(unit[...])))
        high_ref[:, pl.ds(here, BLOCK)] = new_high
        low_ref[:, pl.ds(here, BLOCK)] = new_low
        latest = times_transposed(
            new_high,
            new_low,
            high_ref[pl.ds(next_at, BLOCK), pl.ds(here, BLOCK)],
            low_ref[pl.ds(next_at, BLOCK), pl.ds(here, BLOCK)],
        )
        kept = jnp.where(row_at >= next_at, matrix[following], 0.0)
        base[...] = kept - ahead[...] - latest
        diag[...] = base[pl.ds(next_at, BLOCK), :]
        base[pl.ds(next_at, BLOCK), :] = identity
        return carry

    middle = (first + last) // 2 if last == count else last
    for start, stop in ((first, middle), (middle, last)):
        if start < stop:
            cleared = max(1, stop - 1) * BLOCK
            depth = max(1, min(stop - 1, count - 2)) * BLOCK
            lax.fori_loop(start, stop, functools.partial(block_step, cleared, depth), 0)
    if first:
        store_blocks.wait()


def factor(first, last, core, own, other, state, blocks):
    order = own.shape[1]
    count = order // BLOCK
    vmem = pl.BlockSpec(memory_space=pltpu.VMEM)
    hbm = pl.BlockSpec(memory_space=pltpu.HBM)
    columns = last * BLOCK
    out_shape = [
        pltpu.VMEM((order, columns), BF16),
        pltpu.VMEM((order, columns), BF16),
        pltpu.VMEM((order, BLOCK), F32),
        pltpu.VMEM((BLOCK, BLOCK), F32),
    ]
    scratch = [
        pltpu.VMEM((count, order, BLOCK), F32),
        pltpu.VMEM((BLOCK, BLOCK), F32),
        pltpu.VMEM((order, BLOCK), F32),
        pltpu.VMEM((PANEL // STEP, STEP, STEP, BLOCK), F32),
        pltpu.VMEM((PANEL // STEP, STEP, PANEL - STEP, BLOCK), F32),
        pltpu.VMEM((PANEL // STEP, 2, 2, STEP, BLOCK), F32),
        pltpu.SemaphoreType.DMA((count, 2)),
    ]
    in_specs = [pl.BlockSpec(memory_space=pltpu.SMEM), hbm, vmem]
    out_specs = [vmem] * len(out_shape)
    operands = [core, in_hbm(own), in_vmem(other)]
    limit = 12 * 1024 * 1024
    if first:
        in_specs += [vmem] * len(state) + [hbm]
        operands += [in_vmem(part) for part in state] + [in_hbm(blocks)]
        out_specs.append(hbm)
        out_shape.append(jax.ShapeDtypeStruct(blocks.shape, F32))
        scratch += [pltpu.VMEM(blocks.shape, F32), pltpu.SemaphoreType.DMA((2,))]
        limit += 4 * blocks.size + 4 * 1024 * 1024
    share = last - first
    return pl.pallas_call(
        functools.partial(factor_kernel, first, last),
        out_shape=out_shape,
        in_specs=in_specs,
        out_specs=out_specs,
        scratch_shapes=scratch,
        compiler_params=pltpu.CompilerParams(vmem_limit_bytes=limit),
        cost_estimate=pl.CostEstimate(
            flops=share * order**3, bytes_accessed=share * 20_000_000, transcendentals=0
        ),
        name="factor",
    )(*operands)


def solve_kernel(blk_ref, high_ref, low_ref, *refs):
    *piece_refs, own_ref, rounded_ref, rows, rows_high, rows_low, solved, row_sem = refs
    blk = blk_ref[0]
    held, part, order = piece_refs[0].shape
    n_blk = len(piece_refs) * held
    chunk_rows = rows_high.shape[0]
    chunk = chunk_rows // part
    chunks = n_blk // chunk

    def load(at):
        return pltpu.make_async_copy(piece_refs[0].at[pl.ds(at * chunk, chunk)], rows, row_sem)

    def solve_chunk(at, carry):
        if len(piece_refs) == 1:
            load(at).start()
            load(at).wait()
            rows_high[...], rows_low[...] = halves(rows[...].reshape(chunk_rows, order))
        else:
            for k, piece in enumerate(piece_refs):
                for j in range(held):
                    place = blk ^ (k + j * len(piece_refs))
                    here = pl.ds(pl.multiple_of(place * part, part), part)
                    rows_high[here, :], rows_low[here, :] = halves(piece[j])

        width = 256
        for n in range(order // width):
            cut = slice(n * width, (n + 1) * width)
            deep = (n + 1) * width
            x = jnp.dot(
                rows_high[:, :deep], high_ref[:deep, cut], preferred_element_type=F32
            )
            x += jnp.dot(rows_low[:, :deep], high_ref[:deep, cut], preferred_element_type=F32)
            x += jnp.dot(rows_high[:, :deep], low_ref[:deep, cut], preferred_element_type=F32)
            solved[:, cut] = x
            rounded_ref[pl.ds(pl.multiple_of(at * chunk_rows, chunk_rows), chunk_rows), cut] = (
                x.astype(BF16)
            )

        @pl.when(blk // chunk == at)
        def _():
            own_ref[...] = solved[pl.ds(pl.multiple_of(blk % chunk * part, part), part), :]

        return carry

    lax.fori_loop(0, chunks, solve_chunk, 0)


def solve(blk, high, low, pieces):
    order = high.shape[0]
    held, part, _ = pieces[0].shape
    n_blk = len(pieces) * held
    chunk = n_blk if len(pieces) > 1 else min(n_blk, max(1, 512 // part))
    smem = pl.BlockSpec(memory_space=pltpu.SMEM)
    vmem = pl.BlockSpec(memory_space=pltpu.VMEM)
    if len(pieces) > 1:
        piece_spec, row_shape = vmem, (1, 8, BLOCK)
        pieces = [in_vmem(piece) for piece in pieces]
    else:
        piece_spec, row_shape = pl.BlockSpec(memory_space=pltpu.HBM), (chunk, part, order)
        pieces = [in_hbm(piece) for piece in pieces]
    return pl.pallas_call(
        solve_kernel,
        out_shape=[
            jax.ShapeDtypeStruct((part, order), F32),
            pltpu.VMEM((n_blk * part, order), BF16),
        ],
        in_specs=[smem, vmem, vmem] + [piece_spec] * len(pieces),
        out_specs=[vmem, vmem],
        scratch_shapes=[
            pltpu.VMEM(row_shape, F32),
            pltpu.VMEM((chunk * part, order), BF16),
            pltpu.VMEM((chunk * part, order), BF16),
            pltpu.VMEM((chunk * part, order), F32),
            pltpu.SemaphoreType.DMA,
        ],
        compiler_params=pltpu.CompilerParams(vmem_limit_bytes=20 * 1024 * 1024),
        name="solve",
    )(blk, in_vmem(high), in_vmem(low), *pieces)


def pack_kernel(count, *refs):
    out_ref = refs[-1]
    for j in range(count):
        out_ref[j] = refs[j][0]


def pack(parts, after):
    vmem = pl.BlockSpec(memory_space=pltpu.VMEM)
    return pl.pallas_call(
        functools.partial(pack_kernel, len(parts)),
        out_shape=pltpu.VMEM((len(parts),) + parts[0].shape[1:], parts[0].dtype),
        in_specs=[vmem] * (len(parts) + len(after)),
        out_specs=vmem,
        name="pack",
    )(*[in_vmem(value) for value in list(parts) + list(after)])


def update_kernel(
    core_ref, row_ids_ref, col_ids_ref, block_rows_ref,
    mine_ref, theirs_ref, blocks_ref, copied_ref, out_ref,
    held, found, in_sems, out_sems,
):
    del copied_ref
    core = core_ref[0]
    slots, stored = block_rows_ref.shape
    pieces = row_ids_ref.shape[0]
    half_rows = blocks_ref.shape[2]

    def fetch(n, slot, r):
        return pltpu.make_async_copy(blocks_ref.at[slot, r], held.at[n], in_sems.at[n])

    def place_of(wanted):
        def look(p, at):
            return jnp.where(row_ids_ref[p] == wanted, p, at)

        return jnp.where(wanted >= 0, lax.fori_loop(0, pieces, look, jnp.int32(-1)), -1)

    def scan_slot(slot, n):
        a = place_of(col_ids_ref[slot])

        def scan_stored(r, n):
            b = jnp.where(a >= 0, place_of(block_rows_ref[slot, r]), -1)

            @pl.when(b >= 0)
            def _():
                found[0, n] = slot
                found[1, n] = r
                found[2, n] = a
                found[3, n] = b
                fetch(n, slot, r).start()

            return jnp.where(b >= 0, n + 1, n)

        return lax.fori_loop(0, jnp.where(a >= 0, stored, 0), scan_stored, n)

    total = lax.fori_loop(0, slots, scan_slot, jnp.int32(0))

    def store(n):
        return pltpu.make_async_copy(
            held.at[n], out_ref.at[found[0, n], found[1, n]], out_sems.at[n]
        )

    def apply(n, carry):
        a_rows = pl.ds(pl.multiple_of(found[2, n] * half_rows, half_rows), half_rows)
        b_rows = pl.ds(pl.multiple_of(found[3, n] * half_rows, half_rows), half_rows)
        row = mine_ref[b_rows, :]
        column = jnp.concatenate([mine_ref[a_rows, :], theirs_ref[a_rows, :]], axis=0)
        change = lax.dot_general(row, column, NT, preferred_element_type=F32)
        fetch(n, found[0, n], found[1, n]).wait()
        for which in range(2):
            at = (core if which == 0 else 1 - core) * half_rows
            lanes = pl.ds(pl.multiple_of(at, half_rows), half_rows)
            part = change[:, which * half_rows : (which + 1) * half_rows]
            held[n, :, lanes] = held[n, :, lanes] - part
        store(n).start()
        return carry

    lax.fori_loop(0, total, apply, 0)

    def finish(n, carry):
        store(n).wait()
        return carry

    lax.fori_loop(0, total, finish, 0)


def update(core, row_ids, col_ids, block_rows, mine, theirs, blocks, copied):
    slots, stored = block_rows.shape
    smem = pl.BlockSpec(memory_space=pltpu.SMEM)
    vmem = pl.BlockSpec(memory_space=pltpu.VMEM)
    hbm = pl.BlockSpec(memory_space=pltpu.HBM)
    return pl.pallas_call(
        update_kernel,
        out_shape=jax.ShapeDtypeStruct(blocks.shape, F32),
        in_specs=[smem, smem, smem, smem, vmem, vmem, hbm, hbm],
        out_specs=hbm,
        input_output_aliases={7: 0},
        scratch_shapes=[
            pltpu.VMEM((slots * stored,) + blocks.shape[2:], F32),
            pltpu.SMEM((4, slots * stored), jnp.int32),
            pltpu.SemaphoreType.DMA((slots * stored,)),
            pltpu.SemaphoreType.DMA((slots * stored,)),
        ],
        compiler_params=pltpu.CompilerParams(
            vmem_limit_bytes=8 * 1024 * 1024 + 4 * blocks.size + 4 * mine.size
        ),
        name="update",
    )(
        core, row_ids, col_ids, block_rows, in_vmem(mine), in_vmem(theirs),
        in_hbm(blocks), in_hbm(copied),
    )


def local(diag_block, panel_rows, row_ids, col_ids, block_rows, blocks):
    blk = lax.axis_index("blk").astype(jnp.int32)[None]
    core = lax.axis_index("row").astype(jnp.int32)[None]
    swap = [(0, 1), (1, 0)]
    n_blk = lax.axis_size("blk")
    count = diag_block.shape[1] // BLOCK
    other = lax.ppermute(diag_block, "row", swap)

    def from_partner(value, k):
        return lax.ppermute(value, "blk", [(i, i ^ k) for i in range(n_blk)])

    in_stages = n_blk in (8, 16)
    near = n_blk // 4
    if in_stages:
        arrived = [from_partner(panel_rows, j * near) for j in range(1, 4)]
    else:
        pieces = [lax.all_gather(panel_rows, "blk", axis=0, tiled=True)]
    state = factor(0, 2, core, diag_block, other, [], blocks)
    if in_stages:
        group = pack([panel_rows] + arrived, state)
        pieces = [group] + [from_partner(group, k) for k in range(1, near)]
    high, low, *_, copied = factor(2, count, core, diag_block, other, state, blocks)
    own, mine = solve(blk, high, low, pieces)
    theirs = lax.ppermute(mine, "row", swap)
    new_blocks = update(core, row_ids, col_ids, block_rows, mine, theirs, blocks, copied)
    return own[None], new_blocks


def solution(mesh):
    return jax.shard_map(
        local,
        mesh=mesh,
        in_specs=(
            P("row", None),
            P("row", "blk", None),
            P(),
            P("blk"),
            P("blk", None),
            P("blk", None, "row", None),
        ),
        out_specs=(P("row", "blk", None), P("blk", None, "row", None)),
        check_vma=False,
    )
```
